32 devices in a mesh: pack: 2 (over core), cp: 4 (over z), hd: 4 (over y, x).
Axes of the slice: x: 2, y: 2, z: 4, core: 2. Of those that a mesh axis runs over, the one named last changes fastest.
Arguments:
- inputs: bfloat16 [16384, 1024], P(('pack', 'cp', 'hd')), may hold values from -6 to 6
- cotangent: bfloat16 [16384, 1024], P(('pack', 'cp', 'hd')), may hold values from -6 to 6
- w_qkv: bfloat16 [1024, 3072], P(('pack', 'cp', 'hd')), may hold values from -0.1875 to 0.1875
- w_out: bfloat16 [1024, 1024], P(('pack', 'cp', 'hd')), may hold values from -0.75 to 0.75
- w_gate: bfloat16 [1024, 4096], P(('pack', 'cp', 'hd')), may hold values from -0.1875 to 0.1875
- w_up: bfloat16 [1024, 4096], P(('pack', 'cp', 'hd')), may hold values from -0.1875 to 0.1875
- w_down: bfloat16 [4096, 1024], P(('pack', 'cp', 'hd')), may hold values from -0.09375 to 0.09375
- gain_attn: bfloat16 [1024], P(('pack', 'cp', 'hd')), may hold values from 0.099609375 to 1.8984375
- gain_ffn: bfloat16 [1024], P(('pack', 'cp', 'hd')), may hold values from 0.099609375 to 1.8984375
- q_gain: float32 [64], replicated, may hold values from 0.1 to 1.9
- k_gain: float32 [64], replicated, may hold values from 0.1 to 1.9
- head_bias: float32 [16, 2], replicated, may hold values from -4 to 4
- segment_ids: int32 [16384], P(('pack', 'cp')), may hold values from 0 to 3, as said below
- variate_ids: int32 [16384], P(('pack', 'cp')), may hold values from 0 to 3
- time_index: int32 [16384], P(('pack', 'cp')), may hold values from 0 to 1023
Outputs:
- layer_out: bfloat16 [16384, 1024], P(('pack', 'cp', 'hd'))
- grad_inputs: float32 [16384, 1024], P(('pack', 'cp', 'hd'))
- grad_qkv: float32 [1024, 3072], P(('pack', 'cp', 'hd'))
- grad_out: float32 [1024, 1024], P(('pack', 'cp', 'hd'))
- grad_gate: float32 [1024, 4096], P(('pack', 'cp', 'hd'))
- grad_up: float32 [1024, 4096], P(('pack', 'cp', 'hd'))
- grad_down: float32 [4096, 1024], P(('pack', 'cp', 'hd'))
- grad_gain_attn: float32 [1024], P(('pack', 'cp', 'hd'))
- grad_gain_ffn: float32 [1024], P(('pack', 'cp', 'hd'))
- grad_q_gain: float32 [64], replicated
- grad_k_gain: float32 [64], replicated
- grad_bias: float32 [16, 2], replicated
The draws below stay inside these ranges and needn't reach their ends.
Inputs may be any that keep to these rules, and one draw needn't show every extreme that they name: `segment_ids`: within each of the 2 packs of 8192 tokens the ids start at 0 and never fall; a pack holds at most four documents.
All inputs are finite; a program needn't handle non-finite values.
Results may differ from the reference program's by a relative error of at most 0.015.
The reference program's roundings to bfloat16 on the way count: a program that leaves them out, or rounds other values in their place, can miss the bound.
Values may be sent and summed in bfloat16 or wider, within the bound.
A program may use at most 192 MiB of HBM per device.

```python
import math
import jax
import jax.numpy as jnp
from jax import lax

D = 1024
HEADS = 16
HDIM = 64
FF = 4096
HALF = 512
GROUP = 2048
SEQ = 8192
TOKENS = 16384
QBLOCK = 512
N_PACK = 2


def draw_segment_ids(key, part):
    key = jax.random.fold_in(key, 17)
    key_one, key_two, key_three = jax.random.split(key, 3)
    first_cut = jax.random.randint(key_one, (N_PACK, 1), 1, GROUP // 2 + 1)
    second_cut = SEQ - jax.random.randint(key_two, (N_PACK, 1), 1, GROUP // 2 + 1)
    third_cut = second_cut + jax.random.randint(key_three, (N_PACK, 1), 0, SEQ - second_cut)
    positions = jnp.arange(SEQ)[None, :]
    segment_map = (positions >= first_cut).astype(jnp.int32) + (positions >= second_cut).astype(jnp.int32) + (positions >= third_cut).astype(jnp.int32)
    return segment_map.reshape(-1).astype(jnp.int32)


def plant(entries, stream_key, low, top_value):
    spot = [jax.random.randint(jax.random.fold_in(stream_key, axis), (), 0, length) for axis, length in enumerate(entries.shape)]
    main_axis = entries.shape.index(max(entries.shape))
    neighbour = spot[:main_axis] + [(spot[main_axis] + 1) % entries.shape[main_axis]] + spot[main_axis + 1:]
    return entries.at[tuple(spot)].set(low).at[tuple(neighbour)].set(top_value)


def steps_of(stream_key, dims, cuts, least, top_value):
    def one(axis_at, shards_of):
        heights = jax.random.uniform(jax.random.fold_in(jax.random.fold_in(stream_key, 6), axis_at), (shards_of,), jnp.float32, least / len(cuts), top_value / len(cuts))
        return jnp.repeat(jnp.exp(heights), dims[axis_at] // shards_of).reshape((-1,) + (1,) * (len(dims) - axis_at - 1))

    gain = one(*cuts[0])
    for cut in cuts[1:]:
        gain = gain * one(*cut)
    return gain


def scatter_about(key, shape, spread, limit, pieces=(), held_as=jnp.bfloat16):
    level = steps_of(key, shape, pieces, -0.22, 0.18) if pieces else 1.0
    array = jax.random.normal(key, shape, jnp.float32) * spread * level
    return jnp.minimum(jnp.maximum(array, -limit), limit).astype(held_as)


def setup_inputs(seed: int = 0) -> dict:
    splits = jax.random.split(jax.random.key(seed), 16)
    inputs = scatter_about(splits[0], (TOKENS, D), 1.0, 6.0, ((0, 32),))
    cotangent = scatter_about(splits[1], (TOKENS, D), 1.0, 6.0, ((0, 32),))
    w_qkv = scatter_about(splits[2], (D, 3 * D), D ** -0.5, 0.1875, ((0, 32),))
    w_out = scatter_about(splits[3], (D, D), (D // 16) ** -0.5, 0.75, ((0, 32),))
    w_gate = scatter_about(splits[4], (D, FF), D ** -0.5, 0.1875, ((0, 32),))
    w_up = scatter_about(splits[5], (D, FF), D ** -0.5, 0.1875, ((0, 32),))
    w_down = scatter_about(splits[6], (FF, D), FF ** -0.5, 0.09375, ((0, 32),))
    gain_attn = jnp.clip(1.0 + 0.18 * jax.random.normal(splits[7], (D,), jnp.float32), 0.099609375, 1.8984375).astype(jnp.bfloat16)
    gain_ffn = jnp.clip(1.0 + 0.18 * jax.random.normal(splits[8], (D,), jnp.float32), 0.099609375, 1.8984375).astype(jnp.bfloat16)
    q_gain = jnp.clip(1.0 + 0.18 * jax.random.normal(splits[9], (HDIM,), jnp.float32), 0.1, 1.9)
    k_gain = jnp.clip(1.0 + 0.18 * jax.random.normal(splits[10], (HDIM,), jnp.float32), 0.1, 1.9)
    head_bias = scatter_about(splits[11], (HEADS, 2), 1.0, 4.0, (), jnp.float32)
    segment_ids = draw_segment_ids(jax.random.fold_in(splits[15], 71), 0)
    variate_ids = plant(jax.random.randint(splits[13], (TOKENS,), 0, 4), jax.random.fold_in(splits[13], 1), 0, 3).astype(jnp.int32)
    time_index = plant(jax.random.randint(splits[14], (TOKENS,), 0, 1024), jax.random.fold_in(splits[14], 1), 0, 1023).astype(jnp.int32)
    return dict(inputs=inputs, cotangent=cotangent, w_qkv=w_qkv, w_out=w_out, w_gate=w_gate, w_up=w_up, w_down=w_down, gain_attn=gain_attn, gain_ffn=gain_ffn, q_gain=q_gain, k_gain=k_gain, head_bias=head_bias, segment_ids=segment_ids, variate_ids=variate_ids, time_index=time_index)


eps_norm = 1e-06
theta_base = 10000.0
masked_score = -1e+30

@jax.custom_vjp
def low(v):
    return lax.optimization_barrier(v.astype(jnp.bfloat16)).astype(jnp.float32)

@jax.custom_vjp
def low_back(v):
    return v

def low_keep(v):
    return (low(v), None)

def low_pass(kept, grad):
    return (grad,)

def back_keep(v):
    return (v, None)

def back_low(kept, grad):
    return (low(grad),)
low.defvjp(low_keep, low_pass)
low_back.defvjp(back_keep, back_low)

def rms_gain(values, gain_vec):
    return values * lax.rsqrt(lax.optimization_barrier(jnp.mean(values * values, axis=-1, keepdims=True)) + eps_norm) * gain_vec

def rotate(values, cosine, rot_sine):
    half_dim = values.shape[-1] // 2
    front_half = values[..., :half_dim]
    back_half = values[..., half_dim:]
    return jnp.concatenate([front_half * cosine - back_half * rot_sine, back_half * cosine + front_half * rot_sine], axis=-1)

def rotary_angles(stamps):
    frequency = jnp.exp(-math.log(theta_base) * 2.0 * jnp.arange(HDIM // 2, dtype=jnp.float32) / HDIM)
    rot_angle = stamps.astype(jnp.float32)[:, None] * frequency[None, :]
    return (jnp.cos(rot_angle)[:, None, :], jnp.sin(rot_angle)[:, None, :])

def attend(queries, keys_rot, values, segments, variates, head_bias):
    highest = lax.Precision.HIGHEST
    key_span = QBLOCK + 2 * HALF
    score_scale = 1.0 / math.sqrt(HDIM)
    keys_pad = jnp.pad(keys_rot, ((HALF, HALF), (0, 0), (0, 0)))
    values_pad = jnp.pad(values, ((HALF, HALF), (0, 0), (0, 0)))
    seg_pad = jnp.pad(segments, (HALF, HALF), constant_values=-1)
    var_pad = jnp.pad(variates, (HALF, HALF))
    offsets_grid = jnp.arange(QBLOCK)[:, None] + HALF - jnp.arange(key_span)[None, :]
    within = jnp.abs(offsets_grid) <= HALF

    def one_block(begin_row):
        q_blk = lax.dynamic_slice_in_dim(queries, begin_row, QBLOCK, 0)
        k_blk = lax.dynamic_slice_in_dim(keys_pad, begin_row, key_span, 0)
        v_blk = lax.dynamic_slice_in_dim(values_pad, begin_row, key_span, 0)
        seg_q = lax.dynamic_slice_in_dim(segments, begin_row, QBLOCK, 0)
        seg_k = lax.dynamic_slice_in_dim(seg_pad, begin_row, key_span, 0)
        var_q = lax.dynamic_slice_in_dim(variates, begin_row, QBLOCK, 0)
        var_k = lax.dynamic_slice_in_dim(var_pad, begin_row, key_span, 0)
        scores = jnp.einsum('qhd,khd->hqk', q_blk, k_blk, precision=highest) * score_scale
        same_var = var_q[:, None] == var_k[None, :]
        scores = scores + jnp.where(same_var[None], head_bias[:, 0][:, None, None], head_bias[:, 1][:, None, None])
        scores = low_back(scores)
        allowed = (seg_q[:, None] == seg_k[None, :]) & within
        scores = jnp.where(allowed[None], scores, masked_score)
        weights = jax.nn.softmax(scores, axis=-1)
        return jnp.einsum('hqk,khd->qhd', low(weights), v_blk, precision=highest)
    starts = (jnp.arange(SEQ // QBLOCK) * QBLOCK).astype(jnp.int32)
    blocks = lax.map(jax.checkpoint(one_block), starts)
    return blocks.reshape(SEQ, HEADS * HDIM)

def forward(inputs, w_qkv, w_out, w_gate, w_up, w_down, gain_attn, gain_ffn, q_gain, k_gain, head_bias, segment_ids, variate_ids, time_index):
    highest = lax.Precision.HIGHEST
    normed = low(rms_gain(inputs, gain_attn))
    projected = low(low_back(jnp.dot(normed, w_qkv, precision=highest)))
    queries = projected[:, :D].reshape(TOKENS, HEADS, HDIM)
    keys_raw = projected[:, D:2 * D].reshape(TOKENS, HEADS, HDIM)
    values = projected[:, 2 * D:].reshape(TOKENS, HEADS, HDIM)
    cosine, rot_sine = rotary_angles(time_index)
    q_rot = low(rotate(rms_gain(queries, q_gain), cosine, rot_sine))
    k_rot = low(rotate(rms_gain(keys_raw, k_gain), cosine, rot_sine))
    mixed_list = []
    for pack_row in range(N_PACK):
        lower_row = pack_row * SEQ
        upper_row = lower_row + SEQ
        mixed_list.append(attend(q_rot[lower_row:upper_row], k_rot[lower_row:upper_row], values[lower_row:upper_row], segment_ids[lower_row:upper_row], variate_ids[lower_row:upper_row], head_bias))
    heads_out = low(low_back(jnp.concatenate(mixed_list, axis=0)))
    hidden = inputs + low_back(jnp.dot(heads_out, w_out, precision=highest))
    normed_ffn = low(rms_gain(hidden, gain_ffn))
    gate_pre = low_back(jnp.dot(normed_ffn, w_gate, precision=highest))
    up_pre = low_back(jnp.dot(normed_ffn, w_up, precision=highest))
    product = low(jax.nn.silu(gate_pre) * up_pre)
    return hidden + jnp.dot(product, w_down, precision=highest)

def reference(inputs, cotangent, w_qkv, w_out, w_gate, w_up, w_down, gain_attn, gain_ffn, q_gain, k_gain, head_bias, segment_ids, variate_ids, time_index):

    def layer_fn(inputs_f, qkv_f, out_f, gate_f, up_f, down_f, gattn_f, gffn_f, qgain_f, kgain_f, bias_f):
        return forward(inputs_f, qkv_f, out_f, gate_f, up_f, down_f, gattn_f, gffn_f, qgain_f, kgain_f, bias_f, segment_ids, variate_ids, time_index)
    primal, pullback = jax.vjp(layer_fn, inputs.astype(jnp.float32), w_qkv.astype(jnp.float32), w_out.astype(jnp.float32), w_gate.astype(jnp.float32), w_up.astype(jnp.float32), w_down.astype(jnp.float32), gain_attn.astype(jnp.float32), gain_ffn.astype(jnp.float32), q_gain.astype(jnp.float32), k_gain.astype(jnp.float32), head_bias.astype(jnp.float32))
    grads = pullback(cotangent.astype(jnp.float32))
    return (primal.astype(jnp.bfloat16), grads[0], grads[1], grads[2], grads[3], grads[4], grads[5], grads[6], grads[7], grads[8], grads[9], grads[10])
```

```python
import functools
import math

import jax
import jax.numpy as jnp
from jax import lax
from jax.experimental import pallas as pl
from jax.experimental.pallas import tpu as pltpu
from jax.sharding import PartitionSpec as P

HEADS = 16
HDIM = 64
HALF = 512


eps_norm = 1e-06
theta_base = 10000.0
masked_score = -1e30


def extended_2(cells, sides, width):
    for axis, dim in sides:
        count = lax.axis_size(axis)
        ends = count - 1
        head = lax.slice_in_dim(cells, 0, width, axis=dim)
        tail = lax.slice_in_dim(cells, cells.shape[dim] - width, cells.shape[dim], axis=dim)
        cells = jnp.concatenate(
            [
                lax.ppermute(tail, axis, [(i, (i + 1) % count) for i in range(ends)]),
                cells,
                lax.ppermute(head, axis, [((i + 1) % count, i) for i in range(ends)]),
            ],
            axis=dim,
        )
    return cells


def shifted(value, axis, steps):
    count = lax.axis_size(axis)
    leading, last = (max(0, -steps), min(count, count - steps))
    return lax.ppermute(value, axis, [(source, source + steps) for source in range(leading, last)])


def rotate(values, cosine, rot_sine):
    half_dim = values.shape[-1] // 2
    front_half = values[..., :half_dim]
    back_half = values[..., half_dim:]
    return jnp.concatenate(
        [front_half * cosine - back_half * rot_sine, back_half * cosine + front_half * rot_sine],
        axis=-1,
    )


def rms_scale(values):
    return lax.rsqrt(jnp.mean(values * values, axis=-1, keepdims=True) + eps_norm)


def norm_back(values, inv_rms, gain_vec, grad_in):
    scaled = grad_in * gain_vec
    d_values = inv_rms * scaled - values * inv_rms**3 * jnp.mean(
        scaled * values, axis=-1, keepdims=True
    )
    return (d_values, grad_in * values * inv_rms)


def contract_rows(left_mat, right_mat):
    return lax.dot_general(
        left_mat, right_mat, (((0,), (0,)), ((), ())), preferred_element_type=jnp.float32
    )


def contract_cols(left_mat, right_mat):
    return lax.dot_general(
        left_mat, right_mat, (((1,), (1,)), ((), ())), preferred_element_type=jnp.float32
    )


MESH = pl.DeviceIdType.MESH


def place():
    return lax.axis_index("pack"), lax.axis_index("cp"), lax.axis_index("hd")


def greet(peers):
    barrier = pltpu.get_barrier_semaphore()
    for peer in peers:
        pl.semaphore_signal(barrier, inc=1, device_id=peer, device_id_type=MESH)
    pl.semaphore_wait(barrier, len(peers))


def group_peers(ring):
    p, c, h = place()
    peers = [(1 - p, c, h), (p, c, h + 1 - 2 * lax.rem(h, 2)), (p, c, lax.rem(h + 2, 4))]
    peers += [(p, lax.rem(c + step, ring), h) for step in range(1, ring)]
    return peers


class Scatter:
    def __init__(self, ring, count, pick, buffers, sems, out, write):
        self.ring, self.count, self.pick = ring, count, pick
        self.own, self.b0, self.b1, self.b2, self.b3 = buffers
        self.load_sem, self.send_sem, self.recv_sem = sems
        self.out, self.write = out, write
        self.p, self.c, self.h = place()
        self.hy, self.hx = self.h // 2, lax.rem(self.h, 2)
        self.core = (1 - self.p, self.c, self.h)
        self.xpeer = (self.p, self.c, self.hy * 2 + 1 - self.hx)
        self.ypeer = (self.p, self.c, (1 - self.hy) * 2 + self.hx)

    def remote(self, i, stage, src, dst, device):
        return pltpu.make_async_remote_copy(
            src_ref=src, dst_ref=dst, send_sem=self.send_sem.at[stage, i],
            recv_sem=self.recv_sem.at[stage, i], device_id=device, device_id_type=MESH)

    def copy0(self, i, src):
        return self.remote(i, 0, src, self.b0.at[i], self.core)

    def copy1(self, i, first_y):
        if first_y:
            return self.remote(i, 1, self.own.at[i, :, 1 - self.hy], self.b1.at[i], self.ypeer)
        return self.remote(i, 1, self.own.at[i, :, :, 1 - self.hx], self.b1.at[i], self.xpeer)

    def copy2(self, i, first_y):
        if first_y:
            return self.remote(i, 2, self.own.at[i, :, self.hy, 1 - self.hx], self.b2.at[i], self.xpeer)
        return self.remote(i, 2, self.own.at[i, :, 1 - self.hy, self.hx], self.b2.at[i], self.ypeer)

    def copy3(self, i, step):
        peer = lax.rem(self.c + step, self.ring)
        return self.remote(i, 3, self.own.at[i, peer, self.hy, self.hx], self.b3.at[i, step - 1], (self.p, peer, self.h))

    def begin(self, i):
        def go(mine, other):
            pltpu.make_async_copy(mine, self.own.at[i], self.load_sem.at[i]).start()
            self.copy0(i, other).start()
        self.pick(i, self.p, go)

    def stage1(self, i, first_y):
        pltpu.make_async_copy(self.b0.at[i], self.own.at[i], self.load_sem.at[i]).wait()
        self.copy0(i, self.own.at[i]).wait_recv()
        def add(k, carry):
            self.own[i, k] = self.own[i, k] + self.b0[i, k]
            return carry
        lax.fori_loop(0, self.ring, add, 0)
        self.copy1(i, first_y).start()

    def stage2(self, i, first_y):
        self.copy1(i, first_y).wait_recv()
        def add(k, carry):
            for m in range(2):
                at = (i, k, self.hy, m) if first_y else (i, k, m, self.hx)
                self.own[at] = self.own[at] + self.b1[i, k, m]
            return carry
        lax.fori_loop(0, self.ring, add, 0)
        self.copy2(i, first_y).start()

    def stage3(self, i, first_y):
        self.copy2(i, first_y).wait_recv()
        def add(k, carry):
            at = (i, k, self.hy, self.hx)
            self.own[at] = self.own[at] + self.b2[i, k]
            return carry
        lax.fori_loop(0, self.ring, add, 0)
        for step in range(1, self.ring):
            self.copy3(i, step).start()

    def finish(self, i):
        pltpu.make_async_copy(self.b3.at[i], self.b3.at[i], self.recv_sem.at[3, i]).wait()
        total = self.own[i, self.c, self.hy, self.hx].astype(jnp.float32)
        for step in range(1, self.ring):
            total = total + self.b3[i, step - 1].astype(jnp.float32)
        self.write(i, total)

    def drain(self, i, first_y):
        self.copy0(i, self.own.at[i]).wait_send()
        self.copy1(i, first_y).wait_send()
        self.copy2(i, first_y).wait_send()
        pltpu.make_async_copy(self.b3.at[i], self.b3.at[i], self.send_sem.at[3, i]).wait()

    def step(self, t, ahead=3, lags=(0, 2, 4, 6)):
        pairs = (self.count + 1) // 2
        def both(pair, act):
            for first_y in (True, False):
                i = 2 * pair + (0 if first_y else 1)
                guard = (pair >= 0) & (i < self.count) & (i >= 0)
                pl.when(guard)(functools.partial(act, i, first_y))
        both(t, lambda i, f: self.begin(i))
        both(t - ahead - lags[0], self.stage1)
        both(t - ahead - lags[1], self.stage2)
        both(t - ahead - lags[2], self.stage3)
        both(t - ahead - lags[3], lambda i, f: self.finish(i))

    def steps(self, ahead=3, lags=(0, 2, 4, 6)):
        return (self.count + 1) // 2 + ahead + lags[3]

    def drain_all(self):
        def one(t, carry):
            for first_y in (True, False):
                i = 2 * t + (0 if first_y else 1)
                pl.when(i < self.count)(functools.partial(self.drain, i, first_y))
            return carry
        lax.fori_loop(0, (self.count + 1) // 2, one, 0)


def scatter_scratch(ring, count, rows, cols):
    bf = jnp.bfloat16
    return [
        pltpu.VMEM((count, ring, 2, 2, rows, cols), bf),
        pltpu.VMEM((count, ring, 2, 2, rows, cols), bf),
        pltpu.VMEM((count, ring, 2, rows, cols), bf),
        pltpu.VMEM((count, ring, rows, cols), bf),
        pltpu.VMEM((count, ring - 1, rows, cols), bf),
        pltpu.SemaphoreType.DMA((count,)),
        pltpu.SemaphoreType.DMA((4, count)),
        pltpu.SemaphoreType.DMA((4, count)),
    ]


def scatter_kernel(ring, layout, count, *refs):
    n = len(layout)
    grads, out = refs[:n], refs[n]
    own, b0, b1, b2, b3, load_sem, send_sem, recv_sem = refs[n + 1:]
    greet(group_peers(ring))

    def pick(i, p, go):
        start = 0
        for ref, (size, outer) in zip(grads, layout):
            j = i - start
            def run(ref=ref, j=j, outer=outer):
                if outer:
                    go(ref.at[j, p], ref.at[j, 1 - p])
                else:
                    go(ref.at[p, :, :, :, j], ref.at[1 - p, :, :, :, j])
            pl.when((j >= 0) & (j < size))(run)
            start += size

    def write(i, total):
        out[i] = total

    work = Scatter(ring, count, pick, (own, b0, b1, b2, b3), (load_sem, send_sem, recv_sem), out, write)
    def body(t, carry):
        work.step(t)
        return carry
    lax.fori_loop(0, work.steps(), body, 0)
    work.drain_all()


def scatter(grads, layout, ring, collective_id):
    rows, cols = grads[0].shape[-2:]
    count = sum(size for size, _ in layout)
    return pl.pallas_call(
        functools.partial(scatter_kernel, ring, layout, count),
        out_shape=jax.ShapeDtypeStruct((count, rows, cols), jnp.float32),
        in_specs=[pl.BlockSpec(memory_space=pl.ANY)] * len(grads),
        out_specs=pl.BlockSpec(memory_space=pltpu.VMEM),
        scratch_shapes=scatter_scratch(ring, count, rows, cols),
        compiler_params=pltpu.CompilerParams(collective_id=collective_id, has_side_effects=True, vmem_limit_bytes=60 * 2**20),
        name="rsum",
    )(*grads)


def item_shape(rows):
    full = max(rows, 16)
    return full, rows * 512 // full


def column_items(grad, ring):
    depth = grad.shape[0] // (8 * ring)
    rows, cols = item_shape(depth)
    parts = jnp.moveaxis(grad.reshape(2, ring, 2, 2, depth, -1, 512), 5, 0)
    return parts.reshape(-1, 2, ring, 2, 2, rows, cols)


def back_columns(items, depth):
    return jnp.moveaxis(items.reshape(-1, depth, 512), 0, 1).reshape(depth, -1)


def local(
    inputs,
    cotangent,
    w_qkv,
    w_out,
    w_gate,
    w_up,
    w_down,
    gain_attn,
    gain_ffn,
    q_gain,
    k_gain,
    head_bias,
    segment_ids,
    variate_ids,
    time_index,
):
    gathered = (
        lax.all_gather(w_qkv, ("pack", "cp", "hd"), axis=0, tiled=True),
        lax.all_gather(w_out, ("pack", "cp", "hd"), axis=0, tiled=True),
        lax.all_gather(w_gate, ("pack", "cp", "hd"), axis=0, tiled=True),
        lax.all_gather(w_up, ("pack", "cp", "hd"), axis=0, tiled=True),
        lax.all_gather(w_down, ("pack", "cp", "hd"), axis=0, tiled=True),
        lax.all_gather(gain_attn, ("pack", "cp", "hd"), axis=0, tiled=True),
        lax.all_gather(gain_ffn, ("pack", "cp", "hd"), axis=0, tiled=True),
    )
    full_qkv, full_out, full_gate, full_up, full_down, full_gattn, full_gffn = gathered
    tok_rows = inputs.shape[0]
    model_width = inputs.shape[1]
    hd_count = lax.axis_size("hd")
    local_width = model_width // hd_count
    local_heads = local_width // HDIM
    group_rows = tok_rows * hd_count
    qblock = min(512, group_rows)
    key_span = qblock + 2 * HALF
    score_scale = 1.0 / math.sqrt(HDIM)
    residual = inputs.astype(jnp.float32)
    rms_attn = rms_scale(residual)
    normed = (residual * rms_attn * full_gattn.astype(jnp.float32)).astype(jnp.bfloat16)
    projected = jnp.dot(normed, full_qkv, preferred_element_type=jnp.float32).astype(jnp.bfloat16)
    head_q, head_k, head_v = (
        lax.all_to_all(projected[:, :model_width], "hd", split_axis=1, concat_axis=0, tiled=True),
        lax.all_to_all(
            projected[:, model_width : 2 * model_width],
            "hd",
            split_axis=1,
            concat_axis=0,
            tiled=True,
        ),
        lax.all_to_all(
            projected[:, 2 * model_width :], "hd", split_axis=1, concat_axis=0, tiled=True
        ),
    )
    q_raw = head_q.astype(jnp.float32).reshape(group_rows, local_heads, HDIM)
    k_raw = head_k.astype(jnp.float32).reshape(group_rows, local_heads, HDIM)
    frequency = jnp.exp(
        -math.log(theta_base) * 2.0 * jnp.arange(HDIM // 2, dtype=jnp.float32) / HDIM
    )
    rot_angle = time_index.astype(jnp.float32)[:, None] * frequency[None, :]
    cosine = jnp.cos(rot_angle)[:, None, :]
    rot_sine = jnp.sin(rot_angle)[:, None, :]
    rms_query = rms_scale(q_raw)
    rms_key = rms_scale(k_raw)
    q_rot = rotate(q_raw * rms_query * q_gain, cosine, rot_sine).astype(jnp.bfloat16)
    k_rot = rotate(k_raw * rms_key * k_gain, cosine, rot_sine).astype(jnp.bfloat16)
    stacked = jnp.stack([k_rot.reshape(group_rows, local_width), head_v])
    extended = extended_2(stacked, (("cp", 1),), HALF)
    k_ext = extended[0].reshape(group_rows + 2 * HALF, local_heads, HDIM)
    v_ext = extended[1].reshape(group_rows + 2 * HALF, local_heads, HDIM)
    id_pair = jnp.stack([segment_ids + 1, variate_ids])
    id_ext = extended_2(id_pair, (("cp", 1),), HALF)
    head_index = lax.axis_index("hd")
    bias_local = lax.dynamic_slice_in_dim(head_bias, head_index * local_heads, local_heads, 0)
    offsets_grid = jnp.arange(qblock)[:, None] + HALF - jnp.arange(key_span)[None, :]
    within = jnp.abs(offsets_grid) <= HALF

    def block_scores(begin_row):
        q_blk = lax.dynamic_slice_in_dim(q_rot, begin_row, qblock, 0)
        k_blk = lax.dynamic_slice_in_dim(k_ext, begin_row, key_span, 0)
        v_blk = lax.dynamic_slice_in_dim(v_ext, begin_row, key_span, 0)
        seg_q = lax.dynamic_slice_in_dim(id_ext[0], begin_row + HALF, qblock, 0)
        seg_k = lax.dynamic_slice_in_dim(id_ext[0], begin_row, key_span, 0)
        var_q = lax.dynamic_slice_in_dim(id_ext[1], begin_row + HALF, qblock, 0)
        var_k = lax.dynamic_slice_in_dim(id_ext[1], begin_row, key_span, 0)
        same_var = var_q[:, None] == var_k[None, :]
        scores = (
            jnp.einsum("qhd,khd->hqk", q_blk, k_blk, preferred_element_type=jnp.float32)
            * score_scale
        )
        scores = scores + jnp.where(
            same_var[None], bias_local[:, 0][:, None, None], bias_local[:, 1][:, None, None]
        )
        allowed = (seg_q[:, None] == seg_k[None, :]) & within
        scores = jnp.where(allowed[None], scores, masked_score)
        return (scores, same_var, q_blk, k_blk, v_blk)

    def forward_block(begin_row):
        scores, same_var, q_blk, k_blk, v_blk = block_scores(begin_row)
        top_val = jnp.max(scores, axis=-1, keepdims=True)
        exp_scores = jnp.exp(scores - top_val)
        row_total = jnp.sum(exp_scores, axis=-1, keepdims=True)
        attn_probs = exp_scores / row_total
        mixed_blk = jnp.einsum(
            "hqk,khd->qhd",
            attn_probs.astype(jnp.bfloat16),
            v_blk,
            preferred_element_type=jnp.float32,
        )
        return (mixed_blk.reshape(qblock, local_width), (top_val + jnp.log(row_total))[..., 0])

    starts = jnp.arange(group_rows // qblock, dtype=jnp.int32) * qblock
    mixed_blocks, lse_blocks = lax.map(forward_block, starts)
    heads_out = mixed_blocks.reshape(group_rows, local_width).astype(jnp.bfloat16)
    token_out = lax.all_to_all(heads_out, "hd", split_axis=0, concat_axis=1, tiled=True)
    hidden = residual + jnp.dot(token_out, full_out, preferred_element_type=jnp.float32)
    rms_ffn = rms_scale(hidden)
    normed_ffn = (hidden * rms_ffn * full_gffn.astype(jnp.float32)).astype(jnp.bfloat16)
    gate_pre = jnp.dot(normed_ffn, full_gate, preferred_element_type=jnp.float32)
    up_pre = jnp.dot(normed_ffn, full_up, preferred_element_type=jnp.float32)
    sigmoid_gate = jax.nn.sigmoid(gate_pre)
    silu_gate = gate_pre * sigmoid_gate
    product = (silu_gate * up_pre).astype(jnp.bfloat16)
    layer_out = (hidden + jnp.dot(product, full_down, preferred_element_type=jnp.float32)).astype(
        jnp.bfloat16
    )
    back_set = (
        lax.all_gather(w_qkv, ("pack", "cp", "hd"), axis=0, tiled=True),
        lax.all_gather(w_out, ("pack", "cp", "hd"), axis=0, tiled=True),
        lax.all_gather(w_gate, ("pack", "cp", "hd"), axis=0, tiled=True),
        lax.all_gather(w_up, ("pack", "cp", "hd"), axis=0, tiled=True),
        lax.all_gather(w_down, ("pack", "cp", "hd"), axis=0, tiled=True),
        lax.all_gather(gain_attn, ("pack", "cp", "hd"), axis=0, tiled=True),
        lax.all_gather(gain_ffn, ("pack", "cp", "hd"), axis=0, tiled=True),
    )
    back_qkv, back_out, back_gate, back_up, back_down, back_gattn, back_gffn = back_set
    grad_down = contract_rows(product, cotangent)
    d_product = contract_cols(cotangent, back_down)
    d_gate = (d_product * up_pre * sigmoid_gate * (1.0 + gate_pre * (1.0 - sigmoid_gate))).astype(
        jnp.bfloat16
    )
    d_up = (d_product * silu_gate).astype(jnp.bfloat16)
    grad_gate = contract_rows(normed_ffn, d_gate)
    grad_up = contract_rows(normed_ffn, d_up)
    d_normed_ffn = contract_cols(d_gate, back_gate) + contract_cols(d_up, back_up)
    d_hidden_norm, gffn_terms = norm_back(
        hidden, rms_ffn, back_gffn.astype(jnp.float32), d_normed_ffn
    )
    d_hidden = cotangent.astype(jnp.float32) + d_hidden_norm
    d_attn = d_hidden.astype(jnp.bfloat16)
    grad_out = contract_rows(token_out, d_attn)
    d_token_out = contract_cols(d_attn, back_out).astype(jnp.bfloat16)
    d_heads = lax.all_to_all(d_token_out, "hd", split_axis=1, concat_axis=0, tiled=True)
    d_heads3 = d_heads.reshape(group_rows, local_heads, HDIM)

    def backward_block(carried, block_inputs):
        dk_ext, dv_ext, bias_grad = carried
        begin_row, lse_row = block_inputs
        scores, same_var, q_blk, k_blk, v_blk = block_scores(begin_row)
        attn_probs = jnp.exp(scores - lse_row[..., None])
        do_blk = lax.dynamic_slice_in_dim(d_heads3, begin_row, qblock, 0)
        d_probs = jnp.einsum("qhd,khd->hqk", do_blk, v_blk, preferred_element_type=jnp.float32)
        delta_row = jnp.sum(attn_probs * d_probs, axis=-1, keepdims=True)
        d_scores = (attn_probs * (d_probs - delta_row)).astype(jnp.bfloat16)
        d_wide = d_scores.astype(jnp.float32)
        same_total = jnp.sum(jnp.where(same_var[None], d_wide, 0.0), axis=(1, 2))
        every_total = jnp.sum(d_wide, axis=(1, 2))
        bias_grad = bias_grad + jnp.stack([same_total, every_total - same_total], axis=1)
        dv_blk = jnp.einsum(
            "hqk,qhd->khd",
            attn_probs.astype(jnp.bfloat16),
            do_blk,
            preferred_element_type=jnp.float32,
        )
        dq_blk = (
            jnp.einsum("hqk,khd->qhd", d_scores, k_blk, preferred_element_type=jnp.float32)
            * score_scale
        )
        dk_blk = (
            jnp.einsum("hqk,qhd->khd", d_scores, q_blk, preferred_element_type=jnp.float32)
            * score_scale
        )
        dk_ext = lax.dynamic_update_slice_in_dim(
            dk_ext, lax.dynamic_slice_in_dim(dk_ext, begin_row, key_span, 0) + dk_blk, begin_row, 0
        )
        dv_ext = lax.dynamic_update_slice_in_dim(
            dv_ext, lax.dynamic_slice_in_dim(dv_ext, begin_row, key_span, 0) + dv_blk, begin_row, 0
        )
        return ((dk_ext, dv_ext, bias_grad), dq_blk)

    zero_ext = jnp.zeros((group_rows + 2 * HALF, local_heads, HDIM), jnp.float32)
    init_state = (zero_ext, zero_ext, jnp.zeros((local_heads, 2), jnp.float32))
    (dk_ext, dv_ext, bias_grad), dq_blocks = lax.scan(
        backward_block, init_state, (starts, lse_blocks)
    )
    dk_flat = dk_ext.reshape(group_rows + 2 * HALF, local_width)
    dv_flat = dv_ext.reshape(group_rows + 2 * HALF, local_width)
    rims_low = jnp.stack([dk_flat[:HALF], dv_flat[:HALF]])
    rims_high = jnp.stack([dk_flat[HALF + group_rows :], dv_flat[HALF + group_rows :]])
    from_above = shifted(rims_low.astype(jnp.bfloat16), "cp", -1).astype(rims_low.dtype)
    from_below = shifted(rims_high.astype(jnp.bfloat16), "cp", 1).astype(rims_high.dtype)
    tail_rows = group_rows - HALF
    dk_own = (
        dk_flat[HALF : HALF + group_rows]
        + jnp.pad(from_below[0], ((0, tail_rows), (0, 0)))
        + jnp.pad(from_above[0], ((tail_rows, 0), (0, 0)))
    )
    dv_own = (
        dv_flat[HALF : HALF + group_rows]
        + jnp.pad(from_below[1], ((0, tail_rows), (0, 0)))
        + jnp.pad(from_above[1], ((tail_rows, 0), (0, 0)))
    )
    dq_rot = dq_blocks.reshape(group_rows, local_heads, HDIM)
    dk_rot = dk_own.reshape(group_rows, local_heads, HDIM)
    dq_raw, qgain_terms = norm_back(q_raw, rms_query, q_gain, rotate(dq_rot, cosine, -rot_sine))
    dk_raw, kgain_terms = norm_back(k_raw, rms_key, k_gain, rotate(dk_rot, cosine, -rot_sine))
    grad_query = dq_raw.reshape(group_rows, local_width).astype(jnp.bfloat16)
    grad_key = dk_raw.reshape(group_rows, local_width).astype(jnp.bfloat16)
    back_q, back_k, back_v = (
        lax.all_to_all(grad_query, "hd", split_axis=0, concat_axis=1, tiled=True),
        lax.all_to_all(grad_key, "hd", split_axis=0, concat_axis=1, tiled=True),
        lax.all_to_all(dv_own.astype(jnp.bfloat16), "hd", split_axis=0, concat_axis=1, tiled=True),
    )
    d_projected = jnp.concatenate([back_q, back_k, back_v], axis=1)
    grad_qkv = contract_rows(normed, d_projected)
    d_normed = contract_cols(d_projected, back_qkv)
    d_resid_norm, gattn_terms = norm_back(
        residual, rms_attn, back_gattn.astype(jnp.float32), d_normed
    )
    grad_inputs = d_hidden + d_resid_norm
    ring = lax.axis_size("cp")
    low = jnp.bfloat16
    depth = w_qkv.shape[0]
    down_depth = w_down.shape[0]
    down_items = column_items(
        grad_down.astype(low).reshape(8 * ring, 4, depth, model_width).swapaxes(0, 1).reshape(4, 8 * ring * depth, model_width).swapaxes(0, 1).reshape(8 * ring * depth, 4 * model_width), ring)
    parts = [column_items(grad.astype(low), ring) for grad in (grad_gate, grad_up)]
    parts += [down_items]
    parts += [column_items(grad.astype(low), ring) for grad in (grad_out, grad_qkv)]
    items = scatter(parts, tuple((part.shape[0], True) for part in parts), ring, 0)
    own_gate = back_columns(items[:8], depth)
    own_up = back_columns(items[8:16], depth)
    own_down = back_columns(items[16:24], depth).reshape(depth, 4, model_width).swapaxes(0, 1).reshape(down_depth, model_width)
    own_out = back_columns(items[24:26], depth)
    own_qkv = back_columns(items[26:], depth)
    summed = (
        own_qkv,
        own_out,
        own_gate,
        own_up,
        own_down,
        lax.psum_scatter(
            jnp.sum(gattn_terms, axis=0), ("pack", "cp", "hd"), scatter_dimension=0, tiled=True
        ),
        lax.psum_scatter(
            jnp.sum(gffn_terms, axis=0), ("pack", "cp", "hd"), scatter_dimension=0, tiled=True
        ),
    )
    bias_full = lax.dynamic_update_slice_in_dim(
        jnp.zeros((HEADS, 2), jnp.float32), bias_grad, head_index * local_heads, 0
    )
    small_sums = lax.psum(
        (jnp.sum(qgain_terms, axis=(0, 1)), jnp.sum(kgain_terms, axis=(0, 1)), bias_full),
        ("pack", "cp", "hd"),
    )
    return (
        layer_out,
        grad_inputs,
        summed[0],
        summed[1],
        summed[2],
        summed[3],
        summed[4],
        summed[5],
        summed[6],
        small_sums[0],
        small_sums[1],
        small_sums[2],
    )


def solution(mesh):
    return jax.shard_map(
        local,
        mesh=mesh,
        in_specs=(
            P(("pack", "cp", "hd"), None),
            P(("pack", "cp", "hd"), None),
            P(("pack", "cp", "hd"), None),
            P(("pack", "cp", "hd"), None),
            P(("pack", "cp", "hd"), None),
            P(("pack", "cp", "hd"), None),
            P(("pack", "cp", "hd"), None),
            P(("pack", "cp", "hd")),
            P(("pack", "cp", "hd")),
            P(),
            P(),
            P(),
            P(("pack", "cp")),
            P(("pack", "cp")),
            P(("pack", "cp")),
        ),
        out_specs=(
            P(("pack", "cp", "hd"), None),
            P(("pack", "cp", "hd"), None),
            P(("pack", "cp", "hd"), None),
            P(("pack", "cp", "hd"), None),
            P(("pack", "cp", "hd"), None),
            P(("pack", "cp", "hd"), None),
            P(("pack", "cp", "hd"), None),
            P(("pack", "cp", "hd")),
            P(("pack", "cp", "hd")),
            P(),
            P(),
            P(),
        ),
        check_vma=False,
    )
```

```python
import functools
import math

import jax
import jax.numpy as jnp
from jax import lax
from jax.experimental import pallas as pl
from jax.experimental.pallas import tpu as pltpu
from jax.sharding import PartitionSpec as P

HEADS = 16
HDIM = 64
HALF = 512
QB = 256
SPAN = QB + 2 * HALF
FAR = -1e30
EPS = 1e-6
theta_base = 10000.0
MIB = 2**20
F32, BF = jnp.float32, jnp.bfloat16
MESH = pl.DeviceIdType.MESH
VM = pl.BlockSpec(memory_space=pltpu.VMEM)
ANY = pl.BlockSpec(memory_space=pl.ANY)
ALL = slice(None)


def item_shape(rows):
    full = max(rows, 16)
    return full, rows * 512 // full


def place():
    return lax.axis_index("pack"), lax.axis_index("cp"), lax.axis_index("hd")


def greet(peers):
    barrier = pltpu.get_barrier_semaphore()
    for peer in peers:
        pl.semaphore_signal(barrier, inc=1, device_id=peer, device_id_type=MESH)
    pl.semaphore_wait(barrier, len(peers))


def group_peers(ring):
    p, c, h = place()
    peers = [(1 - p, c, h), (p, c, h + 1 - 2 * lax.rem(h, 2)), (p, c, lax.rem(h + 2, 4))]
    peers += [(p, lax.rem(c + step, ring), h) for step in range(1, ring)]
    return peers


class Scatter:
    def __init__(self, ring, count, pick, buffers, sems, out, write):
        self.ring, self.count, self.pick = ring, count, pick
        self.load, self.own, self.b1, self.b2, self.b3 = buffers
        self.slots = self.load.shape[0]
        self.load_sem, self.send_sem, self.recv_sem = sems
        self.out, self.write = out, write
        self.p, self.c, self.h = place()
        self.hy, self.hx = self.h // 2, lax.rem(self.h, 2)
        self.core = (1 - self.p, self.c, self.h)
        self.xpeer = (self.p, self.c, self.hy * 2 + 1 - self.hx)
        self.ypeer = (self.p, self.c, (1 - self.hy) * 2 + self.hx)

    def remote(self, i, stage, src, dst, device):
        return pltpu.make_async_remote_copy(
            src_ref=src, dst_ref=dst, send_sem=self.send_sem.at[stage, i],
            recv_sem=self.recv_sem.at[stage, i], device_id=device, device_id_type=MESH)

    def copy0(self, i, src):
        return self.remote(i, 0, src, self.own.at[i], self.core)

    def copy1(self, i, first_y):
        if first_y:
            return self.remote(i, 1, self.own.at[i, :, 1 - self.hy], self.b1.at[i], self.ypeer)
        return self.remote(i, 1, self.own.at[i, :, :, 1 - self.hx], self.b1.at[i], self.xpeer)

    def copy2(self, i, first_y):
        if first_y:
            return self.remote(i, 2, self.own.at[i, :, self.hy, 1 - self.hx], self.b2.at[i], self.xpeer)
        return self.remote(i, 2, self.own.at[i, :, 1 - self.hy, self.hx], self.b2.at[i], self.ypeer)

    def copy3(self, i, step):
        peer = lax.rem(self.c + step, self.ring)
        return self.remote(i, 3, self.own.at[i, peer, self.hy, self.hx], self.b3.at[i, step - 1], (self.p, peer, self.h))

    def begin(self, i):
        def go(mine, other):
            slot = lax.rem(i, self.slots)
            pltpu.make_async_copy(mine, self.load.at[slot], self.load_sem.at[slot]).start()
            self.copy0(i, other).start()
        self.pick(i, self.p, go)

    def stage1(self, i, first_y):
        slot = lax.rem(i, self.slots)
        pltpu.make_async_copy(self.load.at[slot], self.load.at[slot], self.load_sem.at[slot]).wait()
        self.copy0(i, self.own.at[i]).wait_recv()
        def add(k, carry):
            self.own[i, k] = self.own[i, k] + self.load[slot, k]
            return carry
        lax.fori_loop(0, self.ring, add, 0)
        self.copy1(i, first_y).start()

    def stage2(self, i, first_y):
        self.copy1(i, first_y).wait_recv()
        def add(k, carry):
            for m in range(2):
                at = (i, k, self.hy, m) if first_y else (i, k, m, self.hx)
                self.own[at] = self.own[at] + self.b1[i, k, m]
            return carry
        lax.fori_loop(0, self.ring, add, 0)
        self.copy2(i, first_y).start()

    def stage3(self, i, first_y):
        self.copy2(i, first_y).wait_recv()
        def add(k, carry):
            at = (i, k, self.hy, self.hx)
            self.own[at] = self.own[at] + self.b2[i, k]
            return carry
        lax.fori_loop(0, self.ring, add, 0)
        for step in range(1, self.ring):
            self.copy3(i, step).start()

    def finish(self, i):
        pltpu.make_async_copy(self.b3.at[i], self.b3.at[i], self.recv_sem.at[3, i]).wait()
        total = self.own[i, self.c, self.hy, self.hx].astype(jnp.float32)
        for step in range(1, self.ring):
            total = total + self.b3[i, step - 1].astype(jnp.float32)
        self.write(i, total)

    def drain(self, i, first_y):
        self.copy0(i, self.own.at[i]).wait_send()
        self.copy1(i, first_y).wait_send()
        self.copy2(i, first_y).wait_send()
        pltpu.make_async_copy(self.b3.at[i], self.b3.at[i], self.send_sem.at[3, i]).wait()

    def step(self, t, ahead=3, lags=(0, 2, 4, 6)):
        pairs = (self.count + 1) // 2
        def both(pair, act):
            for first_y in (True, False):
                i = 2 * pair + (0 if first_y else 1)
                guard = (pair >= 0) & (i < self.count) & (i >= 0)
                pl.when(guard)(functools.partial(act, i, first_y))
        both(t, lambda i, f: self.begin(i))
        both(t - ahead - lags[0], self.stage1)
        both(t - ahead - lags[1], self.stage2)
        both(t - ahead - lags[2], self.stage3)
        both(t - ahead - lags[3], lambda i, f: self.finish(i))

    def steps(self, ahead=3, lags=(0, 2, 4, 6)):
        return (self.count + 1) // 2 + ahead + lags[3]

    def drain_all(self):
        def one(t, carry):
            for first_y in (True, False):
                i = 2 * t + (0 if first_y else 1)
                pl.when(i < self.count)(functools.partial(self.drain, i, first_y))
            return carry
        lax.fori_loop(0, (self.count + 1) // 2, one, 0)


def scatter_scratch(ring, count, rows, cols):
    bf = jnp.bfloat16
    return [
        pltpu.VMEM((8, ring, 2, 2, rows, cols), bf),
        pltpu.VMEM((count, ring, 2, 2, rows, cols), bf),
        pltpu.VMEM((count, ring, 2, rows, cols), bf),
        pltpu.VMEM((count, ring, rows, cols), bf),
        pltpu.VMEM((count, ring - 1, rows, cols), bf),
        pltpu.SemaphoreType.DMA((8,)),
        pltpu.SemaphoreType.DMA((4, count)),
        pltpu.SemaphoreType.DMA((4, count)),
    ]


def scatter_pick(grads, layout, cols):
    def pick(i, p, go):
        start = 0
        for ref, (size, outer) in zip(grads, layout):
            j = i - start
            def run(ref=ref, j=j, outer=outer):
                if outer:
                    go(ref.at[j, p], ref.at[j, 1 - p])
                else:
                    at = pl.ds(pl.multiple_of(lax.rem(j, 2) * cols, cols), cols)
                    go(ref.at[p, :, :, :, j // 2, :, at], ref.at[1 - p, :, :, :, j // 2, :, at])
            pl.when((j >= 0) & (j < size))(run)
            start += size
    return pick


def scatter_kernel(ring, layout, count, *refs):
    n = len(layout)
    grads, out = refs[:n], refs[n]
    load, own, b1, b2, b3, load_sem, send_sem, recv_sem = refs[n + 1:]
    greet(group_peers(ring))
    pick = scatter_pick(grads, layout, out.shape[-1])

    def write(i, total):
        out[i] = total

    work = Scatter(ring, count, pick, (load, own, b1, b2, b3), (load_sem, send_sem, recv_sem), out, write)
    def body(t, carry):
        work.step(t)
        return carry
    lax.fori_loop(0, work.steps(), body, 0)
    work.drain_all()


def scatter(grads, layout, ring, collective_id):
    rows, cols = grads[0].shape[-2:]
    count = sum(size for size, _ in layout)
    return pl.pallas_call(
        functools.partial(scatter_kernel, ring, layout, count),
        out_shape=jax.ShapeDtypeStruct((count, rows, cols), jnp.float32),
        in_specs=[pl.BlockSpec(memory_space=pl.ANY)] * len(grads),
        out_specs=pl.BlockSpec(memory_space=pltpu.VMEM),
        scratch_shapes=scatter_scratch(ring, count, rows, cols),
        compiler_params=pltpu.CompilerParams(collective_id=collective_id, has_side_effects=True, vmem_limit_bytes=60 * 2**20),
        name="rsum",
    )(*grads)


class Gather:
    def __init__(self, ring, count, pick, sems):
        self.ring, self.count, self.pick = ring, count, pick
        self.local_sem, self.send_sem, self.recv_sem = sems
        self.p, self.c, self.h = place()
        self.hy, self.hx = self.h // 2, lax.rem(self.h, 2)
        self.core = (1 - self.p, self.c, self.h)
        self.xpeer = (self.p, self.c, self.hy * 2 + 1 - self.hx)
        self.ypeer = (self.p, self.c, (1 - self.hy) * 2 + self.hx)

    def remote(self, i, stage, src, dst, device):
        return pltpu.make_async_remote_copy(
            src_ref=src, dst_ref=dst, send_sem=self.send_sem.at[stage, i],
            recv_sem=self.recv_sem.at[stage, i], device_id=device, device_id_type=MESH)

    def same(self, i, stage, ref, device):
        return self.remote(i, stage, ref, ref, device)

    def begin(self, i, first_x):
        def go(src, out):
            mine = out(self.p, self.c, self.hy, self.hx)
            pltpu.make_async_copy(src, mine, self.local_sem.at[i]).start()
            for step in range(1, self.ring):
                peer = (self.p, lax.rem(self.c + step, self.ring), self.h)
                self.remote(i, 0, src, mine, peer).start()
        self.pick(i, go)

    def stage1(self, i, first_x):
        def go(src, out):
            mine = out(self.p, self.c, self.hy, self.hx)
            pltpu.make_async_copy(src, mine, self.local_sem.at[i]).wait()
            rest = out(self.p, pl.ds(0, self.ring - 1), self.hy, self.hx)
            pltpu.make_async_copy(rest, rest, self.recv_sem.at[0, i]).wait()
            column = out(self.p, ALL, self.hy, self.hx)
            self.same(i, 1, column, self.xpeer if first_x else self.ypeer).start()
            self.same(i, 3, column, self.core).start()
        self.pick(i, go)

    def first(self, out, mine, first_x):
        if first_x:
            return out(self.p, ALL, self.hy, self.hx if mine else 1 - self.hx)
        return out(self.p, ALL, self.hy if mine else 1 - self.hy, self.hx)

    def second(self, out, mine, first_x):
        if first_x:
            return out(self.p, ALL, self.hy if mine else 1 - self.hy, ALL)
        return out(self.p, ALL, ALL, self.hx if mine else 1 - self.hx)

    def stage2(self, i, first_x):
        def go(src, out):
            came = self.first(out, False, first_x)
            self.same(i, 1, came, self.core).wait_recv()
            self.same(i, 2, self.second(out, True, first_x), self.ypeer if first_x else self.xpeer).start()
            self.same(i, 3, came, self.core).start()
        self.pick(i, go)

    def stage3(self, i, first_x):
        def go(src, out):
            came = self.second(out, False, first_x)
            self.same(i, 2, came, self.core).wait_recv()
            self.same(i, 3, came, self.core).start()
        self.pick(i, go)

    def finish(self, i, first_x):
        def go(src, out):
            half = out(1 - self.p, ALL, ALL, ALL)
            pltpu.make_async_copy(half, half, self.recv_sem.at[3, i]).wait()
        self.pick(i, go)

    def drain(self, i, first_x):
        def go(src, out):
            rest = out(self.p, pl.ds(0, self.ring - 1), self.hy, self.hx)
            pltpu.make_async_copy(rest, rest, self.send_sem.at[0, i]).wait()
            self.same(i, 1, self.first(out, True, first_x), self.core).wait_send()
            self.same(i, 2, self.second(out, True, first_x), self.core).wait_send()
            half = out(self.p, ALL, ALL, ALL)
            pltpu.make_async_copy(half, half, self.send_sem.at[3, i]).wait()
        self.pick(i, go)

    def step(self, t, ahead=3, lags=(0, 2, 4, 6)):
        pairs = (self.count + 1) // 2
        def both(pair, act):
            for first_x in (True, False):
                i = 2 * pair + (0 if first_x else 1)
                guard = (pair >= 0) & (i < self.count) & (i >= 0)
                pl.when(guard)(functools.partial(act, i, first_x))
        both(t, self.begin)
        both(t - ahead - lags[0], self.stage1)
        both(t - ahead - lags[1], self.stage2)
        both(t - ahead - lags[2], self.stage3)
        both(t - ahead - lags[3], self.finish)

    def steps(self, ahead=3, lags=(0, 2, 4, 6)):
        return (self.count + 1) // 2 + ahead + lags[3]

    def drain_all(self):
        def one(t, carry):
            for first_x in (True, False):
                i = 2 * t + (0 if first_x else 1)
                pl.when(i < self.count)(functools.partial(self.drain, i, first_x))
            return carry
        lax.fori_loop(0, (self.count + 1) // 2, one, 0)


def gather_sems(count):
    return [
        pltpu.SemaphoreType.DMA((count,)),
        pltpu.SemaphoreType.DMA((4, count)),
        pltpu.SemaphoreType.DMA((4, count)),
    ]


def gather_pick(src, wide, down, n_wide):
    cols = src.shape[-1]
    def pick(i, go):
        @pl.when(i < n_wide)
        def _():
            go(src.at[i], lambda p, c, y, x: wide.at[i, p, c, y, x])
        @pl.when(i >= n_wide)
        def _():
            j = i - n_wide
            at = pl.ds(pl.multiple_of(lax.rem(j, 2) * cols, cols), cols)
            go(src.at[i], lambda p, c, y, x: down.at[p, c, y, x, j // 2, :, at])
    return pick


def gather_kernel(ring, n_wide, count, src, wide, down, *sems):
    greet(group_peers(ring))
    work = Gather(ring, count, gather_pick(src, wide, down, n_wide), sems)
    def body(t, carry):
        work.step(t)
        return carry
    lax.fori_loop(0, work.steps(), body, 0)
    work.drain_all()


def gather(src, n_wide, ring, collective_id):
    count, rows, cols = src.shape
    return pl.pallas_call(
        functools.partial(gather_kernel, ring, n_wide, count),
        out_shape=(
            jax.ShapeDtypeStruct((n_wide, 2, ring, 2, 2, rows, cols), src.dtype),
            jax.ShapeDtypeStruct((2, ring, 2, 2, (count - n_wide) // 2, rows, 2 * cols), src.dtype),
        ),
        in_specs=[ANY],
        out_specs=(ANY, ANY),
        scratch_shapes=gather_sems(count),
        compiler_params=pltpu.CompilerParams(collective_id=collective_id, has_side_effects=True),
        name="collect",
    )(src)


def dot_tb(a, b):
    return lax.dot_general(a, b, (((1,), (1,)), ((), ())), preferred_element_type=jnp.float32)


def dot(a, b):
    return jnp.dot(a, b, preferred_element_type=jnp.float32)


def lanes(rows):
    return lax.broadcasted_iota(jnp.int32, (rows, 128), 1)


def split3(x):
    hi = x.astype(jnp.bfloat16).astype(jnp.float32)
    mid = (x - hi).astype(jnp.bfloat16).astype(jnp.float32)
    lo = x - hi - mid
    return hi, mid, lo


def at_lanes(base, first, values):
    lane = lanes(base.shape[0])
    for n, value in enumerate(values):
        base = jnp.where(lane == first + n, value, base)
    return base


def halves(x):
    return x, pltpu.roll(x, 64, 1)


def build_keys(pair, k_ref, v_ref, kf_ref, ka, va, kt=None):
    at = pl.ds(pl.multiple_of(pair * 128, 128), 128)
    rows = k_ref.shape[0]
    chunk = 512
    def one(n, carry):
        r = pl.ds(pl.multiple_of(n * chunk, chunk), chunk)
        lane = lanes(chunk)
        keys = halves(k_ref[r, at].astype(jnp.float32))
        values = halves(v_ref[r, at].astype(jnp.float32))
        feat = kf_ref[r, :].astype(jnp.float32)
        for m in range(2):
            full = jnp.where(lane < 64, keys[m], feat)
            ka[m, r, :] = full.astype(jnp.bfloat16)
            if kt is not None:
                kt[m, :, r] = full.T.astype(jnp.bfloat16)
            ones = jnp.where(lane < 67, 1.0, 0.0)
            va[m, r, :] = jnp.where(lane < 64, values[m], ones).astype(jnp.bfloat16)
        return carry
    lax.fori_loop(0, rows // chunk, one, 0)


def forward_block(pair, n, q_ref, qf_ref, hs_ref, ka, va, o_ref, of_ref, qa_ref):
    at = pl.ds(pl.multiple_of(pair * 128, 128), 128)
    r = pl.ds(pl.multiple_of(n * QB, QB), QB)
    lane = lanes(QB)
    queries = halves(q_ref[r, at].astype(jnp.float32) * (1.0 / math.sqrt(HDIM)))
    feat = qf_ref[r, :].astype(jnp.float32)
    row = lax.broadcasted_iota(jnp.int32, (QB, QB), 0)
    col = lax.broadcasted_iota(jnp.int32, (QB, QB), 1)
    outs = []
    for m in range(2):
        qa = jnp.where(lane < 64, queries[m], feat * hs_ref[pl.ds(pair * 2 + m, 1), :])
        qb = qa.astype(jnp.bfloat16)
        def part(first, size, mask=None):
            keys = pl.ds(pl.multiple_of(n * QB + first, QB), size)
            s = dot_tb(qb, ka[m, keys, :])
            if mask is not None:
                s = jnp.where(mask, s, FAR)
            return dot(jnp.exp(s).astype(jnp.bfloat16), va[m, keys, :])
        o = part(0, QB, col >= row) + part(QB, SPAN - 2 * QB) + part(SPAN - QB, QB, col <= row)
        total = o[:, 64:65]
        outs.append(o * (1.0 / total))
        hi, mid, lo = split3(-jnp.log(total))
        qa_ref[pair * 2 + m, r, :] = at_lanes(qa, 80, (hi, mid, lo)).astype(jnp.bfloat16)
    both = jnp.where(lane < 64, outs[0], pltpu.roll(outs[1], 64, 1))
    of_ref[r, at] = both
    o_ref[r, at] = both.astype(jnp.bfloat16)


def forward_kernel(q_ref, k_ref, v_ref, kf_ref, qf_ref, hs_ref, o_ref, of_ref, qa_ref, ka, va):
    blocks = q_ref.shape[0] // QB
    def pair_step(pair, carry):
        build_keys(pair, k_ref, v_ref, kf_ref, ka, va)
        def step(n, c):
            forward_block(pair, n, q_ref, qf_ref, hs_ref, ka, va, o_ref, of_ref, qa_ref)
            return c
        lax.fori_loop(0, blocks, step, 0)
        return carry
    lax.fori_loop(0, 2, pair_step, 0)


def attention_forward(q, k, v, kf, qf, hs):
    rows, ext = q.shape[0], k.shape[0]
    return pl.pallas_call(
        forward_kernel,
        out_shape=(
            jax.ShapeDtypeStruct((rows, 256), jnp.bfloat16),
            jax.ShapeDtypeStruct((rows, 256), jnp.float32),
            jax.ShapeDtypeStruct((4, rows, 128), jnp.bfloat16),
        ),
        in_specs=[VM] * 6,
        out_specs=(VM, VM, VM),
        scratch_shapes=[pltpu.VMEM((2, ext, 128), jnp.bfloat16), pltpu.VMEM((2, ext, 128), jnp.bfloat16)],
        compiler_params=pltpu.CompilerParams(vmem_limit_bytes=56 * 2**20),
        name="attend",
    )(q, k, v, kf, qf, hs)


def backward_block(pair, n, qf_ref, qa_ref, do_ref, of_ref, ka, va, kt, dka, dva, dq_ref, same, every):
    at = pl.ds(pl.multiple_of(pair * 128, 128), 128)
    r = pl.ds(pl.multiple_of(n * QB, QB), QB)
    lane = lanes(QB)
    grads = do_ref[r, at].astype(jnp.float32)
    terms = grads * of_ref[r, at]
    pieces = halves(grads)
    row = lax.broadcasted_iota(jnp.int32, (QB, QB), 0)
    col = lax.broadcasted_iota(jnp.int32, (QB, QB), 1)
    dqs = []
    qft = qf_ref[r, :].astype(jnp.float32).T[64:72, :]
    for m in range(2):
        own = (lane < 64) if m == 0 else (lane >= 64)
        delta = jnp.sum(jnp.where(own, terms, 0.0), axis=1, keepdims=True)
        da = at_lanes(jnp.where(lane < 64, pieces[m], 0.0), 64, split3(-delta)).astype(jnp.bfloat16)
        qb = qa_ref[pair * 2 + m, r, :]
        dq = jnp.zeros((128, QB), jnp.float32)
        for first, size, edge in ((0, QB, 0), (QB, SPAN - 2 * QB, None), (SPAN - QB, QB, 1)):
            keys = pl.ds(pl.multiple_of(n * QB + first, QB), size)
            s = dot_tb(ka[m, keys, :], qb)
            if edge is not None:
                s = jnp.where((row >= col) if edge == 0 else (row <= col), s, FAR)
            p = jnp.exp(s)
            dp = dot_tb(va[m, keys, :], da)
            ds = (p * dp).astype(jnp.bfloat16)
            dva[m, keys, :] += dot(p.astype(jnp.bfloat16), da)
            dka[m, keys, :] += dot(ds, qb)
            dq = dq + dot(kt[m, :, keys], ds)
        dqs.append(dq[:64, :])
        sums = dq[64:72, :]
        pick = lax.broadcasted_iota(jnp.int32, (8, QB), 0) < 4
        h = pair * 2 + m
        same[h] += jnp.where(pick, sums * qft, 0.0)
        every[h] += jnp.where(pick, sums, 0.0)
    dq_ref[r, at] = (jnp.concatenate(dqs, axis=0).T * (1.0 / math.sqrt(HDIM))).astype(dq_ref.dtype)


def backward_finish(pair, dka, dva, dk_ref, dv_ref):
    at = pl.ds(pl.multiple_of(pair * 128, 128), 128)
    chunk = 512
    def one(n, carry):
        r = pl.ds(pl.multiple_of(n * chunk, chunk), chunk)
        lane = lanes(chunk)
        dk_ref[r, at] = jnp.where(lane < 64, dka[0, r, :], pltpu.roll(dka[1, r, :], 64, 1)).astype(dk_ref.dtype)
        dv_ref[r, at] = jnp.where(lane < 64, dva[0, r, :], pltpu.roll(dva[1, r, :], 64, 1)).astype(dv_ref.dtype)
        return carry
    lax.fori_loop(0, dk_ref.shape[0] // chunk, one, 0)


def backward_kernel(k_ref, v_ref, kf_ref, qf_ref, qa_ref, do_ref, of_ref, dq_ref, dk_ref, dv_ref, bias_ref, ka, va, kt, dka, dva, same, every):
    blocks = dq_ref.shape[0] // QB
    same[...] = jnp.zeros_like(same)
    every[...] = jnp.zeros_like(every)
    def pair_step(pair, carry):
        build_keys(pair, k_ref, v_ref, kf_ref, ka, va, kt)
        dka[...] = jnp.zeros_like(dka)
        dva[...] = jnp.zeros_like(dva)
        def step(n, c):
            backward_block(pair, n, qf_ref, qa_ref, do_ref, of_ref, ka, va, kt, dka, dva, dq_ref, same, every)
            return c
        lax.fori_loop(0, blocks, step, 0)
        backward_finish(pair, dka, dva, dk_ref, dv_ref)
        return carry
    lax.fori_loop(0, 2, pair_step, 0)
    def total(x):
        return jnp.sum(jnp.sum(x, axis=1, keepdims=True), axis=2, keepdims=True)
    s, e = total(same[...]), total(every[...])
    lane = lax.broadcasted_iota(jnp.int32, (4, 1, 128), 2)
    bias_ref[...] = jnp.where(lane == 0, s, jnp.where(lane == 1, e - s, 0.0))


def attention_backward(k, v, kf, qf, qa, do, of):
    rows, ext = do.shape[0], k.shape[0]
    f32, bf = jnp.float32, jnp.bfloat16
    return pl.pallas_call(
        backward_kernel,
        out_shape=(
            jax.ShapeDtypeStruct((rows, 256), f32),
            jax.ShapeDtypeStruct((ext, 256), f32),
            jax.ShapeDtypeStruct((ext, 256), f32),
            jax.ShapeDtypeStruct((4, 1, 128), f32),
        ),
        in_specs=[VM] * 7,
        out_specs=(VM,) * 4,
        scratch_shapes=[
            pltpu.VMEM((2, ext, 128), bf), pltpu.VMEM((2, ext, 128), bf), pltpu.VMEM((2, 128, ext), bf),
            pltpu.VMEM((2, ext, 128), f32), pltpu.VMEM((2, ext, 128), f32),
            pltpu.VMEM((4, 8, QB), f32), pltpu.VMEM((4, 8, QB), f32)],
        compiler_params=pltpu.CompilerParams(vmem_limit_bytes=60 * 2**20),
        name="attback",
    )(k, v, kf, qf, qa, do, of)


def key_features(seg_ext, var_ext):
    bf = jnp.bfloat16
    ids = jnp.arange(4)[None, :]
    var = (var_ext[:, None] == ids).astype(bf)
    seg = jnp.where(seg_ext[:, None] == ids, 0.0, FAR).astype(bf)
    n = seg_ext.shape[0]
    return jnp.concatenate([jnp.zeros((n, 64), bf), var, var, var, seg, jnp.ones((n, 3), bf), jnp.zeros((n, 45), bf)], axis=1)


def query_features(seg, var):
    bf = jnp.bfloat16
    ids = jnp.arange(4)[None, :]
    one = (var[:, None] == ids).astype(bf)
    doc = (seg[:, None] == ids).astype(bf)
    n = seg.shape[0]
    return jnp.concatenate([jnp.zeros((n, 64), bf), one, one, one, doc, jnp.zeros((n, 48), bf)], axis=1)


def head_scales(bias):
    hi, mid, lo = split3(bias[:, :1] - bias[:, 1:])
    n = bias.shape[0]
    wide = [jnp.broadcast_to(x, (n, 4)) for x in (hi, mid, lo)]
    return jnp.concatenate([jnp.zeros((n, 64))] + wide + [jnp.ones((n, 4)), jnp.zeros((n, 48))], axis=1)


def scale_of(x):
    return lax.rsqrt(jnp.mean(x * x, axis=-1, keepdims=True) + EPS)


def head_mean(x):
    row = lax.broadcasted_iota(jnp.int32, (128, 128), 0)
    col = lax.broadcasted_iota(jnp.int32, (128, 128), 1)
    group = jnp.where((row < 64) == (col < 64), 1.0 / HDIM, 0.0).astype(BF)
    hi = x.astype(BF)
    rest = x - hi.astype(F32)
    mid = rest.astype(BF)
    low = (rest - mid.astype(F32)).astype(BF)
    return dot(hi, group) + dot(mid, group) + dot(low, group)


def swap_halves(x):
    lane = lax.rem(lanes(x.shape[0]), 64)
    return jnp.where(lane < 32, pltpu.roll(x, 96, 1), pltpu.roll(x, 32, 1))


def project_kernel(x_ref, gain_ref, w_ref, cos_ref, sin_ref, hg_ref, raw_ref, out_ref, nrm):
    t = pl.program_id(0)

    @pl.when(t == 0)
    def _():
        x = x_ref[...].astype(F32)
        nrm[...] = (x * scale_of(x) * gain_ref[...]).astype(BF)

    raw = dot(nrm[...], w_ref[0]).astype(BF)
    raw_ref[...] = raw

    @pl.when(t >= 4)
    def _():
        out_ref[...] = raw

    @pl.when(t < 4)
    def _():
        gain = hg_ref[pl.ds(t // 2, 1), :]
        for n in range(raw.shape[1] // 128):
            u = raw[:, n * 128:(n + 1) * 128].astype(F32)
            y = u * lax.rsqrt(head_mean(u * u) + EPS) * gain
            y = y * cos_ref[...] + swap_halves(y) * sin_ref[...]
            out_ref[:, n * 128:(n + 1) * 128] = y.astype(BF)


def project(x, gain, wide, cosine, sine, head_gains):
    rows, width = x.shape
    def fixed(*shape):
        return pl.BlockSpec(shape, lambda t: (0,) * len(shape))
    tile = pl.BlockSpec((rows, 512), lambda t: (0, t))
    return pl.pallas_call(
        project_kernel,
        grid=(6,),
        out_shape=(jax.ShapeDtypeStruct((rows, 3 * width), BF),) * 2,
        in_specs=[fixed(rows, width), fixed(1, width), pl.BlockSpec((1, width, 512), lambda t: (t, 0, 0)),
                  fixed(rows, 128), fixed(rows, 128), fixed(2, 128)],
        out_specs=(tile, tile),
        scratch_shapes=[pltpu.VMEM((rows, width), BF)],
        compiler_params=pltpu.CompilerParams(vmem_limit_bytes=48 * MIB),
        name="project",
    )(x, gain, wide, cosine, sine, head_gains)


def norm_back_rows(u, r, gain, dy):
    scaled = dy * gain
    du = r * scaled - u * (r * r * r) * jnp.mean(scaled * u, axis=-1, keepdims=True)
    return du, jnp.sum(dy * u * r, axis=0, keepdims=True)


def ffn_kernel(x_ref, heads_ref, cot_ref, gain_ref, wo_ref, wg_ref, wu_ref, wd_ref,
               out_ref, dhid_ref, dheads_ref, gg_ref, gu_ref, gd_ref, go_ref, ggain_ref,
               hidden, acc, dnorm, nrm, nrm_t):
    t = pl.program_id(0)
    cot = cot_ref[...]

    @pl.when(t == 0)
    def _():
        heads = heads_ref[...]
        for n in range(2):
            at = slice(n * 512, (n + 1) * 512)
            hidden[:, at] = x_ref[:, at].astype(F32) + dot(heads, wo_ref[n])
        h = hidden[...]
        y = h * scale_of(h) * gain_ref[...]
        nrm[...] = y.astype(BF)
        nrm_t[...] = y.T.astype(BF)
        acc[...] = h
        dnorm[...] = jnp.zeros_like(dnorm)

    normed = nrm[...]
    wg, wu, wd = wg_ref[0], wu_ref[0], wd_ref[...]
    gate = dot(normed, wg)
    up = dot(normed, wu)
    d_product = dot_tb(cot, wd)
    sig = jax.nn.sigmoid(gate)
    silu = gate * sig
    product = silu * up
    prod_b = product.astype(BF)
    d_gate = (d_product * up * sig * (1.0 + gate * (1.0 - sig))).astype(BF)
    d_up = (d_product * silu).astype(BF)
    acc[...] += dot(prod_b, wd)
    gd_ref[...] = dot(prod_b.astype(F32).T.astype(BF), cot).astype(BF)
    gg_ref[0] = dot(nrm_t[...], d_gate).astype(BF)
    gu_ref[0] = dot(nrm_t[...], d_up).astype(BF)
    dnorm[...] += dot_tb(d_gate, wg) + dot_tb(d_up, wu)

    @pl.when(t == pl.num_programs(0) - 1)
    def _():
        out_ref[...] = acc[...].astype(BF)
        h = hidden[...]
        du, terms = norm_back_rows(h, scale_of(h), gain_ref[...], dnorm[...])
        ggain_ref[...] = terms
        d_hidden = cot_ref[...].astype(F32) + du
        dhid_ref[...] = d_hidden
        d_attn = d_hidden.astype(BF)
        heads_t = heads_ref[...].astype(F32).T.astype(BF)
        total = jnp.zeros(d_hidden.shape, F32)
        for n in range(2):
            at = slice(n * 512, (n + 1) * 512)
            go_ref[n] = dot(heads_t, d_attn[:, at]).astype(BF)
            total = total + dot_tb(d_attn[:, at], wo_ref[n])
        dheads_ref[...] = total.astype(BF)


def ffn(x, heads, cot, gain, wide, down):
    rows, width = x.shape
    ff = down.shape[0]
    steps = ff // 512
    def fixed(*shape):
        return pl.BlockSpec(shape, lambda t: (0,) * len(shape))
    def items(first):
        return pl.BlockSpec((1, width, 512), lambda t: (first + t, 0, 0))
    return pl.pallas_call(
        ffn_kernel,
        grid=(steps,),
        out_shape=(
            jax.ShapeDtypeStruct((rows, width), BF), jax.ShapeDtypeStruct((rows, width), F32),
            jax.ShapeDtypeStruct((rows, width), BF),
            jax.ShapeDtypeStruct((steps, width, 512), BF), jax.ShapeDtypeStruct((steps, width, 512), BF),
            jax.ShapeDtypeStruct((ff, width), BF), jax.ShapeDtypeStruct((2, width, 512), BF),
            jax.ShapeDtypeStruct((1, width), F32)),
        in_specs=[fixed(rows, width), fixed(rows, width), fixed(rows, width), fixed(1, width),
                  pl.BlockSpec((2, width, 512), lambda t: (0, 0, 0)), items(2), items(10),
                  pl.BlockSpec((512, width), lambda t: (t, 0))],
        out_specs=(fixed(rows, width), fixed(rows, width), fixed(rows, width), items(0), items(0),
                   pl.BlockSpec((512, width), lambda t: (t, 0)), fixed(2, width, 512), fixed(1, width)),
        scratch_shapes=[pltpu.VMEM((rows, width), F32), pltpu.VMEM((rows, width), F32), pltpu.VMEM((rows, width), F32),
                        pltpu.VMEM((rows, width), BF), pltpu.VMEM((width, rows), BF)],
        compiler_params=pltpu.CompilerParams(vmem_limit_bytes=60 * MIB),
        name="feedforward",
    )(x, heads, cot, gain, wide, wide, wide, down)


def unproject_kernel(x_ref, gain_ref, w_ref, cos_ref, sin_ref, hg_ref, raw_ref, d_ref, dhid_ref,
                     gw_ref, gin_ref, ggain_ref, ghead_ref, nrm_t, dnorm):
    t = pl.program_id(0)

    @pl.when(t == 0)
    def _():
        x = x_ref[...].astype(F32)
        nrm_t[...] = (x * scale_of(x) * gain_ref[...]).T.astype(BF)
        dnorm[...] = jnp.zeros_like(dnorm)
        ghead_ref[...] = jnp.zeros_like(ghead_ref)

    def use(d_proj):
        gw_ref[0] = dot(nrm_t[...], d_proj).astype(BF)
        dnorm[...] += dot_tb(d_proj, w_ref[0])

    @pl.when(t >= 4)
    def _():
        use(d_ref[...])

    @pl.when(t < 4)
    def _():
        kind = t // 2
        gain = hg_ref[pl.ds(kind, 1), :]
        pieces = []
        for n in range(d_ref.shape[1] // 128):
            at = slice(n * 128, (n + 1) * 128)
            u = raw_ref[:, at].astype(F32)
            dy = d_ref[:, at].astype(F32)
            dy = dy * cos_ref[...] - swap_halves(dy) * sin_ref[...]
            r = lax.rsqrt(head_mean(u * u) + EPS)
            scaled = dy * gain
            pieces.append((r * scaled - u * (r * r * r) * head_mean(scaled * u)).astype(BF))
            ghead_ref[pl.ds(kind, 1), :] += jnp.sum(dy * u * r, axis=0, keepdims=True)
        use(jnp.concatenate(pieces, axis=1))

    @pl.when(t == 5)
    def _():
        x = x_ref[...].astype(F32)
        du, terms = norm_back_rows(x, scale_of(x), gain_ref[...], dnorm[...])
        gin_ref[...] = dhid_ref[...] + du
        ggain_ref[...] = terms


def unproject(x, gain, wide, cosine, sine, head_gains, raw, grads, d_hidden):
    rows, width = x.shape
    def fixed(*shape):
        return pl.BlockSpec(shape, lambda t: (0,) * len(shape))
    tile = pl.BlockSpec((rows, 512), lambda t: (0, t))
    item = pl.BlockSpec((1, width, 512), lambda t: (t, 0, 0))
    return pl.pallas_call(
        unproject_kernel,
        grid=(6,),
        out_shape=(jax.ShapeDtypeStruct((6, width, 512), BF), jax.ShapeDtypeStruct((rows, width), F32),
                   jax.ShapeDtypeStruct((1, width), F32), jax.ShapeDtypeStruct((2, 128), F32)),
        in_specs=[fixed(rows, width), fixed(1, width), item, fixed(rows, 128), fixed(rows, 128), fixed(2, 128),
                  tile, tile, fixed(rows, width)],
        out_specs=(item, fixed(rows, width), fixed(1, width), fixed(2, 128)),
        scratch_shapes=[pltpu.VMEM((width, rows), BF), pltpu.VMEM((rows, width), F32)],
        compiler_params=pltpu.CompilerParams(vmem_limit_bytes=48 * MIB),
        name="unproject",
    )(x, gain, wide, cosine, sine, head_gains, raw, grads, d_hidden)


def remote(src, dst, send, recv, device):
    return pltpu.make_async_remote_copy(
        src_ref=src, dst_ref=dst, send_sem=send, recv_sem=recv, device_id=device, device_id_type=MESH)


def local_copy(src, dst, sem):
    return pltpu.make_async_copy(src, dst, sem)


def wide_at(first):
    return pl.ds(pl.multiple_of(first, 256), 256)


class Rim:
    def __init__(self, ring):
        self.p, self.c, self.h = place()
        self.ring = ring
        self.has_low, self.has_high = self.c > 0, self.c < ring - 1
        self.low = lax.rem(self.c + ring - 1, ring)
        self.high = lax.rem(self.c + 1, ring)
        self.low_edge = self.has_low & (self.h == 0)
        self.high_edge = self.has_high & (self.h == 3)

    def greet(self):
        beyond = [(self.p, block, n) for block in (self.low, self.high) for n in range(4)]
        greet(group_peers(self.ring) + [(self.p, self.c, 3 - self.h)] + beyond)


def attend_kernel(ring, n_wide, count, src, qkv, kf_ref, qf_ref, hs_ref,
                  tok_ref, of_ref, qa_ref, kx, vx, wide, down,
                  q_loc, o_loc, ka, va, local_sem, a2a_send, a2a_recv, rim_send, rim_recv, out_send, out_recv, *sems):
    p, c, h = place()
    rim = Rim(ring)
    rim.greet()
    rows = tok_ref.shape[0]
    width = tok_ref.shape[1]
    mine = pl.ds(pl.multiple_of(h * rows, rows), rows)
    mine_x = pl.ds(pl.multiple_of(HALF + h * rows, rows), rows)
    group = 4 * rows
    places = ((0, q_loc, mine), (1, kx, mine_x), (2, vx, mine_x))

    def part(kind, head):
        return qkv.at[:, wide_at(kind * width + head * 256)]

    for kind, ref, at in places:
        local_copy(part(kind, h), ref.at[at], local_sem.at[kind]).start()
        for step in range(1, 4):
            to = lax.rem(h + step, 4)
            remote(part(kind, to), ref.at[at], a2a_send.at[kind], a2a_recv.at[kind], (p, c, to)).start()

    low_rim, high_rim = pl.ds(0, HALF), pl.ds(HALF + group, HALF)
    for kind, ref in ((0, kx), (1, vx)):
        @pl.when(rim.high_edge)
        def _():
            for to in range(4):
                remote(part(kind + 1, to), ref.at[low_rim], rim_send.at[0, kind], rim_recv.at[0, kind], (p, rim.high, to)).start()
        @pl.when(rim.low_edge)
        def _():
            for to in range(4):
                remote(part(kind + 1, to), ref.at[high_rim], rim_send.at[1, kind], rim_recv.at[1, kind], (p, rim.low, to)).start()
        @pl.when(jnp.logical_not(rim.has_low))
        def _():
            ref[0:HALF, :] = jnp.zeros((HALF, 256), BF)
        @pl.when(jnp.logical_not(rim.has_high))
        def _():
            ref[HALF + group:2 * HALF + group, :] = jnp.zeros((HALF, 256), BF)

    work = Gather(ring, count, gather_pick(src, wide, down, n_wide), sems)
    def begin(t, carry):
        work.step(t)
        return carry
    lax.fori_loop(0, 3, begin, 0)

    three = pl.ds(0, 3 * rows)
    for kind, ref, at in places:
        local_copy(ref.at[at], ref.at[at], local_sem.at[kind]).wait()
        local_copy(ref.at[three], ref.at[three], a2a_recv.at[kind]).wait()
    for kind, ref in ((0, kx), (1, vx)):
        @pl.when(rim.has_low)
        def _():
            local_copy(ref.at[low_rim], ref.at[low_rim], rim_recv.at[0, kind]).wait()
        @pl.when(rim.has_high)
        def _():
            local_copy(ref.at[high_rim], ref.at[high_rim], rim_recv.at[1, kind]).wait()

    blocks = group // QB
    def pair_step(pair, carry):
        build_keys(pair, kx, vx, kf_ref, ka, va)
        def step(n, c):
            work.step(3 + pair * blocks + n)
            forward_block(pair, n, q_loc, qf_ref, hs_ref, ka, va, o_loc, of_ref, qa_ref)
            return c
        lax.fori_loop(0, blocks, step, 0)
        return carry
    lax.fori_loop(0, 2, pair_step, 0)

    heads = wide_at(h * 256)
    local_copy(o_loc.at[mine], tok_ref.at[:, heads], local_sem.at[3]).start()
    for step in range(1, 4):
        to = lax.rem(h + step, 4)
        theirs = pl.ds(pl.multiple_of(to * rows, rows), rows)
        remote(o_loc.at[theirs], tok_ref.at[:, heads], out_send, out_recv, (p, c, to)).start()
    def rest(t, carry):
        work.step(t)
        return carry
    lax.fori_loop(3 + 2 * blocks, work.steps(), rest, 0)
    local_copy(o_loc.at[mine], tok_ref.at[:, heads], local_sem.at[3]).wait()
    three_wide = tok_ref.at[:, pl.ds(0, 768)]
    local_copy(three_wide, three_wide, out_recv).wait()
    local_copy(three_wide, three_wide, out_send).wait()
    for kind, ref, at in places:
        local_copy(ref.at[three], ref.at[three], a2a_send.at[kind]).wait()
    for kind in range(2):
        four = qkv.at[:, pl.ds(0, 4 * 256)]
        @pl.when(rim.high_edge)
        def _():
            local_copy(four, four, rim_send.at[0, kind]).wait()
        @pl.when(rim.low_edge)
        def _():
            local_copy(four, four, rim_send.at[1, kind]).wait()
    work.drain_all()


def attend(src, qkv, kf, qf, hs, n_wide, ring, collective_id):
    rows, width = qkv.shape[0], qkv.shape[1] // 3
    group = 4 * rows
    ext = group + 2 * HALF
    count, r, w = src.shape
    dma = pltpu.SemaphoreType.DMA
    return pl.pallas_call(
        functools.partial(attend_kernel, ring, n_wide, count),
        out_shape=(
            jax.ShapeDtypeStruct((rows, width), BF),
            jax.ShapeDtypeStruct((group, 256), F32),
            jax.ShapeDtypeStruct((4, group, 128), BF),
            jax.ShapeDtypeStruct((ext, 256), BF),
            jax.ShapeDtypeStruct((ext, 256), BF),
            jax.ShapeDtypeStruct((n_wide, 2, ring, 2, 2, r, w), BF),
            jax.ShapeDtypeStruct((2, ring, 2, 2, (count - n_wide) // 2, r, 2 * w), BF),
        ),
        in_specs=[ANY, ANY, VM, VM, VM],
        out_specs=(VM,) * 5 + (ANY, ANY),
        scratch_shapes=[
            pltpu.VMEM((group, 256), BF), pltpu.VMEM((group, 256), BF),
            pltpu.VMEM((2, ext, 128), BF), pltpu.VMEM((2, ext, 128), BF),
            dma((4,)), dma((3,)), dma((3,)), dma((2, 2)), dma((2, 2)), dma, dma,
        ] + gather_sems(count),
        compiler_params=pltpu.CompilerParams(collective_id=collective_id, has_side_effects=True, vmem_limit_bytes=56 * MIB),
        name="attend",
    )(src, qkv, kf, qf, hs)


def return_kernel(ring, layout, count, *refs):
    n = len(layout)
    grads = refs[:n]
    (d_tok, kx, vx, kf_ref, qf_ref, qa_ref, of_ref, back, bias_ref, out,
     do_loc, dq_loc, dk_loc, dv_loc, rims, ka, va, kt, dka, dva, same, every,
     local_sem, in_send, in_recv, back_send, back_recv, rim_send, rim_recv,
     load, own, b1, b2, b3, load_sem, send_sem, recv_sem) = refs[n:]
    p, c, h = place()
    rim = Rim(ring)
    rim.greet()
    rows, width = d_tok.shape
    group = 4 * rows
    mine = pl.ds(pl.multiple_of(h * rows, rows), rows)
    three = pl.ds(0, 3 * rows)

    local_copy(d_tok.at[:, wide_at(h * 256)], do_loc.at[mine], local_sem.at[0]).start()
    for step in range(1, 4):
        to = lax.rem(h + step, 4)
        remote(d_tok.at[:, wide_at(to * 256)], do_loc.at[mine], in_send, in_recv, (p, c, to)).start()

    def write(i, total):
        out[i] = total

    work = Scatter(ring, count, scatter_pick(grads, layout, out.shape[-1]), (load, own, b1, b2, b3),
                   (load_sem, send_sem, recv_sem), out, write)
    def begin(t, carry):
        work.step(t)
        return carry
    lax.fori_loop(0, 3, begin, 0)
    same[...] = jnp.zeros_like(same)
    every[...] = jnp.zeros_like(every)
    local_copy(do_loc.at[mine], do_loc.at[mine], local_sem.at[0]).wait()
    local_copy(do_loc.at[three], do_loc.at[three], in_recv).wait()

    blocks = group // QB
    def pair_step(pair, carry):
        build_keys(pair, kx, vx, kf_ref, ka, va, kt)
        dka[...] = jnp.zeros_like(dka)
        dva[...] = jnp.zeros_like(dva)
        def step(m, c):
            work.step(3 + pair * blocks + m)
            backward_block(pair, m, qf_ref, qa_ref, do_loc, of_ref, ka, va, kt, dka, dva, dq_loc, same, every)
            return c
        lax.fori_loop(0, blocks, step, 0)
        backward_finish(pair, dka, dva, dk_loc, dv_loc)
        return carry
    lax.fori_loop(0, 2, pair_step, 0)

    heads = wide_at(h * 256)
    trios = ((0, dq_loc, 0), (1, dk_loc, HALF), (2, dv_loc, HALF))
    for kind, ref, skip in trios:
        at = wide_at(kind * width + h * 256)
        for step in range(4):
            to = lax.rem(h + step, 4)
            theirs = ref.at[pl.ds(pl.multiple_of(skip + to * rows, rows), rows)]
            if step == 0:
                local_copy(theirs, back.at[:, at], local_sem.at[1 + kind]).start()
            else:
                remote(theirs, back.at[:, at], back_send.at[kind], back_recv.at[kind], (p, c, to)).start()
    for kind, ref in ((0, dk_loc), (1, dv_loc)):
        @pl.when(rim.has_low)
        def _():
            remote(ref.at[pl.ds(0, HALF)], rims.at[kind, :, heads], rim_send.at[0, kind], rim_recv.at[kind], (p, rim.low, 3)).start()
        @pl.when(rim.has_high)
        def _():
            remote(ref.at[pl.ds(HALF + group, HALF)], rims.at[kind, :, heads], rim_send.at[1, kind], rim_recv.at[kind], (p, rim.high, 0)).start()

    def total(x):
        return jnp.sum(jnp.sum(x, axis=1, keepdims=True), axis=2, keepdims=True)
    s, e = total(same[...]), total(every[...])
    lane = lax.broadcasted_iota(jnp.int32, (4, 1, 128), 2)
    bias_ref[...] = jnp.where(lane == 0, s, jnp.where(lane == 1, e - s, 0.0))

    def rest(t, carry):
        work.step(t)
        return carry
    lax.fori_loop(3 + 2 * blocks, work.steps(), rest, 0)

    for kind, ref, skip in trios:
        at = wide_at(kind * width + h * 256)
        local_copy(back.at[:, at], back.at[:, at], local_sem.at[1 + kind]).wait()
        part = back.at[:, pl.ds(0, 768)]
        local_copy(part, part, back_recv.at[kind]).wait()
    for kind in range(2):
        @pl.when(rim.low_edge | rim.high_edge)
        def _():
            local_copy(rims.at[kind], rims.at[kind], rim_recv.at[kind]).wait()
            for n in range(4):
                rows_n = pl.ds(n * 128, 128)
                at = pl.ds((kind + 1) * width, width)
                back[rows_n, at] = (back[rows_n, at].astype(F32) + rims[kind, rows_n, :].astype(F32)).astype(BF)
    local_copy(do_loc.at[three], do_loc.at[three], in_send).wait()
    for kind in range(3):
        part = back.at[:, pl.ds(0, 768)]
        local_copy(part, part, back_send.at[kind]).wait()
    for kind, ref in ((0, dk_loc), (1, dv_loc)):
        rim_part = ref.at[pl.ds(0, HALF)]
        @pl.when(rim.has_low)
        def _():
            local_copy(rim_part, rim_part, rim_send.at[0, kind]).wait()
        @pl.when(rim.has_high)
        def _():
            local_copy(rim_part, rim_part, rim_send.at[1, kind]).wait()
    work.drain_all()


def attend_back(grads, layout, d_tok, kx, vx, kf, qf, qa, of, ring, collective_id):
    rows, width = d_tok.shape
    group = 4 * rows
    ext = group + 2 * HALF
    r, w = grads[0].shape[-2:]
    count = sum(size for size, _ in layout)
    dma = pltpu.SemaphoreType.DMA
    return pl.pallas_call(
        functools.partial(return_kernel, ring, layout, count),
        out_shape=(
            jax.ShapeDtypeStruct((rows, 3 * width), BF),
            jax.ShapeDtypeStruct((4, 1, 128), F32),
            jax.ShapeDtypeStruct((count, r, w), F32),
        ),
        in_specs=[ANY] * len(grads) + [ANY] + [VM] * 6,
        out_specs=(VM,) * 3,
        scratch_shapes=[
            pltpu.VMEM((group, 256), BF), pltpu.VMEM((group, 256), BF), pltpu.VMEM((ext, 256), BF), pltpu.VMEM((ext, 256), BF),
            pltpu.VMEM((2, HALF, width), BF),
            pltpu.VMEM((2, ext, 128), BF), pltpu.VMEM((2, ext, 128), BF), pltpu.VMEM((2, 128, ext), BF),
            pltpu.VMEM((2, ext, 128), F32), pltpu.VMEM((2, ext, 128), F32),
            pltpu.VMEM((4, 8, QB), F32), pltpu.VMEM((4, 8, QB), F32),
            dma((4,)), dma, dma, dma((3,)), dma((3,)), dma((2, 2)), dma((2,)),
        ] + scatter_scratch(ring, count, r, w),
        compiler_params=pltpu.CompilerParams(collective_id=collective_id, has_side_effects=True, vmem_limit_bytes=63 * MIB),
        name="attend_back",
    )(*grads, d_tok, kx, vx, kf, qf, qa, of)


def first_kernel(ring, src, gain_src, wide, gains, *sems):
    greet(group_peers(ring))
    count = src.shape[0]
    work = Gather(ring, count, lambda i, go: go(src.at[i], lambda p, c, y, x: wide.at[i, p, c, y, x]), sems[:3])
    small = Gather(ring, 1, lambda i, go: go(gain_src, lambda p, c, y, x: gains.at[p, c, y, x]), sems[3:])
    lags = (2, (0, 1, 2, 3))
    def body(t, carry):
        small.step(t, *lags)
        work.step(t, *lags)
        return carry
    lax.fori_loop(0, work.steps(*lags), body, 0)
    work.drain_all()
    small.drain_all()


def first_gather(src, gain_src, ring, collective_id):
    count, r, w = src.shape
    return pl.pallas_call(
        functools.partial(first_kernel, ring),
        out_shape=(jax.ShapeDtypeStruct((count, 2, ring, 2, 2, r, w), BF),
                   jax.ShapeDtypeStruct((2, ring, 2, 2) + gain_src.shape, BF)),
        in_specs=[ANY, ANY],
        out_specs=(ANY, ANY),
        scratch_shapes=gather_sems(count) + gather_sems(1),
        compiler_params=pltpu.CompilerParams(collective_id=collective_id, has_side_effects=True),
        name="collect",
    )(src, gain_src)


def last_kernel(ring, count, grads, small, out, small_out, sums, came, far, small_send, small_recv, *rest):
    greet(group_peers(ring))
    buffers, sems = rest[:5], rest[5:]
    def write(i, total):
        out[i] = total
    work = Scatter(ring, count, scatter_pick((grads,), ((count, True),), out.shape[-1]), buffers, sems, out, write)
    p, c, h = place()
    peers = (work.core, work.xpeer, work.ypeer)

    def hop(n):
        return remote(sums.at[n], came.at[n], small_send.at[n], small_recv.at[n], peers[n])

    def far_hop(step):
        return remote(sums.at[3], far.at[step - 1], small_send.at[3], small_recv.at[3], (p, lax.rem(c + step, ring), h))

    sums[0] = small[...]
    hop(0).start()
    def body(t, carry):
        work.step(t)
        for n in range(3):
            @pl.when(t == 2 + 2 * n)
            def _():
                hop(n).wait_recv()
                sums[n + 1] = sums[n] + came[n]
                if n < 2:
                    hop(n + 1).start()
                else:
                    for step in range(1, ring):
                        far_hop(step).start()
        return carry
    lax.fori_loop(0, work.steps(), body, 0)
    local_copy(far, far, small_recv.at[3]).wait()
    total = sums[3]
    for step in range(1, ring):
        total = total + far[step - 1]
    small_out[...] = total
    for n in range(3):
        hop(n).wait_send()
    local_copy(far, far, small_send.at[3]).wait()
    work.drain_all()


def last_scatter(grads, small, ring, collective_id):
    count = grads.shape[0]
    r, w = grads.shape[-2:]
    n = small.shape[0]
    dma = pltpu.SemaphoreType.DMA
    return pl.pallas_call(
        functools.partial(last_kernel, ring, count),
        out_shape=(jax.ShapeDtypeStruct((count, r, w), F32), jax.ShapeDtypeStruct((n, 128), F32)),
        in_specs=[ANY, VM],
        out_specs=(VM, VM),
        scratch_shapes=[pltpu.VMEM((4, n, 128), F32), pltpu.VMEM((3, n, 128), F32), pltpu.VMEM((ring - 1, n, 128), F32),
                        dma((4,)), dma((4,))] + scatter_scratch(ring, count, r, w),
        compiler_params=pltpu.CompilerParams(collective_id=collective_id, has_side_effects=True, vmem_limit_bytes=40 * MIB),
        name="rsum",
    )(grads, small)


def edges(ids, ring):
    up = [(i, i + 1) for i in range(ring - 1)]
    down = [(i + 1, i) for i in range(ring - 1)]
    below = lax.ppermute(ids[:, -HALF:] + 1, "cp", up) - 1
    above = lax.ppermute(ids[:, :HALF] + 1, "cp", down) - 1
    return jnp.concatenate([below, ids, above], axis=1)


def local(
    inputs, cotangent, w_qkv, w_out, w_gate, w_up, w_down, gain_attn, gain_ffn, q_gain, k_gain, head_bias,
    segment_ids, variate_ids, time_index,
):
    ring = lax.axis_size("cp")
    head = lax.axis_index("hd")
    rows, width = inputs.shape
    depth = w_qkv.shape[0]
    r, w = item_shape(depth)

    def pieces(weight):
        return weight.reshape(depth, -1, 512).swapaxes(0, 1).reshape(-1, r, w)

    first = pieces(w_qkv)
    down_pieces = w_down.reshape(4, r, 2, w).swapaxes(1, 2).reshape(8, r, w)
    second = jnp.concatenate([pieces(w_out), pieces(w_gate), pieces(w_up), down_pieces])
    gain_src = jnp.pad(jnp.stack([gain_attn, gain_ffn]), ((0, 14), (0, 128 - depth)))
    qkv_wide, gains = first_gather(first, gain_src, ring, 0)
    qkv_wide = qkv_wide.reshape(-1, width, 512)
    gains = gains[..., :2, :depth].reshape(-1, 2, depth).swapaxes(0, 1).reshape(2, 1, width).astype(F32)

    times = lax.dynamic_slice_in_dim(time_index, head * rows, rows, 0)
    frequency = jnp.exp(-math.log(theta_base) * 2.0 * jnp.arange(HDIM // 2, dtype=jnp.float32) / HDIM)
    angle = times.astype(F32)[:, None] * frequency[None, :]
    cosine, sine = jnp.cos(angle), jnp.sin(angle)
    cosine = jnp.concatenate([cosine] * 4, axis=1)
    sine = jnp.concatenate([-sine, sine, -sine, sine], axis=1)
    head_gains = jnp.stack([jnp.concatenate([q_gain, q_gain]), jnp.concatenate([k_gain, k_gain])])

    ids = edges(jnp.stack([segment_ids, variate_ids]), ring)
    kf = key_features(ids[0], ids[1])
    qf = query_features(segment_ids, variate_ids)
    hs = head_scales(lax.dynamic_slice_in_dim(head_bias, head * 4, 4, 0))

    raw, rotated = project(inputs, gains[0], qkv_wide, cosine, sine, head_gains)
    heads_out, of, qa, kx, vx, wide, down = attend(second, rotated, kf, qf, hs, 18, ring, 1)
    layer_out, d_hidden, d_heads, g_gate, g_up, g_down, g_out, g_gffn = ffn(
        inputs, heads_out, cotangent, gains[1], wide.reshape(-1, width, 512), down.reshape(-1, width))

    def blocks(grad):
        return grad.reshape(-1, 2, ring, 2, 2, r, w)

    grads = (blocks(g_out), blocks(g_gate), blocks(g_up), g_down.reshape(2, ring, 2, 2, 4, r, 2 * w))
    layout = ((2, True), (8, True), (8, True), (8, False))
    d_proj, g_bias, items = attend_back(grads, layout, d_heads, kx, vx, kf, qf, qa, of, ring, 2)
    g_qkv, grad_inputs, g_gattn, g_heads = unproject(
        inputs, gains[0], qkv_wide, cosine, sine, head_gains, raw, d_proj, d_hidden)
    bias_all = lax.dynamic_update_slice_in_dim(jnp.zeros((HEADS, 2), F32), g_bias[:, 0, :2], head * 4, 0)
    small = jnp.concatenate([
        g_gattn.reshape(8, 128), g_gffn.reshape(8, 128), g_heads,
        jnp.pad(bias_all.reshape(1, 32), ((0, 5), (0, 96)))])
    last, small = last_scatter(blocks(g_qkv), small, ring, 3)

    def columns(part):
        return part.reshape(-1, depth, 512).swapaxes(0, 1).reshape(depth, -1)

    me = (lax.axis_index("pack") * ring + lax.axis_index("cp")) * 4 + head
    own_gains = lax.dynamic_slice_in_dim(small[:16].reshape(2, width), me * depth, depth, 1)
    own_heads = small[16:18, :HDIM] + small[16:18, HDIM:]
    return (
        layer_out, grad_inputs, columns(last), columns(items[:2]), columns(items[2:10]), columns(items[10:18]),
        items[18:].reshape(4, 2, r, w).swapaxes(1, 2).reshape(w_down.shape),
        own_gains[0], own_gains[1], own_heads[0], own_heads[1], small[18, :32].reshape(HEADS, 2),
    )


def solution(mesh):
    return jax.shard_map(
        local,
        mesh=mesh,
        in_specs=(
            P(("pack", "cp", "hd"), None),
            P(("pack", "cp", "hd"), None),
            P(("pack", "cp", "hd"), None),
            P(("pack", "cp", "hd"), None),
            P(("pack", "cp", "hd"), None),
            P(("pack", "cp", "hd"), None),
            P(("pack", "cp", "hd"), None),
            P(("pack", "cp", "hd")),
            P(("pack", "cp", "hd")),
            P(),
            P(),
            P(),
            P(("pack", "cp")),
            P(("pack", "cp")),
            P(("pack", "cp")),
        ),
        out_specs=(
            P(("pack", "cp", "hd"), None),
            P(("pack", "cp", "hd"), None),
            P(("pack", "cp", "hd"), None),
            P(("pack", "cp", "hd"), None),
            P(("pack", "cp", "hd"), None),
            P(("pack", "cp", "hd"), None),
            P(("pack", "cp", "hd"), None),
            P(("pack", "cp", "hd")),
            P(("pack", "cp", "hd")),
            P(),
            P(),
            P(),
        ),
        check_vma=False,
    )
```

```python
import functools
import math

import jax
import jax.numpy as jnp
from jax import lax
from jax.experimental import pallas as pl
from jax.experimental.pallas import tpu as pltpu
from jax.sharding import PartitionSpec as P

HEADS = 16
HDIM = 64
HALF = 512
QB = 256
SPAN = QB + 2 * HALF
FAR = -1e30
EPS = 1e-6
theta_base = 10000.0
MIB = 2**20
F32, BF = jnp.float32, jnp.bfloat16
MESH = pl.DeviceIdType.MESH
VM = pl.BlockSpec(memory_space=pltpu.VMEM)
ANY = pl.BlockSpec(memory_space=pl.ANY)
ALL = slice(None)


def item_shape(rows):
    full = max(rows, 16)
    return full, rows * 512 // full


def place():
    return lax.axis_index("pack"), lax.axis_index("cp"), lax.axis_index("hd")


def greet(peers):
    barrier = pltpu.get_barrier_semaphore()
    for peer in peers:
        pl.semaphore_signal(barrier, inc=1, device_id=peer, device_id_type=MESH)
    pl.semaphore_wait(barrier, len(peers))


def group_peers(ring):
    p, c, h = place()
    peers = [(1 - p, c, h), (p, c, h + 1 - 2 * lax.rem(h, 2)), (p, c, lax.rem(h + 2, 4))]
    peers += [(p, lax.rem(c + step, ring), h) for step in range(1, ring)]
    return peers


class Scatter:
    def __init__(self, ring, count, pick, buffers, sems, out, write):
        self.ring, self.count, self.pick = ring, count, pick
        self.load, self.own, self.b1, self.b2, self.b3 = buffers
        self.slots = self.load.shape[0]
        self.load_sem, self.send_sem, self.recv_sem = sems
        self.out, self.write = out, write
        self.p, self.c, self.h = place()
        self.hy, self.hx = self.h // 2, lax.rem(self.h, 2)
        self.core = (1 - self.p, self.c, self.h)
        self.xpeer = (self.p, self.c, self.hy * 2 + 1 - self.hx)
        self.ypeer = (self.p, self.c, (1 - self.hy) * 2 + self.hx)

    def remote(self, i, stage, src, dst, device):
        return pltpu.make_async_remote_copy(
            src_ref=src, dst_ref=dst, send_sem=self.send_sem.at[stage, i],
            recv_sem=self.recv_sem.at[stage, i], device_id=device, device_id_type=MESH)

    def copy0(self, i, src):
        return self.remote(i, 0, src, self.own.at[i], self.core)

    def copy1(self, i, first_y):
        if first_y:
            return self.remote(i, 1, self.own.at[i, :, 1 - self.hy], self.b1.at[i], self.ypeer)
        return self.remote(i, 1, self.own.at[i, :, :, 1 - self.hx], self.b1.at[i], self.xpeer)

    def copy2(self, i, first_y):
        if first_y:
            return self.remote(i, 2, self.own.at[i, :, self.hy, 1 - self.hx], self.b2.at[i], self.xpeer)
        return self.remote(i, 2, self.own.at[i, :, 1 - self.hy, self.hx], self.b2.at[i], self.ypeer)

    def copy3(self, i, step):
        peer = lax.rem(self.c + step, self.ring)
        return self.remote(i, 3, self.own.at[i, peer, self.hy, self.hx], self.b3.at[i, step - 1], (self.p, peer, self.h))

    def begin(self, i):
        def go(mine, other):
            slot = lax.rem(i, self.slots)
            pltpu.make_async_copy(mine, self.load.at[slot], self.load_sem.at[slot]).start()
            self.copy0(i, other).start()
        self.pick(i, self.p, go)

    def mine(self, i, k):
        return self.load[lax.rem(i, self.slots), k]

    def landed(self, i):
        slot = lax.rem(i, self.slots)
        pltpu.make_async_copy(self.load.at[slot], self.load.at[slot], self.load_sem.at[slot]).wait()

    def stage1(self, i, first_y):
        self.landed(i)
        self.copy0(i, self.own.at[i]).wait_recv()
        def add(k, carry):
            self.own[i, k] = self.own[i, k] + self.mine(i, k)
            return carry
        lax.fori_loop(0, self.ring, add, 0)
        self.copy1(i, first_y).start()

    def stage2(self, i, first_y):
        self.copy1(i, first_y).wait_recv()
        def add(k, carry):
            for m in range(2):
                at = (i, k, self.hy, m) if first_y else (i, k, m, self.hx)
                self.own[at] = self.own[at] + self.b1[i, k, m]
            return carry
        lax.fori_loop(0, self.ring, add, 0)
        self.copy2(i, first_y).start()

    def stage3(self, i, first_y):
        self.copy2(i, first_y).wait_recv()
        def add(k, carry):
            at = (i, k, self.hy, self.hx)
            self.own[at] = self.own[at] + self.b2[i, k]
            return carry
        lax.fori_loop(0, self.ring, add, 0)
        for step in range(1, self.ring):
            self.copy3(i, step).start()

    def finish(self, i):
        pltpu.make_async_copy(self.b3.at[i], self.b3.at[i], self.recv_sem.at[3, i]).wait()
        total = self.own[i, self.c, self.hy, self.hx].astype(jnp.float32)
        for step in range(1, self.ring):
            total = total + self.b3[i, step - 1].astype(jnp.float32)
        self.write(i, total)

    def drain(self, i, first_y):
        self.copy0(i, self.own.at[i]).wait_send()
        self.copy1(i, first_y).wait_send()
        self.copy2(i, first_y).wait_send()
        pltpu.make_async_copy(self.b3.at[i], self.b3.at[i], self.send_sem.at[3, i]).wait()

    def step(self, t, ahead=3, lags=(0, 2, 4, 6)):
        pairs = (self.count + 1) // 2
        def both(pair, act):
            for first_y in (True, False):
                i = 2 * pair + (0 if first_y else 1)
                guard = (pair >= 0) & (i < self.count) & (i >= 0)
                pl.when(guard)(functools.partial(act, i, first_y))
        both(t, lambda i, f: self.begin(i))
        both(t - ahead - lags[0], self.stage1)
        both(t - ahead - lags[1], self.stage2)
        both(t - ahead - lags[2], self.stage3)
        both(t - ahead - lags[3], lambda i, f: self.finish(i))

    def steps(self, ahead=3, lags=(0, 2, 4, 6)):
        return (self.count + 1) // 2 + ahead + lags[3]

    def drain_all(self):
        def one(t, carry):
            for first_y in (True, False):
                i = 2 * t + (0 if first_y else 1)
                pl.when(i < self.count)(functools.partial(self.drain, i, first_y))
            return carry
        lax.fori_loop(0, (self.count + 1) // 2, one, 0)


class StagedScatter(Scatter):
    def begin(self, i):
        self.copy0(i, self.load.at[lax.rem(i, self.slots), 1 - self.p]).start()

    def mine(self, i, k):
        return self.load[lax.rem(i, self.slots), self.p, k]

    def landed(self, i):
        pass

    def reuse(self, i):
        self.copy0(i, self.own.at[i]).wait_send()

    def drain(self, i, first_y):
        pl.when(i >= self.count - self.slots)(lambda: self.reuse(i))
        self.copy1(i, first_y).wait_send()
        self.copy2(i, first_y).wait_send()
        pltpu.make_async_copy(self.b3.at[i], self.b3.at[i], self.send_sem.at[3, i]).wait()


def scatter_scratch(ring, count, rows, cols, staged=0):
    bf = jnp.bfloat16
    load = (staged, 2) if staged else (8,)
    return [
        pltpu.VMEM(load + (ring, 2, 2, rows, cols), bf),
        pltpu.VMEM((count, ring, 2, 2, rows, cols), bf),
        pltpu.VMEM((count, ring, 2, rows, cols), bf),
        pltpu.VMEM((count, ring, rows, cols), bf),
        pltpu.VMEM((count, ring - 1, rows, cols), bf),
        pltpu.SemaphoreType.DMA((8,)),
        pltpu.SemaphoreType.DMA((4, count)),
        pltpu.SemaphoreType.DMA((4, count)),
    ]


def scatter_pick(grads, layout, cols):
    def pick(i, p, go):
        start = 0
        for ref, (size, outer) in zip(grads, layout):
            j = i - start
            def run(ref=ref, j=j, outer=outer):
                if outer:
                    go(ref.at[j, p], ref.at[j, 1 - p])
                else:
                    at = pl.ds(pl.multiple_of(lax.rem(j, 2) * cols, cols), cols)
                    go(ref.at[p, :, :, :, j // 2, :, at], ref.at[1 - p, :, :, :, j // 2, :, at])
            pl.when((j >= 0) & (j < size))(run)
            start += size
    return pick


def scatter_kernel(ring, layout, count, *refs):
    n = len(layout)
    grads, out = refs[:n], refs[n]
    load, own, b1, b2, b3, load_sem, send_sem, recv_sem = refs[n + 1:]
    greet(group_peers(ring))
    pick = scatter_pick(grads, layout, out.shape[-1])

    def write(i, total):
        out[i] = total

    work = Scatter(ring, count, pick, (load, own, b1, b2, b3), (load_sem, send_sem, recv_sem), out, write)
    def body(t, carry):
        work.step(t)
        return carry
    lax.fori_loop(0, work.steps(), body, 0)
    work.drain_all()


def scatter(grads, layout, ring, collective_id):
    rows, cols = grads[0].shape[-2:]
    count = sum(size for size, _ in layout)
    return pl.pallas_call(
        functools.partial(scatter_kernel, ring, layout, count),
        out_shape=jax.ShapeDtypeStruct((count, rows, cols), jnp.float32),
        in_specs=[pl.BlockSpec(memory_space=pl.ANY)] * len(grads),
        out_specs=pl.BlockSpec(memory_space=pltpu.VMEM),
        scratch_shapes=scatter_scratch(ring, count, rows, cols),
        compiler_params=pltpu.CompilerParams(collective_id=collective_id, has_side_effects=True, vmem_limit_bytes=60 * 2**20),
        name="rsum",
    )(*grads)


class Gather:
    def __init__(self, ring, count, pick, sems):
        self.ring, self.count, self.pick = ring, count, pick
        self.local_sem, self.send_sem, self.recv_sem = sems
        self.p, self.c, self.h = place()
        self.hy, self.hx = self.h // 2, lax.rem(self.h, 2)
        self.core = (1 - self.p, self.c, self.h)
        self.xpeer = (self.p, self.c, self.hy * 2 + 1 - self.hx)
        self.ypeer = (self.p, self.c, (1 - self.hy) * 2 + self.hx)

    def remote(self, i, stage, src, dst, device):
        return pltpu.make_async_remote_copy(
            src_ref=src, dst_ref=dst, send_sem=self.send_sem.at[stage, i],
            recv_sem=self.recv_sem.at[stage, i], device_id=device, device_id_type=MESH)

    def same(self, i, stage, ref, device):
        return self.remote(i, stage, ref, ref, device)

    def begin(self, i, first_x):
        def go(src, out):
            mine = out(self.p, self.c, self.hy, self.hx)
            pltpu.make_async_copy(src, mine, self.local_sem.at[i]).start()
            for step in range(1, self.ring):
                peer = (self.p, lax.rem(self.c + step, self.ring), self.h)
                self.remote(i, 0, src, mine, peer).start()
        self.pick(i, go)

    def stage1(self, i, first_x):
        def go(src, out):
            mine = out(self.p, self.c, self.hy, self.hx)
            pltpu.make_async_copy(src, mine, self.local_sem.at[i]).wait()
            rest = out(self.p, pl.ds(0, self.ring - 1), self.hy, self.hx)
            pltpu.make_async_copy(rest, rest, self.recv_sem.at[0, i]).wait()
            column = out(self.p, ALL, self.hy, self.hx)
            self.same(i, 1, column, self.xpeer if first_x else self.ypeer).start()
            self.same(i, 3, column, self.core).start()
        self.pick(i, go)

    def first(self, out, mine, first_x):
        if first_x:
            return out(self.p, ALL, self.hy, self.hx if mine else 1 - self.hx)
        return out(self.p, ALL, self.hy if mine else 1 - self.hy, self.hx)

    def second(self, out, mine, first_x):
        if first_x:
            return out(self.p, ALL, self.hy if mine else 1 - self.hy, ALL)
        return out(self.p, ALL, ALL, self.hx if mine else 1 - self.hx)

    def stage2(self, i, first_x):
        def go(src, out):
            came = self.first(out, False, first_x)
            self.same(i, 1, came, self.core).wait_recv()
            self.same(i, 2, self.second(out, True, first_x), self.ypeer if first_x else self.xpeer).start()
            self.same(i, 3, came, self.core).start()
        self.pick(i, go)

    def stage3(self, i, first_x):
        def go(src, out):
            came = self.second(out, False, first_x)
            self.same(i, 2, came, self.core).wait_recv()
            self.same(i, 3, came, self.core).start()
        self.pick(i, go)

    def finish(self, i, first_x):
        def go(src, out):
            half = out(1 - self.p, ALL, ALL, ALL)
            pltpu.make_async_copy(half, half, self.recv_sem.at[3, i]).wait()
        self.pick(i, go)

    def drain(self, i, first_x):
        def go(src, out):
            rest = out(self.p, pl.ds(0, self.ring - 1), self.hy, self.hx)
            pltpu.make_async_copy(rest, rest, self.send_sem.at[0, i]).wait()
            self.same(i, 1, self.first(out, True, first_x), self.core).wait_send()
            self.same(i, 2, self.second(out, True, first_x), self.core).wait_send()
            half = out(self.p, ALL, ALL, ALL)
            pltpu.make_async_copy(half, half, self.send_sem.at[3, i]).wait()
        self.pick(i, go)

    def step(self, t, ahead=3, lags=(0, 2, 4, 6)):
        pairs = (self.count + 1) // 2
        def both(pair, act):
            for first_x in (True, False):
                i = 2 * pair + (0 if first_x else 1)
                guard = (pair >= 0) & (i < self.count) & (i >= 0)
                pl.when(guard)(functools.partial(act, i, first_x))
        both(t, self.begin)
        both(t - ahead - lags[0], self.stage1)
        both(t - ahead - lags[1], self.stage2)
        both(t - ahead - lags[2], self.stage3)
        both(t - ahead - lags[3], self.finish)

    def steps(self, ahead=3, lags=(0, 2, 4, 6)):
        return (self.count + 1) // 2 + ahead + lags[3]

    def drain_all(self):
        def one(t, carry):
            for first_x in (True, False):
                i = 2 * t + (0 if first_x else 1)
                pl.when(i < self.count)(functools.partial(self.drain, i, first_x))
            return carry
        lax.fori_loop(0, (self.count + 1) // 2, one, 0)


def gather_sems(count):
    return [
        pltpu.SemaphoreType.DMA((count,)),
        pltpu.SemaphoreType.DMA((4, count)),
        pltpu.SemaphoreType.DMA((4, count)),
    ]


def gather_pick(src, wide, down, n_wide):
    cols = src.shape[-1]
    def pick(i, go):
        @pl.when(i < n_wide)
        def _():
            go(src.at[i], lambda p, c, y, x: wide.at[i, p, c, y, x])
        @pl.when(i >= n_wide)
        def _():
            j = i - n_wide
            at = pl.ds(pl.multiple_of(lax.rem(j, 2) * cols, cols), cols)
            go(src.at[i], lambda p, c, y, x: down.at[p, c, y, x, j // 2, :, at])
    return pick


def gather_kernel(ring, n_wide, count, src, wide, down, *sems):
    greet(group_peers(ring))
    work = Gather(ring, count, gather_pick(src, wide, down, n_wide), sems)
    def body(t, carry):
        work.step(t)
        return carry
    lax.fori_loop(0, work.steps(), body, 0)
    work.drain_all()


def gather(src, n_wide, ring, collective_id):
    count, rows, cols = src.shape
    return pl.pallas_call(
        functools.partial(gather_kernel, ring, n_wide, count),
        out_shape=(
            jax.ShapeDtypeStruct((n_wide, 2, ring, 2, 2, rows, cols), src.dtype),
            jax.ShapeDtypeStruct((2, ring, 2, 2, (count - n_wide) // 2, rows, 2 * cols), src.dtype),
        ),
        in_specs=[ANY],
        out_specs=(ANY, ANY),
        scratch_shapes=gather_sems(count),
        compiler_params=pltpu.CompilerParams(collective_id=collective_id, has_side_effects=True),
        name="collect",
    )(src)


def dot_tb(a, b):
    return lax.dot_general(a, b, (((1,), (1,)), ((), ())), preferred_element_type=jnp.float32)


def dot(a, b):
    return jnp.dot(a, b, preferred_element_type=jnp.float32)


def lanes(rows):
    return lax.broadcasted_iota(jnp.int32, (rows, 128), 1)


def split3(x):
    hi = x.astype(jnp.bfloat16).astype(jnp.float32)
    mid = (x - hi).astype(jnp.bfloat16).astype(jnp.float32)
    lo = x - hi - mid
    return hi, mid, lo


def at_lanes(base, first, values):
    lane = lanes(base.shape[0])
    for n, value in enumerate(values):
        base = jnp.where(lane == first + n, value, base)
    return base


def halves(x):
    return x, pltpu.roll(x, 64, 1)


def build_keys(pair, k_ref, v_ref, kf_ref, ka, va, kt=None, first=0, last=None):
    at = pl.ds(pl.multiple_of(pair * 128, 128), 128)
    rows = k_ref.shape[0]
    chunk = 512
    def one(n, carry):
        r = pl.ds(pl.multiple_of(n * chunk, chunk), chunk)
        lane = lanes(chunk)
        keys = halves(k_ref[r, at].astype(jnp.float32))
        values = halves(v_ref[r, at].astype(jnp.float32))
        feat = kf_ref[r, :].astype(jnp.float32)
        for m in range(2):
            full = jnp.where(lane < 64, keys[m], feat)
            ka[m, r, :] = full.astype(jnp.bfloat16)
            if kt is not None:
                kt[m, :, r] = full.T.astype(jnp.bfloat16)
            ones = jnp.where(lane < 67, 1.0, 0.0)
            va[m, r, :] = jnp.where(lane < 64, values[m], ones).astype(jnp.bfloat16)
        return carry
    lax.fori_loop(first, rows // chunk if last is None else last, one, 0)


def forward_block(pair, n, q_ref, qf_ref, hs_ref, ka, va, o_ref, of_ref, qa_ref):
    at = pl.ds(pl.multiple_of(pair * 128, 128), 128)
    r = pl.ds(pl.multiple_of(n * QB, QB), QB)
    lane = lanes(QB)
    queries = halves(q_ref[r, at].astype(jnp.float32) * (1.0 / math.sqrt(HDIM)))
    feat = qf_ref[r, :].astype(jnp.float32)
    row = lax.broadcasted_iota(jnp.int32, (QB, QB), 0)
    col = lax.broadcasted_iota(jnp.int32, (QB, QB), 1)
    outs = []
    for m in range(2):
        qa = jnp.where(lane < 64, queries[m], feat * hs_ref[pl.ds(pair * 2 + m, 1), :])
        qb = qa.astype(jnp.bfloat16)
        def part(first, size, mask=None):
            keys = pl.ds(pl.multiple_of(n * QB + first, QB), size)
            s = dot_tb(qb, ka[m, keys, :])
            if mask is not None:
                s = jnp.where(mask, s, FAR)
            return dot(jnp.exp(s).astype(jnp.bfloat16), va[m, keys, :])
        o = part(0, QB, col >= row) + part(QB, SPAN - 2 * QB) + part(SPAN - QB, QB, col <= row)
        total = o[:, 64:65]
        outs.append(o * (1.0 / total))
        hi, mid, lo = split3(-jnp.log(total))
        qa_ref[pair * 2 + m, r, :] = at_lanes(qa, 80, (hi, mid, lo)).astype(jnp.bfloat16)
    both = jnp.where(lane < 64, outs[0], pltpu.roll(outs[1], 64, 1))
    of_ref[r, at] = both
    o_ref[r, at] = both.astype(jnp.bfloat16)


def backward_block(pair, n, qf_ref, qa_ref, do_ref, of_ref, ka, va, kt, dka, dva, dq_ref, same, every):
    at = pl.ds(pl.multiple_of(pair * 128, 128), 128)
    r = pl.ds(pl.multiple_of(n * QB, QB), QB)
    lane = lanes(QB)
    grads = do_ref[r, at].astype(jnp.float32)
    terms = grads * of_ref[r, at]
    pieces = halves(grads)
    row = lax.broadcasted_iota(jnp.int32, (QB, QB), 0)
    col = lax.broadcasted_iota(jnp.int32, (QB, QB), 1)
    dqs = []
    qft = qf_ref[r, :].astype(jnp.float32).T[64:72, :]
    for m in range(2):
        own = (lane < 64) if m == 0 else (lane >= 64)
        delta = jnp.sum(jnp.where(own, terms, 0.0), axis=1, keepdims=True)
        da = at_lanes(jnp.where(lane < 64, pieces[m], 0.0), 64, split3(-delta)).astype(jnp.bfloat16)
        qb = qa_ref[pair * 2 + m, r, :]
        dq = jnp.zeros((128, QB), jnp.float32)
        for first, size, edge in ((0, QB, 0), (QB, SPAN - 2 * QB, None), (SPAN - QB, QB, 1)):
            keys = pl.ds(pl.multiple_of(n * QB + first, QB), size)
            s = dot_tb(ka[m, keys, :], qb)
            if edge is not None:
                s = jnp.where((row >= col) if edge == 0 else (row <= col), s, FAR)
            p = jnp.exp(s)
            dp = dot_tb(va[m, keys, :], da)
            ds = (p * dp).astype(jnp.bfloat16)
            dva[m, keys, :] += dot(p.astype(jnp.bfloat16), da)
            dka[m, keys, :] += dot(ds, qb)
            dq = dq + dot(kt[m, :, keys], ds)
        dqs.append(dq[:64, :])
        sums = dq[64:72, :]
        pick = lax.broadcasted_iota(jnp.int32, (8, QB), 0) < 4
        h = pair * 2 + m
        same[h] += jnp.where(pick, sums * qft, 0.0)
        every[h] += jnp.where(pick, sums, 0.0)
    dq_ref[r, at] = (jnp.concatenate(dqs, axis=0).T * (1.0 / math.sqrt(HDIM))).astype(dq_ref.dtype)


def backward_finish(pair, dka, dva, dk_ref, dv_ref):
    at = pl.ds(pl.multiple_of(pair * 128, 128), 128)
    chunk = 512
    def one(n, carry):
        r = pl.ds(pl.multiple_of(n * chunk, chunk), chunk)
        lane = lanes(chunk)
        dk_ref[r, at] = jnp.where(lane < 64, dka[0, r, :], pltpu.roll(dka[1, r, :], 64, 1)).astype(dk_ref.dtype)
        dv_ref[r, at] = jnp.where(lane < 64, dva[0, r, :], pltpu.roll(dva[1, r, :], 64, 1)).astype(dv_ref.dtype)
        return carry
    lax.fori_loop(0, dk_ref.shape[0] // chunk, one, 0)


def features(seg, var):
    lane = jnp.arange(128)[None, :]
    same = (var[:, None] == (lane - 64) % 4) & (lane >= 64) & (lane < 76)
    doc = (lane >= 76) & (lane < 80)
    here = seg[:, None] == lane - 76
    keys = jnp.where(doc & ~here, FAR, jnp.where(same | ((lane >= 80) & (lane < 83)), 1.0, 0.0))
    queries = jnp.where(same | (doc & here), 1.0, 0.0)
    return queries.astype(jnp.bfloat16), keys.astype(jnp.bfloat16)


def head_scales(bias):
    hi, mid, lo = split3(bias[:, :1] - bias[:, 1:])
    lane = jnp.arange(128)[None, :]
    parts = jnp.where(lane < 68, hi, jnp.where(lane < 72, mid, lo))
    return jnp.where(lane < 64, 0.0, jnp.where(lane < 76, parts, jnp.where(lane < 80, 1.0, 0.0)))


def scale_of(x):
    return lax.rsqrt(jnp.mean(x * x, axis=-1, keepdims=True) + EPS)


def head_mean(x):
    row = lax.broadcasted_iota(jnp.int32, (128, 128), 0)
    col = lax.broadcasted_iota(jnp.int32, (128, 128), 1)
    group = jnp.where((row < 64) == (col < 64), 1.0 / HDIM, 0.0).astype(BF)
    hi = x.astype(BF)
    rest = x - hi.astype(F32)
    mid = rest.astype(BF)
    low = (rest - mid.astype(F32)).astype(BF)
    return dot(hi, group) + dot(mid, group) + dot(low, group)


def swap_halves(x):
    lane = lax.rem(lanes(x.shape[0]), 64)
    return jnp.where(lane < 32, pltpu.roll(x, 96, 1), pltpu.roll(x, 32, 1))


def norm_back_rows(u, r, gain, dy):
    scaled = dy * gain
    du = r * scaled - u * (r * r * r) * jnp.mean(scaled * u, axis=-1, keepdims=True)
    return du, jnp.sum(dy * u * r, axis=0, keepdims=True)


def as_blocks(value, shape):
    rows, cols = shape[-2:]
    if cols == value.shape[1]:
        return value.astype(BF).reshape(shape)
    depth = rows * cols // value.shape[1]
    parts = value.reshape(-1, depth, value.shape[1])
    parts = [parts[:, :, n:n + cols] for n in range(0, value.shape[1], cols)]
    return jnp.concatenate(parts, axis=1).astype(BF).reshape(shape)


FFN_LAGS = (1, (0, 1, 2, 4))
SLOTS = 6


def ffn_kernel(ring, x_ref, heads_ref, cot_ref, gain_ref, wo_ref, wg_ref, wu_ref, wd_ref,
               out_ref, dhid_ref, dheads_ref, gd_ref, go_ref, ggain_ref, sums_ref,
               hidden, acc, nrm, nrm_t, load, own, b1, b2, b3, load_sem, send_sem, recv_sem):
    t = pl.program_id(0)
    steps = pl.num_programs(0)
    cot = cot_ref[...]

    def write(i, total):
        sums_ref[i] = total

    work = StagedScatter(ring, own.shape[0], None, (load, own, b1, b2, b3), (load_sem, send_sem, recv_sem), sums_ref, write)

    @pl.when(t == 0)
    def _():
        greet(group_peers(ring))
        heads = heads_ref[...]
        for n in range(2):
            at = slice(n * 512, (n + 1) * 512)
            hidden[:, at] = x_ref[:, at].astype(F32) + dot(heads, wo_ref[n])
        h = hidden[...]
        y = h * scale_of(h) * gain_ref[...]
        nrm[...] = y.astype(BF)
        nrm_t[...] = y.T.astype(BF)
        acc[...] = h
        dhid_ref[...] = jnp.zeros_like(dhid_ref)

    normed = nrm[...]
    wg, wu, wd = wg_ref[0], wu_ref[0], wd_ref[...]
    gate = dot(normed, wg)
    up = dot(normed, wu)
    d_product = dot_tb(cot, wd)
    sig = jax.nn.sigmoid(gate)
    silu = gate * sig
    product = silu * up
    prod_b = product.astype(BF)
    d_gate = (d_product * up * sig * (1.0 + gate * (1.0 - sig))).astype(BF)
    d_up = (d_product * silu).astype(BF)
    slot = lax.rem(2 * t, SLOTS)
    @pl.when(t >= SLOTS // 2)
    def _():
        work.reuse(2 * t - SLOTS)
        work.reuse(2 * t + 1 - SLOTS)
    load[slot] = as_blocks(dot(nrm_t[...], d_gate), load.shape[1:])
    load[slot + 1] = as_blocks(dot(nrm_t[...], d_up), load.shape[1:])
    work.step(t, *FFN_LAGS)
    acc[...] += dot(prod_b, wd)
    gd_ref[...] = dot(prod_b.astype(F32).T.astype(BF), cot).astype(BF)
    dhid_ref[...] += dot_tb(d_gate, wg) + dot_tb(d_up, wu)

    @pl.when(t == steps - 1)
    def _():
        work.step(t + 1, *FFN_LAGS)
        out_ref[...] = acc[...].astype(BF)
        h = hidden[...]
        du, terms = norm_back_rows(h, scale_of(h), gain_ref[...], dhid_ref[...])
        ggain_ref[...] = terms
        d_hidden = cot_ref[...].astype(F32) + du
        dhid_ref[...] = d_hidden
        work.step(t + 2, *FFN_LAGS)
        d_attn = d_hidden.astype(BF)
        heads_t = heads_ref[...].astype(F32).T.astype(BF)
        total = jnp.zeros(d_hidden.shape, F32)
        for n in range(2):
            at = slice(n * 512, (n + 1) * 512)
            go_ref[n] = dot(heads_t, d_attn[:, at]).astype(BF)
            total = total + dot_tb(d_attn[:, at], wo_ref[n])
        dheads_ref[...] = total.astype(BF)
        def rest(n, carry):
            work.step(n, *FFN_LAGS)
            return carry
        lax.fori_loop(t + 3, work.steps(*FFN_LAGS), rest, 0)
        work.drain_all()


def ffn(x, heads, cot, gain, wide, down, ring, item, collective_id):
    rows, width = x.shape
    ff = down.shape[0]
    steps = ff // 512
    once = pl.Buffered(1)
    def fixed(*shape):
        return pl.BlockSpec(shape, lambda t: (0,) * len(shape), pipeline_mode=once)
    def out(*shape):
        return pl.BlockSpec(shape, lambda t: (0,) * len(shape))
    def items(first):
        return pl.BlockSpec((1, width, 512), lambda t: (first + t, 0, 0))
    return pl.pallas_call(
        functools.partial(ffn_kernel, ring),
        grid=(steps,),
        out_shape=(
            jax.ShapeDtypeStruct((rows, width), BF), jax.ShapeDtypeStruct((rows, width), F32),
            jax.ShapeDtypeStruct((rows, width), BF),
            jax.ShapeDtypeStruct((ff, width), BF), jax.ShapeDtypeStruct((2, width, 512), BF),
            jax.ShapeDtypeStruct((1, width), F32), jax.ShapeDtypeStruct((2 * steps,) + item, F32)),
        in_specs=[fixed(rows, width), fixed(rows, width), fixed(rows, width), fixed(1, width),
                  pl.BlockSpec((2, width, 512), lambda t: (3, 0, 0), pipeline_mode=once), items(8), items(16),
                  pl.BlockSpec((512, width), lambda t: (t, 0))],
        out_specs=(VM, VM, VM,
                   pl.BlockSpec((512, width), lambda t: (t, 0)), VM, VM, VM),
        scratch_shapes=[pltpu.VMEM((rows, width), F32), pltpu.VMEM((rows, width), F32),
                        pltpu.VMEM((rows, width), BF), pltpu.VMEM((width, rows), BF)]
        + scatter_scratch(ring, 2 * steps, item[0], item[1], SLOTS),
        compiler_params=pltpu.CompilerParams(collective_id=collective_id, has_side_effects=True, vmem_limit_bytes=62 * MIB),
        name="feedforward",
    )(x, heads, cot, gain, wide, wide, wide, down)


def unproject_kernel(x_ref, gain_ref, w_ref, cos_ref, sin_ref, hg_ref, raw_ref, d_ref, dhid_ref,
                     gw_ref, gin_ref, ggain_ref, ghead_ref, nrm_t, dnorm):
    t = pl.program_id(0)

    @pl.when(t == 0)
    def _():
        x = x_ref[...].astype(F32)
        nrm_t[...] = (x * scale_of(x) * gain_ref[...]).T.astype(BF)
        dnorm[...] = jnp.zeros_like(dnorm)
        ghead_ref[...] = jnp.zeros_like(ghead_ref)

    def use(d_proj):
        gw_ref[0] = dot(nrm_t[...], d_proj).astype(BF)
        dnorm[...] += dot_tb(d_proj, w_ref[0])

    @pl.when(t >= 4)
    def _():
        use(d_ref[...])

    @pl.when(t < 4)
    def _():
        kind = t // 2
        gain = hg_ref[pl.ds(kind, 1), :]
        pieces = []
        for n in range(d_ref.shape[1] // 128):
            at = slice(n * 128, (n + 1) * 128)
            u = raw_ref[:, at].astype(F32)
            dy = d_ref[:, at].astype(F32)
            dy = dy * cos_ref[...] - swap_halves(dy) * sin_ref[...]
            r = lax.rsqrt(head_mean(u * u) + EPS)
            scaled = dy * gain
            pieces.append((r * scaled - u * (r * r * r) * head_mean(scaled * u)).astype(BF))
            ghead_ref[pl.ds(kind, 1), :] += jnp.sum(dy * u * r, axis=0, keepdims=True)
        use(jnp.concatenate(pieces, axis=1))

    @pl.when(t == 5)
    def _():
        x = x_ref[...].astype(F32)
        du, terms = norm_back_rows(x, scale_of(x), gain_ref[...], dnorm[...])
        gin_ref[...] = dhid_ref[...] + du
        ggain_ref[...] = terms


def unproject(x, gain, wide, cosine, sine, head_gains, raw, grads, d_hidden):
    rows, width = x.shape
    def fixed(*shape):
        return pl.BlockSpec(shape, lambda t: (0,) * len(shape))
    tile = pl.BlockSpec((rows, 512), lambda t: (0, t))
    item = pl.BlockSpec((1, width, 512), lambda t: (t, 0, 0))
    return pl.pallas_call(
        unproject_kernel,
        grid=(6,),
        out_shape=(jax.ShapeDtypeStruct((6, width, 512), BF), jax.ShapeDtypeStruct((rows, width), F32),
                   jax.ShapeDtypeStruct((1, width), F32), jax.ShapeDtypeStruct((2, 128), F32)),
        in_specs=[fixed(rows, width), fixed(1, width), item, fixed(rows, 128), fixed(rows, 128), fixed(2, 128),
                  tile, tile, fixed(rows, width)],
        out_specs=(item, fixed(rows, width), fixed(1, width), fixed(2, 128)),
        scratch_shapes=[pltpu.VMEM((width, rows), BF), pltpu.VMEM((rows, width), F32)],
        compiler_params=pltpu.CompilerParams(vmem_limit_bytes=48 * MIB),
        name="unproject",
    )(x, gain, wide, cosine, sine, head_gains, raw, grads, d_hidden)


def remote(src, dst, send, recv, device):
    return pltpu.make_async_remote_copy(
        src_ref=src, dst_ref=dst, send_sem=send, recv_sem=recv, device_id=device, device_id_type=MESH)


def local_copy(src, dst, sem):
    return pltpu.make_async_copy(src, dst, sem)


def wide_at(first):
    return pl.ds(pl.multiple_of(first, 256), 256)


class Rim:
    def __init__(self, ring):
        self.p, self.c, self.h = place()
        self.ring = ring
        self.has_low, self.has_high = self.c > 0, self.c < ring - 1
        self.low = lax.rem(self.c + ring - 1, ring)
        self.high = lax.rem(self.c + 1, ring)
        self.low_edge = self.has_low & (self.h == 0)
        self.high_edge = self.has_high & (self.h == 3)

    def greet(self):
        beyond = [(self.p, block, n) for block in (self.low, self.high) for n in range(4)]
        greet(group_peers(self.ring) + [(self.p, self.c, 3 - self.h)] + beyond)


def pair_at(first, pair):
    return pl.ds(pl.multiple_of(first + pair * 128, 128), 128)


LAGS = (2, (0, 1, 2, 3))


def as_matrix(value):
    rows, cols = value.shape[-2:]
    if cols == 512:
        return value.reshape(-1, 512)
    depth = rows * cols // 512
    parts = value.astype(F32).reshape(-1, rows, cols)
    parts = [parts[:, n:n + depth] for n in range(0, rows, depth)]
    return jnp.concatenate(parts, axis=2).reshape(-1, 512).astype(BF)


def attend_kernel(ring, n_wide, count, x_ref, cos_ref, sin_ref, hg_ref, kf_own, qf_ref, hs_ref, src, gain_src,
                  tok_ref, of_ref, qa_ref, kx, vx, kf_ref, raw_ref, gain_ref, wide, down,
                  rot, nrm, w_tile, gains, q_loc, o_loc, ka, va, tile_sem, local_sem, a2a_send, a2a_recv, rim_send, rim_recv,
                  kf_send, kf_recv, out_send, out_recv, *sems):
    p, c, h = place()
    rim = Rim(ring)
    greet(group_peers(ring) + [(p, c, 3 - h)])
    rows, width = tok_ref.shape
    group = 4 * rows
    mine = pl.ds(pl.multiple_of(h * rows, rows), rows)
    mine_x = pl.ds(pl.multiple_of(HALF + h * rows, rows), rows)
    places = ((0, q_loc, mine), (1, kx, mine_x), (2, vx, mine_x))
    three = pl.ds(0, 3 * rows)
    sides = ((rim.has_high, rim.high, group, 0), (rim.has_low, rim.low, HALF, HALF + group))

    small = Gather(ring, 1, lambda i, go: go(gain_src, lambda p, c, y, x: gains.at[p, c, y, x]), sems[:3])
    work = Gather(ring, count, gather_pick(src, wide, down, n_wide), sems[3:])

    def kf_copy(side):
        there, block, first, to = sides[side]
        return remote(kf_own.at[pl.ds(first - HALF * side if side else first - HALF, HALF)], kf_ref.at[pl.ds(to, HALF)],
                      kf_send.at[side], kf_recv.at[side], (p, block, h))

    def begin(t, carry):
        small.step(t, *LAGS)
        work.step(t, *LAGS)
        return carry
    lax.fori_loop(0, 2, begin, 0)
    for side in range(2):
        pl.when(sides[side][0])(lambda: kf_copy(side).start())
    kf_ref[HALF:HALF + group, :] = kf_own[...]
    lane = lax.broadcasted_iota(jnp.int32, (HALF, 128), 1)
    nothing = jnp.where((lane >= 76) & (lane < 80), FAR, 0.0).astype(BF)
    @pl.when(jnp.logical_not(rim.has_low))
    def _():
        kf_ref[0:HALF, :] = nothing
        for ref in (kx, vx):
            ref[0:HALF, :] = jnp.zeros((HALF, 256), BF)
    @pl.when(jnp.logical_not(rim.has_high))
    def _():
        kf_ref[HALF + group:2 * HALF + group, :] = nothing
        for ref in (kx, vx):
            ref[HALF + group:2 * HALF + group, :] = jnp.zeros((HALF, 256), BF)
    lax.fori_loop(2, 5, begin, 0)

    def share(kind, head, pair):
        ref, at = places[kind][1:]
        cols = pair_at(0, pair)
        part = rot.at[:, pair_at(kind * width + head * 256, pair)]
        there = ref.at[at, cols]
        @pl.when(head == h)
        def _():
            local_copy(part, there, local_sem.at[kind, pair]).start()
        @pl.when(head != h)
        def _():
            remote(part, there, a2a_send.at[kind, pair], a2a_recv.at[kind, pair], (p, c, head)).start()

    def tile_copy(t):
        return local_copy(wide.at[t], w_tile.at[lax.rem(t, 2)], tile_sem.at[lax.rem(t, 2)])

    for k in range(3):
        begin(5 + k, 0)
        for m in range(2):
            tile_copy(2 * k + m).start()
        if k == 0:
            total = gains[0, 0, 0, 0].astype(F32)
            for d in range(1, 8 * ring):
                total = total + gains[d // (4 * ring), d // 4 % ring, d // 2 % 2, d % 2].astype(F32)
            gain_ref[...] = total
            def norm(n, carry):
                at = pl.ds(pl.multiple_of(n * 128, 128), 128)
                x = x_ref[at, :].astype(F32)
                y = x * scale_of(x)
                for m in range(width // 128):
                    part = slice(m * 128, (m + 1) * 128)
                    nrm[at, part] = (y[:, part] * total[m:m + 1, :]).astype(BF)
                return carry
            lax.fori_loop(0, rows // 128, norm, 0)
        for m in range(2):
            t = 2 * k + m
            tile_copy(t).wait()
            def project(n, carry):
                at = pl.ds(pl.multiple_of(n * 128, 128), 128)
                raw = dot(nrm[at, :], as_matrix(w_tile[t % 2])).astype(BF)
                if t < 4:
                    raw_ref[at, t * 512:(t + 1) * 512] = raw
                    gain = hg_ref[t // 2:t // 2 + 1, :]
                    for m in range(4):
                        u = raw[:, m * 128:(m + 1) * 128].astype(F32)
                        y = u * lax.rsqrt(head_mean(u * u) + EPS) * gain
                        y = y * cos_ref[at, :] + swap_halves(y) * sin_ref[at, :]
                        rot[at, t * 512 + m * 128:t * 512 + (m + 1) * 128] = y.astype(BF)
                else:
                    rot[at, t * 512:(t + 1) * 512] = raw
                return carry
            lax.fori_loop(0, rows // 128, project, 0)
            for pair in range(2):
                for m2 in range(2):
                    share(t // 2, t % 2 * 2 + m2, pair)

    def rim_copy(ref, side, kind, pair):
        there, block, first, to = sides[side]
        return remote(ref.at[pl.ds(first, HALF), pair_at(0, pair)], ref.at[pl.ds(to, HALF), pair_at(0, pair)],
                      rim_send.at[side, kind, pair], rim_recv.at[side, kind, pair], (p, block, h))

    blocks = group // QB
    margin = HALF // QB
    def pair_step(pair, carry):
        cols = pair_at(0, pair)
        for kind, ref, at in places:
            local_copy(ref.at[at, cols], ref.at[at, cols], local_sem.at[kind, pair]).wait()
            local_copy(ref.at[three, cols], ref.at[three, cols], a2a_recv.at[kind, pair]).wait()
        for side in range(2):
            @pl.when(sides[side][0])
            def _():
                for kind, ref in ((0, kx), (1, vx)):
                    rim_copy(ref, side, kind, pair).start()
        build_keys(pair, kx, vx, kf_ref, ka, va, None, 1, 1 + group // HALF)
        def step(n, c):
            work.step(8 + pair * blocks + n, *LAGS)
            forward_block(pair, lax.rem(n + margin, blocks), q_loc, qf_ref, hs_ref, ka, va, o_loc, of_ref, qa_ref)
            return c
        lax.fori_loop(0, blocks - 2 * margin, step, 0)
        for side in range(2):
            @pl.when(sides[1 - side][0])
            def _():
                for kind, ref in ((0, kx), (1, vx)):
                    rim_copy(ref, side, kind, pair).wait_recv()
                pl.when(pair == 0)(lambda: kf_copy(side).wait_recv())
        build_keys(pair, kx, vx, kf_ref, ka, va, None, 0, 1)
        build_keys(pair, kx, vx, kf_ref, ka, va, None, 1 + group // HALF, 2 + group // HALF)
        lax.fori_loop(blocks - 2 * margin, blocks, step, 0)
        to_cols = pair_at(h * 256, pair)
        local_copy(o_loc.at[mine, cols], tok_ref.at[:, to_cols], local_sem.at[3, pair]).start()
        for step_ in range(1, 4):
            to = lax.rem(h + step_, 4)
            theirs = pl.ds(pl.multiple_of(to * rows, rows), rows)
            remote(o_loc.at[theirs, cols], tok_ref.at[:, to_cols], out_send.at[pair], out_recv.at[pair], (p, c, to)).start()
        return carry
    lax.fori_loop(0, 2, pair_step, 0)

    def rest(t, carry):
        work.step(t, *LAGS)
        return carry
    lax.fori_loop(8 + 2 * blocks, jnp.maximum(8 + 2 * blocks, work.steps(*LAGS)), rest, 0)
    for pair in range(2):
        cols = pair_at(0, pair)
        local_copy(o_loc.at[mine, cols], tok_ref.at[:, pair_at(h * 256, pair)], local_sem.at[3, pair]).wait()
        part = tok_ref.at[:, pl.ds(0, 384)]
        local_copy(part, part, out_recv.at[pair]).wait()
        local_copy(part, part, out_send.at[pair]).wait()
        for kind, ref, at in places:
            local_copy(ref.at[three, cols], ref.at[three, cols], a2a_send.at[kind, pair]).wait()
        for side in range(2):
            @pl.when(sides[side][0])
            def _():
                for kind, ref in ((0, kx), (1, vx)):
                    rim_copy(ref, side, kind, pair).wait_send()
                if pair == 0:
                    kf_copy(side).wait_send()
    small.drain_all()
    work.drain_all()


def attend(x, cosine, sine, head_gains, kf, qf, hs, src, gain_src, n_wide, ring, collective_id):
    rows, width = x.shape
    group = 4 * rows
    ext = group + 2 * HALF
    count, r, w = src.shape
    dma = pltpu.SemaphoreType.DMA
    return pl.pallas_call(
        functools.partial(attend_kernel, ring, n_wide, count),
        out_shape=(
            jax.ShapeDtypeStruct((rows, width), BF),
            jax.ShapeDtypeStruct((group, 256), F32),
            jax.ShapeDtypeStruct((4, group, 128), BF),
            jax.ShapeDtypeStruct((ext, 256), BF),
            jax.ShapeDtypeStruct((ext, 256), BF),
            jax.ShapeDtypeStruct((ext, 128), BF),
            jax.ShapeDtypeStruct((rows, 2 * width), BF),
            jax.ShapeDtypeStruct((16, 128), F32),
            jax.ShapeDtypeStruct((n_wide, 2, ring, 2, 2, r, w), BF),
            jax.ShapeDtypeStruct((2, ring, 2, 2, (count - n_wide) // 2, r, 2 * w), BF),
        ),
        in_specs=[VM] * 7 + [ANY, ANY],
        out_specs=(VM,) * 8 + (ANY, ANY),
        scratch_shapes=[
            pltpu.VMEM((rows, 3 * width), BF), pltpu.VMEM((rows, width), BF), pltpu.VMEM((2, 2, ring, 2, 2, r, w), BF),
            pltpu.VMEM((2, ring, 2, 2, 16, 128), BF),
            pltpu.VMEM((group, 256), BF), pltpu.VMEM((group, 256), BF),
            pltpu.VMEM((2, ext, 128), BF), pltpu.VMEM((2, ext, 128), BF),
            dma((2,)), dma((4, 2)), dma((3, 2)), dma((3, 2)), dma((2, 2, 2)), dma((2, 2, 2)), dma((2,)), dma((2,)), dma((2,)), dma((2,)),
        ] + gather_sems(1) + gather_sems(count),
        compiler_params=pltpu.CompilerParams(collective_id=collective_id, has_side_effects=True, vmem_limit_bytes=60 * MIB),
        name="attend",
    )(x, cosine, sine, head_gains, kf, qf, hs, src, gain_src)


def return_kernel(ring, layout, count, *refs):
    n = len(layout)
    grads = refs[:n]
    (d_tok, kx, vx, kf_ref, qf_ref, qa_ref, of_ref, back, bias_ref, out,
     do_loc, dq_loc, dk_loc, dv_loc, rims, ka, va, kt, dka, dva, same, every,
     local_sem, in_send, in_recv, back_send, back_recv, rim_send, rim_recv,
     load, own, b1, b2, b3, load_sem, send_sem, recv_sem) = refs[n:]
    p, c, h = place()
    rim = Rim(ring)
    greet(group_peers(ring) + [(p, c, 3 - h)])
    rows, width = d_tok.shape
    group = 4 * rows
    mine = pl.ds(pl.multiple_of(h * rows, rows), rows)
    three = pl.ds(0, 3 * rows)
    for pair in range(2):
        cols = pair_at(0, pair)
        local_copy(d_tok.at[:, pair_at(h * 256, pair)], do_loc.at[mine, cols], local_sem.at[0, pair]).start()
        for step in range(1, 4):
            to = lax.rem(h + step, 4)
            remote(d_tok.at[:, pair_at(to * 256, pair)], do_loc.at[mine, cols], in_send.at[pair], in_recv.at[pair], (p, c, to)).start()

    def write(i, total):
        out[i] = total

    work = Scatter(ring, count, scatter_pick(grads, layout, out.shape[-1]), (load, own, b1, b2, b3),
                   (load_sem, send_sem, recv_sem), out, write)
    def begin(t, carry):
        work.step(t)
        return carry
    lax.fori_loop(0, 3, begin, 0)
    same[...] = jnp.zeros_like(same)
    every[...] = jnp.zeros_like(every)

    trios = ((0, dq_loc, 0), (1, dk_loc, HALF), (2, dv_loc, HALF))
    kinds = ((0, dk_loc), (1, dv_loc))
    sides = ((rim.has_high, rim.high, HALF + group), (rim.has_low, rim.low, 0))

    def rim_copy(ref, side, kind, pair):
        there, block, first = sides[side]
        cols = pair_at(0, pair)
        return remote(ref.at[pl.ds(first, HALF), cols], rims.at[side, kind, :, cols],
                      rim_send.at[side, kind, pair], rim_recv.at[side, kind, pair], (p, block, h))

    def give(kind, pair, wanted):
        _, ref, skip = trios[kind]
        cols, at = pair_at(0, pair), pair_at(kind * width + h * 256, pair)
        for step in range(4):
            to = lax.rem(h + step, 4)
            theirs = ref.at[pl.ds(pl.multiple_of(skip + to * rows, rows), rows), cols]
            def go():
                if step == 0:
                    local_copy(theirs, back.at[:, at], local_sem.at[1 + kind, pair]).start()
                else:
                    remote(theirs, back.at[:, at], back_send.at[kind, pair], back_recv.at[kind, pair], (p, c, to)).start()
            if wanted is None:
                go()
            else:
                edge = (to == 0) | (to == 3)
                pl.when(edge if wanted else jnp.logical_not(edge))(go)

    def edges_back(pair):
        cols = pair_at(0, pair)
        for side in range(2):
            first = HALF if side == 0 else group
            @pl.when(sides[1 - side][0])
            def _():
                for kind, ref in kinds:
                    rim_copy(ref, side, kind, pair).wait_recv()
                    for m in range(4):
                        to = pl.ds(first + m * 128, 128)
                        more = rims[side, kind, pl.ds(m * 128, 128), cols].astype(F32)
                        ref[to, cols] = (ref[to, cols].astype(F32) + more).astype(BF)
        give(1, pair, True)
        give(2, pair, True)

    blocks = group // QB
    def pair_step(pair, carry):
        cols = pair_at(0, pair)
        build_keys(pair, kx, vx, kf_ref, ka, va, kt)
        dka[...] = jnp.zeros_like(dka)
        dva[...] = jnp.zeros_like(dva)
        local_copy(do_loc.at[mine, cols], do_loc.at[mine, cols], local_sem.at[0, pair]).wait()
        local_copy(do_loc.at[three, cols], do_loc.at[three, cols], in_recv.at[pair]).wait()
        def step(m, c):
            work.step(3 + pair * blocks + m)
            backward_block(pair, m, qf_ref, qa_ref, do_loc, of_ref, ka, va, kt, dka, dva, dq_loc, same, every)
            return c
        lax.fori_loop(0, blocks // 2, step, 0)
        pl.when(pair == 1)(lambda: edges_back(0))
        lax.fori_loop(blocks // 2, blocks, step, 0)
        backward_finish(pair, dka, dva, dk_loc, dv_loc)
        for side in range(2):
            @pl.when(sides[side][0])
            def _():
                for kind, ref in kinds:
                    rim_copy(ref, side, kind, pair).start()
        give(1, pair, False)
        give(2, pair, False)
        give(0, pair, None)
        return carry
    lax.fori_loop(0, 2, pair_step, 0)

    def total(x):
        return jnp.sum(jnp.sum(x, axis=1, keepdims=True), axis=2, keepdims=True)
    s, e = total(same[...]), total(every[...])
    lane = lax.broadcasted_iota(jnp.int32, (4, 1, 128), 2)
    bias_ref[...] = jnp.where(lane == 0, s, jnp.where(lane == 1, e - s, 0.0))
    edges_back(1)

    def rest(t, carry):
        work.step(t)
        return carry
    lax.fori_loop(3 + 2 * blocks, jnp.maximum(3 + 2 * blocks, work.steps()), rest, 0)

    part = back.at[:, pl.ds(0, 384)]
    for pair in range(2):
        cols = pair_at(0, pair)
        for kind in range(3):
            at = pair_at(kind * width + h * 256, pair)
            local_copy(back.at[:, at], back.at[:, at], local_sem.at[1 + kind, pair]).wait()
            local_copy(part, part, back_recv.at[kind, pair]).wait()
            local_copy(part, part, back_send.at[kind, pair]).wait()
        local_copy(do_loc.at[three, cols], do_loc.at[three, cols], in_send.at[pair]).wait()
        for side in range(2):
            @pl.when(sides[side][0])
            def _():
                for kind, ref in kinds:
                    rim_copy(ref, side, kind, pair).wait_send()
    work.drain_all()


def attend_back(grads, layout, d_tok, kx, vx, kf, qf, qa, of, ring, collective_id):
    rows, width = d_tok.shape
    group = 4 * rows
    ext = group + 2 * HALF
    r, w = grads[0].shape[-2:]
    count = sum(size for size, _ in layout)
    dma = pltpu.SemaphoreType.DMA
    return pl.pallas_call(
        functools.partial(return_kernel, ring, layout, count),
        out_shape=(
            jax.ShapeDtypeStruct((rows, 3 * width), BF),
            jax.ShapeDtypeStruct((4, 1, 128), F32),
            jax.ShapeDtypeStruct((count, r, w), F32),
        ),
        in_specs=[ANY] * len(grads) + [ANY] + [VM] * 6,
        out_specs=(VM,) * 3,
        scratch_shapes=[
            pltpu.VMEM((group, 256), BF), pltpu.VMEM((group, 256), BF), pltpu.VMEM((ext, 256), BF), pltpu.VMEM((ext, 256), BF),
            pltpu.VMEM((2, 2, HALF, 256), BF),
            pltpu.VMEM((2, ext, 128), BF), pltpu.VMEM((2, ext, 128), BF), pltpu.VMEM((2, 128, ext), BF),
            pltpu.VMEM((2, ext, 128), F32), pltpu.VMEM((2, ext, 128), F32),
            pltpu.VMEM((4, 8, QB), F32), pltpu.VMEM((4, 8, QB), F32),
            dma((4, 2)), dma((2,)), dma((2,)), dma((3, 2)), dma((3, 2)), dma((2, 2, 2)), dma((2, 2, 2)),
        ] + scatter_scratch(ring, count, r, w),
        compiler_params=pltpu.CompilerParams(collective_id=collective_id, has_side_effects=True, vmem_limit_bytes=63 * MIB),
        name="attend_back",
    )(*grads, d_tok, kx, vx, kf, qf, qa, of)


def last_kernel(ring, count, grads, small, out, small_out, sums, came, far, small_send, small_recv, *rest):
    greet(group_peers(ring))
    buffers, sems = rest[:5], rest[5:]
    def write(i, total):
        out[i] = total
    work = Scatter(ring, count, scatter_pick((grads,), ((count, True),), out.shape[-1]), buffers, sems, out, write)
    p, c, h = place()
    peers = (work.core, work.xpeer, work.ypeer)

    def hop(n):
        return remote(sums.at[n], came.at[n], small_send.at[n], small_recv.at[n], peers[n])

    def far_hop(step):
        return remote(sums.at[3], far.at[step - 1], small_send.at[3], small_recv.at[3], (p, lax.rem(c + step, ring), h))

    sums[0] = small[...]
    hop(0).start()
    def body(t, carry):
        work.step(t)
        for n in range(3):
            @pl.when(t == 2 + 2 * n)
            def _():
                hop(n).wait_recv()
                sums[n + 1] = sums[n] + came[n]
                if n < 2:
                    hop(n + 1).start()
                else:
                    for step in range(1, ring):
                        far_hop(step).start()
        return carry
    lax.fori_loop(0, work.steps(), body, 0)
    local_copy(far, far, small_recv.at[3]).wait()
    total = sums[3]
    for step in range(1, ring):
        total = total + far[step - 1]
    small_out[...] = total
    for n in range(3):
        hop(n).wait_send()
    local_copy(far, far, small_send.at[3]).wait()
    work.drain_all()


def last_scatter(grads, small, ring, collective_id):
    count = grads.shape[0]
    r, w = grads.shape[-2:]
    n = small.shape[0]
    dma = pltpu.SemaphoreType.DMA
    return pl.pallas_call(
        functools.partial(last_kernel, ring, count),
        out_shape=(jax.ShapeDtypeStruct((count, r, w), F32), jax.ShapeDtypeStruct((n, 128), F32)),
        in_specs=[ANY, VM],
        out_specs=(VM, VM),
        scratch_shapes=[pltpu.VMEM((4, n, 128), F32), pltpu.VMEM((3, n, 128), F32), pltpu.VMEM((ring - 1, n, 128), F32),
                        dma((4,)), dma((4,))] + scatter_scratch(ring, count, r, w),
        compiler_params=pltpu.CompilerParams(collective_id=collective_id, has_side_effects=True, vmem_limit_bytes=40 * MIB),
        name="rsum",
    )(grads, small)


def to_blocks(weight, depth, r, w):
    parts = weight.reshape(-1, depth, weight.shape[1] // 512, r // depth, w)
    return parts.transpose(2, 0, 3, 1, 4).reshape(weight.shape[1] // 512, -1, r, w)


def from_blocks(blocks, depth):
    n, (r, w) = blocks.shape[0], blocks.shape[-2:]
    return blocks.reshape(n, -1, r // depth, depth, w).swapaxes(2, 3).reshape(n, -1, 512)


def local(
    inputs, cotangent, w_qkv, w_out, w_gate, w_up, w_down, gain_attn, gain_ffn, q_gain, k_gain, head_bias,
    segment_ids, variate_ids, time_index,
):
    ring = lax.axis_size("cp")
    head = lax.axis_index("hd")
    rows, width = inputs.shape
    depth = w_qkv.shape[0]
    r, w = item_shape(depth)

    me = (lax.axis_index("pack") * ring + lax.axis_index("cp")) * 4 + head
    down_pieces = w_down.reshape(4, r, 2, w).swapaxes(1, 2).reshape(8, r, w)
    src = jnp.concatenate([to_blocks(weight, depth, r, w)[:, 0] for weight in (w_qkv, w_out, w_gate, w_up)] + [down_pieces])
    gain_src = lax.dynamic_update_slice(jnp.zeros((2, width), BF), jnp.stack([gain_attn, gain_ffn]), (0, me * depth))
    gain_src = gain_src.reshape(16, 128)

    times = lax.dynamic_slice_in_dim(time_index, head * rows, rows, 0)
    lane = jnp.arange(128)
    frequency = jnp.exp(-math.log(theta_base) * 2.0 * (lane % 32).astype(F32) / HDIM)
    angle = times.astype(F32)[:, None] * frequency[None, :]
    cosine = jnp.cos(angle)
    sine = jnp.sin(angle) * jnp.where(lane % 64 < 32, -1.0, 1.0)[None, :]
    head_gains = jnp.stack([jnp.concatenate([q_gain, q_gain]), jnp.concatenate([k_gain, k_gain])])

    qf, kf_own = features(segment_ids, variate_ids)
    hs = head_scales(lax.dynamic_slice_in_dim(head_bias, head * 4, 4, 0))

    heads_out, of, qa, kx, vx, kf, raw, gains, wide, down = attend(
        inputs, cosine, sine, head_gains, kf_own, qf, hs, src, gain_src, 24, ring, 1)
    wide = from_blocks(wide, depth)
    gains = gains.reshape(2, 1, width)
    layer_out, d_hidden, d_heads, g_down, g_out, g_gffn, pairs = ffn(
        inputs, heads_out, cotangent, gains[1], wide, down.reshape(-1, width), ring, (r, w), 4)

    def blocks(grad):
        parts = grad.reshape(grad.shape[0], -1, depth, r // depth, w).swapaxes(2, 3)
        return parts.reshape(-1, 2, ring, 2, 2, r, w)

    grads = (blocks(g_out), g_down.reshape(2, ring, 2, 2, 4, r, 2 * w))
    layout = ((2, True), (8, False))
    d_proj, g_bias, items = attend_back(grads, layout, d_heads, kx, vx, kf, qf, qa, of, ring, 2)
    g_qkv, grad_inputs, g_gattn, g_heads = unproject(
        inputs, gains[0], wide, cosine, sine, head_gains, raw, d_proj, d_hidden)
    bias_all = lax.dynamic_update_slice_in_dim(jnp.zeros((HEADS, 2), F32), g_bias[:, 0, :2], head * 4, 0)
    small = jnp.concatenate([
        g_gattn.reshape(8, 128), g_gffn.reshape(8, 128), g_heads,
        jnp.pad(bias_all.reshape(1, 32), ((0, 5), (0, 96)))])
    last, small = last_scatter(blocks(g_qkv), small, ring, 3)

    def columns(part):
        return from_blocks(part, depth).swapaxes(0, 1).reshape(depth, -1)

    pairs = pairs.reshape(8, 2, r, w)
    own_gains = lax.dynamic_slice_in_dim(small[:16].reshape(2, width), me * depth, depth, 1)
    own_heads = small[16:18, :HDIM] + small[16:18, HDIM:]
    return (
        layer_out, grad_inputs, columns(last), columns(items[:2]), columns(pairs[:, 0]), columns(pairs[:, 1]),
        items[2:].reshape(4, 2, r, w).swapaxes(1, 2).reshape(w_down.shape),
        own_gains[0], own_gains[1], own_heads[0], own_heads[1], small[18, :32].reshape(HEADS, 2),
    )


def solution(mesh):
    return jax.shard_map(
        local,
        mesh=mesh,
        in_specs=(
            P(("pack", "cp", "hd"), None),
            P(("pack", "cp", "hd"), None),
            P(("pack", "cp", "hd"), None),
            P(("pack", "cp", "hd"), None),
            P(("pack", "cp", "hd"), None),
            P(("pack", "cp", "hd"), None),
            P(("pack", "cp", "hd"), None),
            P(("pack", "cp", "hd")),
            P(("pack", "cp", "hd")),
            P(),
            P(),
            P(),
            P(("pack", "cp")),
            P(("pack", "cp")),
            P(("pack", "cp")),
        ),
        out_specs=(
            P(("pack", "cp", "hd"), None),
            P(("pack", "cp", "hd"), None),
            P(("pack", "cp", "hd"), None),
            P(("pack", "cp", "hd"), None),
            P(("pack", "cp", "hd"), None),
            P(("pack", "cp", "hd"), None),
            P(("pack", "cp", "hd"), None),
            P(("pack", "cp", "hd")),
            P(("pack", "cp", "hd")),
            P(),
            P(),
            P(),
        ),
        check_vma=False,
    )
```

```python
import functools
import math

import jax
import jax.numpy as jnp
from jax import lax
from jax.experimental import pallas as pl
from jax.experimental.pallas import tpu as pltpu
from jax.sharding import PartitionSpec as P

HEADS = 16
HDIM = 64
HALF = 512
QB = 256
SPAN = QB + 2 * HALF
FAR = -1e30
EPS = 1e-6
theta_base = 10000.0
MIB = 2**20
F32, BF = jnp.float32, jnp.bfloat16
MESH = pl.DeviceIdType.MESH
VM = pl.BlockSpec(memory_space=pltpu.VMEM)
ANY = pl.BlockSpec(memory_space=pl.ANY)
ALL = slice(None)


def item_shape(rows):
    full = max(rows, 16)
    return full, rows * 512 // full


def place():
    return lax.axis_index("pack"), lax.axis_index("cp"), lax.axis_index("hd")


def greet(peers):
    barrier = pltpu.get_barrier_semaphore()
    for peer in peers:
        pl.semaphore_signal(barrier, inc=1, device_id=peer, device_id_type=MESH)
    pl.semaphore_wait(barrier, len(peers))


def group_peers(ring):
    p, c, h = place()
    peers = [(1 - p, c, h), (p, c, h + 1 - 2 * lax.rem(h, 2)), (p, c, lax.rem(h + 2, 4))]
    peers += [(p, lax.rem(c + step, ring), h) for step in range(1, ring)]
    return peers


class Scatter:
    def __init__(self, ring, count, pick, buffers, sems, out, write):
        self.ring, self.count, self.pick = ring, count, pick
        self.load, self.own, self.b1, self.b2, self.b3 = buffers
        self.slots = self.load.shape[0]
        self.load_sem, self.send_sem, self.recv_sem = sems
        self.out, self.write = out, write
        self.p, self.c, self.h = place()
        self.hy, self.hx = self.h // 2, lax.rem(self.h, 2)
        self.core = (1 - self.p, self.c, self.h)
        self.xpeer = (self.p, self.c, self.hy * 2 + 1 - self.hx)
        self.ypeer = (self.p, self.c, (1 - self.hy) * 2 + self.hx)

    def remote(self, i, stage, src, dst, device):
        return pltpu.make_async_remote_copy(
            src_ref=src, dst_ref=dst, send_sem=self.send_sem.at[stage, i],
            recv_sem=self.recv_sem.at[stage, i], device_id=device, device_id_type=MESH)

    def copy0(self, i, src):
        return self.remote(i, 0, src, self.own.at[i], self.core)

    def copy1(self, i, first_y):
        if first_y:
            return self.remote(i, 1, self.own.at[i, :, 1 - self.hy], self.b1.at[i], self.ypeer)
        return self.remote(i, 1, self.own.at[i, :, :, 1 - self.hx], self.b1.at[i], self.xpeer)

    def copy2(self, i, first_y):
        if first_y:
            return self.remote(i, 2, self.own.at[i, :, self.hy, 1 - self.hx], self.b2.at[i], self.xpeer)
        return self.remote(i, 2, self.own.at[i, :, 1 - self.hy, self.hx], self.b2.at[i], self.ypeer)

    def copy3(self, i, step):
        peer = lax.rem(self.c + step, self.ring)
        return self.remote(i, 3, self.own.at[i, peer, self.hy, self.hx], self.b3.at[i, step - 1], (self.p, peer, self.h))

    def begin(self, i):
        def go(mine, other):
            slot = lax.rem(i, self.slots)
            pltpu.make_async_copy(mine, self.load.at[slot], self.load_sem.at[slot]).start()
            self.copy0(i, other).start()
        self.pick(i, self.p, go)

    def mine(self, i, k):
        return self.load[lax.rem(i, self.slots), k]

    def landed(self, i):
        slot = lax.rem(i, self.slots)
        pltpu.make_async_copy(self.load.at[slot], self.load.at[slot], self.load_sem.at[slot]).wait()

    def stage1(self, i, first_y):
        self.landed(i)
        self.copy0(i, self.own.at[i]).wait_recv()
        def add(k, carry):
            self.own[i, k] = self.own[i, k] + self.mine(i, k)
            return carry
        lax.fori_loop(0, self.ring, add, 0)
        self.copy1(i, first_y).start()

    def stage2(self, i, first_y):
        self.copy1(i, first_y).wait_recv()
        def add(k, carry):
            for m in range(2):
                at = (i, k, self.hy, m) if first_y else (i, k, m, self.hx)
                self.own[at] = self.own[at] + self.b1[i, k, m]
            return carry
        lax.fori_loop(0, self.ring, add, 0)
        self.copy2(i, first_y).start()

    def stage3(self, i, first_y):
        self.copy2(i, first_y).wait_recv()
        def add(k, carry):
            at = (i, k, self.hy, self.hx)
            self.own[at] = self.own[at] + self.b2[i, k]
            return carry
        lax.fori_loop(0, self.ring, add, 0)
        for step in range(1, self.ring):
            self.copy3(i, step).start()

    def finish(self, i):
        pltpu.make_async_copy(self.b3.at[i], self.b3.at[i], self.recv_sem.at[3, i]).wait()
        total = self.own[i, self.c, self.hy, self.hx].astype(jnp.float32)
        for step in range(1, self.ring):
            total = total + self.b3[i, step - 1].astype(jnp.float32)
        self.write(i, total)

    def drain(self, i, first_y):
        self.copy0(i, self.own.at[i]).wait_send()
        self.copy1(i, first_y).wait_send()
        self.copy2(i, first_y).wait_send()
        pltpu.make_async_copy(self.b3.at[i], self.b3.at[i], self.send_sem.at[3, i]).wait()

    def step(self, t, ahead=3, lags=(0, 2, 4, 6)):
        pairs = (self.count + 1) // 2
        def both(pair, act):
            for first_y in (True, False):
                i = 2 * pair + (0 if first_y else 1)
                guard = (pair >= 0) & (i < self.count) & (i >= 0)
                pl.when(guard)(functools.partial(act, i, first_y))
        both(t, lambda i, f: self.begin(i))
        both(t - ahead - lags[0], self.stage1)
        both(t - ahead - lags[1], self.stage2)
        both(t - ahead - lags[2], self.stage3)
        both(t - ahead - lags[3], lambda i, f: self.finish(i))

    def steps(self, ahead=3, lags=(0, 2, 4, 6)):
        return (self.count + 1) // 2 + ahead + lags[3]

    def drain_all(self):
        def one(t, carry):
            for first_y in (True, False):
                i = 2 * t + (0 if first_y else 1)
                pl.when(i < self.count)(functools.partial(self.drain, i, first_y))
            return carry
        lax.fori_loop(0, (self.count + 1) // 2, one, 0)


def scatter_scratch(ring, count, rows, cols):
    bf = jnp.bfloat16
    return [
        pltpu.VMEM((4, ring, 2, 2, rows, cols), bf),
        pltpu.VMEM((count, ring, 2, 2, rows, cols), bf),
        pltpu.VMEM((count, ring, 2, rows, cols), bf),
        pltpu.VMEM((count, ring, rows, cols), bf),
        pltpu.VMEM((count, ring - 1, rows, cols), bf),
        pltpu.SemaphoreType.DMA((4,)),
        pltpu.SemaphoreType.DMA((4, count)),
        pltpu.SemaphoreType.DMA((4, count)),
    ]


def scatter_pick(grads, layout, cols):
    def pick(i, p, go):
        start = 0
        for ref, (size, outer) in zip(grads, layout):
            j = i - start
            def run(ref=ref, j=j, outer=outer):
                if outer:
                    go(ref.at[j, p], ref.at[j, 1 - p])
                else:
                    at = pl.ds(pl.multiple_of(lax.rem(j, 2) * cols, cols), cols)
                    go(ref.at[p, :, :, :, j // 2, :, at], ref.at[1 - p, :, :, :, j // 2, :, at])
            pl.when((j >= 0) & (j < size))(run)
            start += size
    return pick


class Gather:
    def __init__(self, ring, count, pick, sems):
        self.ring, self.count, self.pick = ring, count, pick
        self.local_sem, self.send_sem, self.recv_sem = sems
        self.p, self.c, self.h = place()
        self.hy, self.hx = self.h // 2, lax.rem(self.h, 2)
        self.core = (1 - self.p, self.c, self.h)
        self.xpeer = (self.p, self.c, self.hy * 2 + 1 - self.hx)
        self.ypeer = (self.p, self.c, (1 - self.hy) * 2 + self.hx)

    def remote(self, i, stage, src, dst, device):
        return pltpu.make_async_remote_copy(
            src_ref=src, dst_ref=dst, send_sem=self.send_sem.at[stage, i],
            recv_sem=self.recv_sem.at[stage, i], device_id=device, device_id_type=MESH)

    def same(self, i, stage, ref, device):
        return self.remote(i, stage, ref, ref, device)

    def begin(self, i, first_x, mid):
        def go(src, out):
            mine = out(self.p, self.c, self.hy, self.hx)
            pltpu.make_async_copy(src, mine, self.local_sem.at[i]).start()
            if mid:
                self.remote(i, 0, src, mine, self.near(first_x)).start()
                return
            for step in range(1, self.ring):
                peer = (self.p, lax.rem(self.c + step, self.ring), self.h)
                self.remote(i, 0, src, mine, peer).start()
        self.pick(i, go)

    def near(self, first_x):
        return self.xpeer if first_x else self.ypeer

    def block(self, out, first_x, mine):
        if first_x:
            return out(self.p, self.c, self.hy, self.hx if mine else 1 - self.hx)
        return out(self.p, self.c, self.hy if mine else 1 - self.hy, self.hx)

    def couple(self, out, first_x, at):
        return out(self.p, at, self.hy, ALL) if first_x else out(self.p, at, ALL, self.hx)

    def wait_for(self, ref, sem):
        pltpu.make_async_copy(ref, ref, sem).wait()

    def stage1(self, i, first_x, mid):
        def go(src, out):
            mine = out(self.p, self.c, self.hy, self.hx)
            pltpu.make_async_copy(src, mine, self.local_sem.at[i]).wait()
            if mid:
                self.same(i, 0, self.block(out, first_x, False), self.core).wait_recv()
                both = self.couple(out, first_x, self.c)
                for step in range(1, self.ring):
                    self.same(i, 1, both, (self.p, lax.rem(self.c + step, self.ring), self.h)).start()
                return
            self.wait_for(out(self.p, pl.ds(0, self.ring - 1), self.hy, self.hx), self.recv_sem.at[0, i])
            column = out(self.p, ALL, self.hy, self.hx)
            self.same(i, 1, column, self.near(first_x)).start()
            self.same(i, 3, column, self.core).start()
        self.pick(i, go)

    def first(self, out, mine, first_x):
        if first_x:
            return out(self.p, ALL, self.hy, self.hx if mine else 1 - self.hx)
        return out(self.p, ALL, self.hy if mine else 1 - self.hy, self.hx)

    def second(self, out, mine, first_x):
        if first_x:
            return out(self.p, ALL, self.hy if mine else 1 - self.hy, ALL)
        return out(self.p, ALL, ALL, self.hx if mine else 1 - self.hx)

    def stage2(self, i, first_x, mid):
        def go(src, out):
            half = self.second(out, True, first_x)
            if mid:
                self.wait_for(self.couple(out, first_x, pl.ds(0, self.ring - 1)), self.recv_sem.at[1, i])
                self.same(i, 2, half, self.near(not first_x)).start()
                self.same(i, 3, half, self.core).start()
                return
            came = self.first(out, False, first_x)
            self.same(i, 1, came, self.core).wait_recv()
            self.same(i, 2, half, self.near(not first_x)).start()
            self.same(i, 3, came, self.core).start()
        self.pick(i, go)

    def stage3(self, i, first_x, mid):
        def go(src, out):
            came = self.second(out, False, first_x)
            self.same(i, 2, came, self.core).wait_recv()
            self.same(i, 3, came, self.core).start()
        self.pick(i, go)

    def finish(self, i, first_x, mid):
        def go(src, out):
            self.wait_for(out(1 - self.p, ALL, ALL, ALL), self.recv_sem.at[3, i])
        self.pick(i, go)

    def drain(self, i, first_x, mid):
        def go(src, out):
            if mid:
                self.same(i, 0, self.block(out, first_x, True), self.core).wait_send()
                self.wait_for(self.couple(out, first_x, pl.ds(0, self.ring - 1)), self.send_sem.at[1, i])
            else:
                self.wait_for(out(self.p, pl.ds(0, self.ring - 1), self.hy, self.hx), self.send_sem.at[0, i])
                self.same(i, 1, self.first(out, True, first_x), self.core).wait_send()
            self.same(i, 2, self.second(out, True, first_x), self.core).wait_send()
            self.wait_for(out(self.p, ALL, ALL, ALL), self.send_sem.at[3, i])
        self.pick(i, go)

    def both(self, pair, act):
        middle = lax.rem(pair, 2) != 0
        for first_x in (True, False):
            i = 2 * pair + (0 if first_x else 1)
            there = (pair >= 0) & (i < self.count) & (i >= 0)
            pl.when(there & middle)(functools.partial(act, i, first_x, True))
            pl.when(there & jnp.logical_not(middle))(functools.partial(act, i, first_x, False))

    def step(self, t, ahead=2, lags=(0, 1, 2, 3)):
        self.both(t, self.begin)
        self.both(t - ahead - lags[0], self.stage1)
        self.both(t - ahead - lags[1], self.stage2)
        self.both(t - ahead - lags[2], self.stage3)
        self.both(t - ahead - lags[3], self.finish)

    def steps(self, ahead=2, lags=(0, 1, 2, 3)):
        return (self.count + 1) // 2 + ahead + lags[3]

    def drain_all(self):
        def one(t, carry):
            self.both(t, self.drain)
            return carry
        lax.fori_loop(0, (self.count + 1) // 2, one, 0)


def gather_sems(count):
    return [
        pltpu.SemaphoreType.DMA((count,)),
        pltpu.SemaphoreType.DMA((4, count)),
        pltpu.SemaphoreType.DMA((4, count)),
    ]


def gather_pick(src, wide, down, n_wide):
    cols = src.shape[-1]
    def pick(i, go):
        @pl.when(i < n_wide)
        def _():
            go(src.at[i], lambda p, c, y, x: wide.at[i, p, c, y, x])
        @pl.when(i >= n_wide)
        def _():
            j = i - n_wide
            at = pl.ds(pl.multiple_of(lax.rem(j, 2) * cols, cols), cols)
            go(src.at[i], lambda p, c, y, x: down.at[p, c, y, x, j // 2, :, at])
    return pick


def dot_tb(a, b):
    return lax.dot_general(a, b, (((1,), (1,)), ((), ())), preferred_element_type=jnp.float32)


def dot(a, b):
    return jnp.dot(a, b, preferred_element_type=jnp.float32)


def lanes(rows):
    return lax.broadcasted_iota(jnp.int32, (rows, 128), 1)


def split3(x):
    hi = x.astype(jnp.bfloat16).astype(jnp.float32)
    mid = (x - hi).astype(jnp.bfloat16).astype(jnp.float32)
    lo = x - hi - mid
    return hi, mid, lo


def at_lanes(base, first, values):
    lane = lanes(base.shape[0])
    for n, value in enumerate(values):
        base = jnp.where(lane == first + n, value, base)
    return base


def halves(x):
    return x, pltpu.roll(x, 64, 1)


def build_keys(pair, k_ref, v_ref, kf_ref, ka, va, kt=None, first=0, last=None):
    at = pl.ds(pl.multiple_of(pair * 128, 128), 128)
    rows = k_ref.shape[0]
    chunk = 512
    def one(n, carry):
        r = pl.ds(pl.multiple_of(n * chunk, chunk), chunk)
        lane = lanes(chunk)
        keys = halves(k_ref[r, at].astype(jnp.float32))
        values = halves(v_ref[r, at].astype(jnp.float32))
        feat = kf_ref[r, :].astype(jnp.float32)
        for m in range(2):
            full = jnp.where(lane < 64, keys[m], feat)
            ka[m, r, :] = full.astype(jnp.bfloat16)
            if kt is not None:
                kt[m, :, r] = full.T.astype(jnp.bfloat16)
            ones = jnp.where(lane < 67, 1.0, 0.0)
            va[m, r, :] = jnp.where(lane < 64, values[m], ones).astype(jnp.bfloat16)
        return carry
    lax.fori_loop(first, rows // chunk if last is None else last, one, 0)


def forward_block(pair, n, q_ref, qf_ref, hs_ref, ka, va, o_ref, of_ref, qa_ref):
    at = pl.ds(pl.multiple_of(pair * 128, 128), 128)
    r = pl.ds(pl.multiple_of(n * QB, QB), QB)
    lane = lanes(QB)
    queries = halves(q_ref[r, at].astype(jnp.float32) * (1.0 / math.sqrt(HDIM)))
    feat = qf_ref[r, :].astype(jnp.float32)
    row = lax.broadcasted_iota(jnp.int32, (QB, QB), 0)
    col = lax.broadcasted_iota(jnp.int32, (QB, QB), 1)
    outs = []
    for m in range(2):
        qa = jnp.where(lane < 64, queries[m], feat * hs_ref[pl.ds(pair * 2 + m, 1), :])
        qb = qa.astype(jnp.bfloat16)
        def part(first, size, mask=None):
            keys = pl.ds(pl.multiple_of(n * QB + first, QB), size)
            s = dot_tb(qb, ka[m, keys, :])
            if mask is not None:
                s = jnp.where(mask, s, FAR)
            return dot(jnp.exp(s).astype(jnp.bfloat16), va[m, keys, :])
        o = part(0, QB, col >= row) + part(QB, SPAN - 2 * QB) + part(SPAN - QB, QB, col <= row)
        total = o[:, 64:65]
        outs.append(o * (1.0 / total))
        hi, mid, lo = split3(-jnp.log(total))
        qa_ref[pair * 2 + m, r, :] = at_lanes(qa, 80, (hi, mid, lo)).astype(jnp.bfloat16)
    both = jnp.where(lane < 64, outs[0], pltpu.roll(outs[1], 64, 1))
    of_ref[r, at] = both
    o_ref[r, at] = both.astype(jnp.bfloat16)


def backward_block(pair, n, qf_ref, qa_ref, do_ref, of_ref, ka, va, kt, dka, dva, dq_ref, same, every):
    at = pl.ds(pl.multiple_of(pair * 128, 128), 128)
    r = pl.ds(pl.multiple_of(n * QB, QB), QB)
    lane = lanes(QB)
    grads = do_ref[r, at].astype(jnp.float32)
    terms = grads * of_ref[r, :]
    pieces = halves(grads)
    row = lax.broadcasted_iota(jnp.int32, (QB, QB), 0)
    col = lax.broadcasted_iota(jnp.int32, (QB, QB), 1)
    dqs = []
    qft = qf_ref[r, :].astype(jnp.float32).T[64:72, :]
    for m in range(2):
        own = (lane < 64) if m == 0 else (lane >= 64)
        delta = jnp.sum(jnp.where(own, terms, 0.0), axis=1, keepdims=True)
        da = at_lanes(jnp.where(lane < 64, pieces[m], 0.0), 64, split3(-delta)).astype(jnp.bfloat16)
        qb = qa_ref[m, r, :]
        dq = jnp.zeros((128, QB), jnp.float32)
        for first, size, edge in ((0, QB, 0), (QB, SPAN - 2 * QB, None), (SPAN - QB, QB, 1)):
            keys = pl.ds(pl.multiple_of(n * QB + first, QB), size)
            s = dot_tb(ka[m, keys, :], qb)
            if edge is not None:
                s = jnp.where((row >= col) if edge == 0 else (row <= col), s, FAR)
            p = jnp.exp(s)
            dp = dot_tb(va[m, keys, :], da)
            ds = (p * dp).astype(jnp.bfloat16)
            dva[m, keys, :] += dot(p.astype(jnp.bfloat16), da)
            dka[m, keys, :] += dot(ds, qb)
            dq = dq + dot(kt[m, :, keys], ds)
        dqs.append(dq[:64, :])
        sums = dq[64:72, :]
        pick = lax.broadcasted_iota(jnp.int32, (8, QB), 0) < 4
        h = pair * 2 + m
        same[h] += jnp.where(pick, sums * qft, 0.0)
        every[h] += jnp.where(pick, sums, 0.0)
    dq_ref[r, at] = (jnp.concatenate(dqs, axis=0).T * (1.0 / math.sqrt(HDIM))).astype(dq_ref.dtype)


def backward_finish(pair, dka, dva, dk_ref, dv_ref):
    at = pl.ds(pl.multiple_of(pair * 128, 128), 128)
    chunk = 512
    def one(n, carry):
        r = pl.ds(pl.multiple_of(n * chunk, chunk), chunk)
        lane = lanes(chunk)
        dk_ref[r, at] = jnp.where(lane < 64, dka[0, r, :], pltpu.roll(dka[1, r, :], 64, 1)).astype(dk_ref.dtype)
        dv_ref[r, at] = jnp.where(lane < 64, dva[0, r, :], pltpu.roll(dva[1, r, :], 64, 1)).astype(dv_ref.dtype)
        return carry
    lax.fori_loop(0, dk_ref.shape[0] // chunk, one, 0)


def features(seg, var):
    lane = jnp.arange(128)[None, :]
    same = (var[:, None] == (lane - 64) % 4) & (lane >= 64) & (lane < 76)
    doc = (lane >= 76) & (lane < 80)
    here = seg[:, None] == lane - 76
    keys = jnp.where(doc & ~here, FAR, jnp.where(same | ((lane >= 80) & (lane < 83)), 1.0, 0.0))
    queries = jnp.where(same | (doc & here), 1.0, 0.0)
    return queries.astype(jnp.bfloat16), keys.astype(jnp.bfloat16)


def head_scales(bias):
    hi, mid, lo = split3(bias[:, :1] - bias[:, 1:])
    lane = jnp.arange(128)[None, :]
    parts = jnp.where(lane < 68, hi, jnp.where(lane < 72, mid, lo))
    return jnp.where(lane < 64, 0.0, jnp.where(lane < 76, parts, jnp.where(lane < 80, 1.0, 0.0)))


def scale_of(x):
    return lax.rsqrt(jnp.mean(x * x, axis=-1, keepdims=True) + EPS)


def head_mean(x):
    row = lax.broadcasted_iota(jnp.int32, (128, 128), 0)
    col = lax.broadcasted_iota(jnp.int32, (128, 128), 1)
    group = jnp.where((row < 64) == (col < 64), 1.0 / HDIM, 0.0).astype(BF)
    hi = x.astype(BF)
    rest = x - hi.astype(F32)
    mid = rest.astype(BF)
    low = (rest - mid.astype(F32)).astype(BF)
    return dot(hi, group) + dot(mid, group) + dot(low, group)


def swap_halves(x):
    lane = lax.rem(lanes(x.shape[0]), 64)
    return jnp.where(lane < 32, pltpu.roll(x, 96, 1), pltpu.roll(x, 32, 1))


def norm_back_rows(u, r, gain, dy):
    scaled = dy * gain
    du = r * scaled - u * (r * r * r) * jnp.mean(scaled * u, axis=-1, keepdims=True)
    return du, jnp.sum(dy * u * r, axis=0, keepdims=True)


def as_blocks(value, shape):
    rows, cols = shape[-2:]
    if cols == value.shape[1]:
        return value.astype(BF).reshape(shape)
    depth = rows * cols // value.shape[1]
    parts = value.reshape(-1, depth, value.shape[1])
    parts = [parts[:, :, n:n + cols] for n in range(0, value.shape[1], cols)]
    return jnp.concatenate(parts, axis=1).astype(BF).reshape(shape)


def remote(src, dst, send, recv, device):
    return pltpu.make_async_remote_copy(
        src_ref=src, dst_ref=dst, send_sem=send, recv_sem=recv, device_id=device, device_id_type=MESH)


def local_copy(src, dst, sem):
    return pltpu.make_async_copy(src, dst, sem)


def wide_at(first):
    return pl.ds(pl.multiple_of(first, 256), 256)


class Rim:
    def __init__(self, ring):
        self.p, self.c, self.h = place()
        self.ring = ring
        self.has_low, self.has_high = self.c > 0, self.c < ring - 1
        self.low = lax.rem(self.c + ring - 1, ring)
        self.high = lax.rem(self.c + 1, ring)
        self.low_edge = self.has_low & (self.h == 0)
        self.high_edge = self.has_high & (self.h == 3)

    def greet(self):
        beyond = [(self.p, block, n) for block in (self.low, self.high) for n in range(4)]
        greet(group_peers(self.ring) + [(self.p, self.c, 3 - self.h)] + beyond)


def pair_at(first, pair):
    return pl.ds(pl.multiple_of(first + pair * 128, 128), 128)


LAGS = (2, (0, 1, 2, 3))
FIRST = LAGS[0] + LAGS[1][3]
EXTRA = 2
EVERY = 4


def as_matrix(value):
    rows, cols = value.shape[-2:]
    if cols == 512:
        return value.reshape(-1, 512)
    depth = rows * cols // 512
    parts = value.astype(F32).reshape(-1, rows, cols)
    parts = [parts[:, n:n + depth] for n in range(0, rows, depth)]
    return jnp.concatenate(parts, axis=2).reshape(-1, 512).astype(BF)


def attend_kernel(ring, n_wide, count, x_ref, cos_ref, sin_ref, hg_ref, kf_own, qf_ref, hs_ref, src, gain_src,
                  tok_ref, of_ref, qa_ref, kx, vx, kf_ref, raw_ref, gain_ref, wide, down,
                  rot, nrm, w_tile, gains, q_loc, o_loc, ka, va, tile_sem, local_sem, a2a_send, a2a_recv, rim_send, rim_recv,
                  kf_send, kf_recv, out_send, out_recv, *sems):
    p, c, h = place()
    rim = Rim(ring)
    greet(group_peers(ring) + [(p, c, 3 - h)])
    rows, width = tok_ref.shape
    group = 4 * rows
    mine = pl.ds(pl.multiple_of(h * rows, rows), rows)
    mine_x = pl.ds(pl.multiple_of(HALF + h * rows, rows), rows)
    places = ((0, q_loc, mine), (1, kx, mine_x), (2, vx, mine_x))
    three = pl.ds(0, 3 * rows)
    sides = ((rim.has_high, rim.high, group, 0), (rim.has_low, rim.low, HALF, HALF + group))

    small = Gather(ring, 1, lambda i, go: go(gain_src, lambda p, c, y, x: gains.at[p, c, y, x]), sems[:3])
    work = Gather(ring, count, gather_pick(src, wide, down, n_wide), sems[3:])

    def kf_copy(side):
        there, block, first, to = sides[side]
        return remote(kf_own.at[pl.ds(first - HALF * side if side else first - HALF, HALF)], kf_ref.at[pl.ds(to, HALF)],
                      kf_send.at[side], kf_recv.at[side], (p, block, h))

    def begin(t, carry):
        small.step(t, *LAGS)
        work.step(t, *LAGS)
        return carry
    lax.fori_loop(0, 2, begin, 0)
    for side in range(2):
        pl.when(sides[side][0])(lambda: kf_copy(side).start())
    kf_ref[HALF:HALF + group, :] = kf_own[...]
    lane = lax.broadcasted_iota(jnp.int32, (HALF, 128), 1)
    nothing = jnp.where((lane >= 76) & (lane < 80), FAR, 0.0).astype(BF)
    @pl.when(jnp.logical_not(rim.has_low))
    def _():
        kf_ref[0:HALF, :] = nothing
        for ref in (kx, vx):
            ref[0:HALF, :] = jnp.zeros((HALF, 256), BF)
    @pl.when(jnp.logical_not(rim.has_high))
    def _():
        kf_ref[HALF + group:2 * HALF + group, :] = nothing
        for ref in (kx, vx):
            ref[HALF + group:2 * HALF + group, :] = jnp.zeros((HALF, 256), BF)
    lax.fori_loop(2, FIRST, begin, 0)

    def share(kind, head, pair):
        ref, at = places[kind][1:]
        cols = pair_at(0, pair)
        part = rot.at[:, pair_at(kind * width + head * 256, pair)]
        there = ref.at[at, cols]
        @pl.when(head == h)
        def _():
            local_copy(part, there, local_sem.at[kind, pair]).start()
        @pl.when(head != h)
        def _():
            remote(part, there, a2a_send.at[kind, pair], a2a_recv.at[kind, pair], (p, c, head)).start()

    def tile_copy(t):
        return local_copy(wide.at[t], w_tile.at[lax.rem(t, 2)], tile_sem.at[lax.rem(t, 2)])

    for k in range(3):
        begin(FIRST + k, 0)
        for m in range(2):
            tile_copy(2 * k + m).start()
        if k == 0:
            total = gains[0, 0, 0, 0].astype(F32)
            for d in range(1, 8 * ring):
                total = total + gains[d // (4 * ring), d // 4 % ring, d // 2 % 2, d % 2].astype(F32)
            gain_ref[...] = total
            def norm(n, carry):
                at = pl.ds(pl.multiple_of(n * 128, 128), 128)
                x = x_ref[at, :].astype(F32)
                y = x * scale_of(x)
                for m in range(width // 128):
                    part = slice(m * 128, (m + 1) * 128)
                    nrm[at, part] = (y[:, part] * total[m:m + 1, :]).astype(BF)
                return carry
            lax.fori_loop(0, rows // 128, norm, 0)
        for m in range(2):
            t = 2 * k + m
            tile_copy(t).wait()
            def project(n, carry):
                at = pl.ds(pl.multiple_of(n * 128, 128), 128)
                raw = dot(nrm[at, :], as_matrix(w_tile[t % 2])).astype(BF)
                if t < 4:
                    raw_ref[at, t * 512:(t + 1) * 512] = raw
                    gain = hg_ref[t // 2:t // 2 + 1, :]
                    for m in range(4):
                        u = raw[:, m * 128:(m + 1) * 128].astype(F32)
                        y = u * lax.rsqrt(head_mean(u * u) + EPS) * gain
                        y = y * cos_ref[at, :] + swap_halves(y) * sin_ref[at, :]
                        rot[at, t * 512 + m * 128:t * 512 + (m + 1) * 128] = y.astype(BF)
                else:
                    rot[at, t * 512:(t + 1) * 512] = raw
                return carry
            lax.fori_loop(0, rows // 128, project, 0)
            for pair in range(2):
                for m2 in range(2):
                    share(t // 2, t % 2 * 2 + m2, pair)

    def rim_copy(ref, side, kind, pair):
        there, block, first, to = sides[side]
        return remote(ref.at[pl.ds(first, HALF), pair_at(0, pair)], ref.at[pl.ds(to, HALF), pair_at(0, pair)],
                      rim_send.at[side, kind, pair], rim_recv.at[side, kind, pair], (p, block, h))

    blocks = group // QB
    margin = HALF // QB
    def more(t, carry):
        work.step(t, *LAGS)
        return carry
    lax.fori_loop(FIRST + 3, FIRST + 3 + EXTRA, more, 0)
    def pair_step(pair, carry):
        cols = pair_at(0, pair)
        for kind, ref, at in places:
            local_copy(ref.at[at, cols], ref.at[at, cols], local_sem.at[kind, pair]).wait()
            local_copy(ref.at[three, cols], ref.at[three, cols], a2a_recv.at[kind, pair]).wait()
        for side in range(2):
            @pl.when(sides[side][0])
            def _():
                for kind, ref in ((0, kx), (1, vx)):
                    rim_copy(ref, side, kind, pair).start()
        build_keys(pair, kx, vx, kf_ref, ka, va, None, 1, 1 + group // HALF)
        def step(n, c):
            @pl.when(lax.rem(n, EVERY) == 0)
            def _():
                work.step(FIRST + 3 + EXTRA + (pair * blocks + n) // EVERY, *LAGS)
            forward_block(pair, lax.rem(n + margin, blocks), q_loc, qf_ref, hs_ref, ka, va, o_loc, of_ref, qa_ref)
            return c
        lax.fori_loop(0, blocks - 2 * margin, step, 0)
        for side in range(2):
            @pl.when(sides[1 - side][0])
            def _():
                for kind, ref in ((0, kx), (1, vx)):
                    rim_copy(ref, side, kind, pair).wait_recv()
                pl.when(pair == 0)(lambda: kf_copy(side).wait_recv())
        build_keys(pair, kx, vx, kf_ref, ka, va, None, 0, 1)
        build_keys(pair, kx, vx, kf_ref, ka, va, None, 1 + group // HALF, 2 + group // HALF)
        lax.fori_loop(blocks - 2 * margin, blocks, step, 0)
        to_cols = pair_at(h * 256, pair)
        local_copy(o_loc.at[mine, cols], tok_ref.at[:, to_cols], local_sem.at[3, pair]).start()
        for step_ in range(1, 4):
            to = lax.rem(h + step_, 4)
            theirs = pl.ds(pl.multiple_of(to * rows, rows), rows)
            remote(o_loc.at[theirs, cols], tok_ref.at[:, to_cols], out_send.at[pair], out_recv.at[pair], (p, c, to)).start()
        return carry
    lax.fori_loop(0, 2, pair_step, 0)

    done = FIRST + 3 + EXTRA + 2 * blocks // EVERY
    lax.fori_loop(done, max(done, work.steps(*LAGS)), more, 0)
    for pair in range(2):
        cols = pair_at(0, pair)
        local_copy(o_loc.at[mine, cols], tok_ref.at[:, pair_at(h * 256, pair)], local_sem.at[3, pair]).wait()
        part = tok_ref.at[:, pl.ds(0, 384)]
        local_copy(part, part, out_recv.at[pair]).wait()
        local_copy(part, part, out_send.at[pair]).wait()
        for kind, ref, at in places:
            local_copy(ref.at[three, cols], ref.at[three, cols], a2a_send.at[kind, pair]).wait()
        for side in range(2):
            @pl.when(sides[side][0])
            def _():
                for kind, ref in ((0, kx), (1, vx)):
                    rim_copy(ref, side, kind, pair).wait_send()
                if pair == 0:
                    kf_copy(side).wait_send()
    small.drain_all()
    work.drain_all()


def attend(x, cosine, sine, head_gains, kf, qf, hs, src, gain_src, n_wide, ring, collective_id):
    rows, width = x.shape
    group = 4 * rows
    ext = group + 2 * HALF
    count, r, w = src.shape
    dma = pltpu.SemaphoreType.DMA
    return pl.pallas_call(
        functools.partial(attend_kernel, ring, n_wide, count),
        out_shape=(
            jax.ShapeDtypeStruct((rows, width), BF),
            jax.ShapeDtypeStruct((group, 256), F32),
            jax.ShapeDtypeStruct((4, group, 128), BF),
            jax.ShapeDtypeStruct((ext, 256), BF),
            jax.ShapeDtypeStruct((ext, 256), BF),
            jax.ShapeDtypeStruct((ext, 128), BF),
            jax.ShapeDtypeStruct((rows, 2 * width), BF),
            jax.ShapeDtypeStruct((16, 128), F32),
            jax.ShapeDtypeStruct((n_wide, 2, ring, 2, 2, r, w), BF),
            jax.ShapeDtypeStruct((2, ring, 2, 2, (count - n_wide) // 2, r, 2 * w), BF),
        ),
        in_specs=[VM] * 7 + [ANY, ANY],
        out_specs=(VM,) * 8 + (ANY, ANY),
        scratch_shapes=[
            pltpu.VMEM((rows, 3 * width), BF), pltpu.VMEM((rows, width), BF), pltpu.VMEM((2, 2, ring, 2, 2, r, w), BF),
            pltpu.VMEM((2, ring, 2, 2, 16, 128), BF),
            pltpu.VMEM((group, 256), BF), pltpu.VMEM((group, 256), BF),
            pltpu.VMEM((2, ext, 128), BF), pltpu.VMEM((2, ext, 128), BF),
            dma((2,)), dma((4, 2)), dma((3, 2)), dma((3, 2)), dma((2, 2, 2)), dma((2, 2, 2)), dma((2,)), dma((2,)), dma((2,)), dma((2,)),
        ] + gather_sems(1) + gather_sems(count),
        compiler_params=pltpu.CompilerParams(collective_id=collective_id, has_side_effects=True, vmem_limit_bytes=60 * MIB),
        name="attend",
    )(x, cosine, sine, head_gains, kf, qf, hs, src, gain_src)


BACK_LAGS = (1, (0, 1, 2, 3))
BACK_EVERY = 1


def down_blocks(value, shape):
    rows, cols = shape[-2:]
    if cols == value.shape[1]:
        return value.astype(BF).reshape(shape)
    depth = rows * cols // value.shape[1]
    parts = value.reshape(-1, depth, value.shape[1])
    parts = [parts[:, :, n:n + cols] for n in range(0, value.shape[1], cols)]
    return jnp.concatenate(parts, axis=1).astype(BF).reshape(shape)


def feed_phase(work, heads_hbm, cot_hbm, x_hbm, gain, wide, down, g_gu, g_go, g_gd, out_hbm, dhid_hbm, d_tok, gffn_ref,
               back, hidden, acc, dnorm, nrm_t, w_gu, w_d, stage, stage_d, in_sem, w_sem, stage_sem, out_sem):
    tiles = down.shape[0] // 512
    width = back.shape[1] // 3
    heads, cot, nrm = (back.at[:, n * width:(n + 1) * width] for n in range(3))
    spots = g_gd.shape[1] * g_gd.shape[0] // tiles

    def weights(t, slot):
        return [local_copy(wide.at[8 + t], w_gu.at[slot, 0], w_sem.at[slot, 0]),
                local_copy(wide.at[16 + t], w_gu.at[slot, 1], w_sem.at[slot, 1]),
                local_copy(down.at[pl.ds(pl.multiple_of(t * 512, 512), 512)], w_d.at[slot], w_sem.at[slot, 2])]

    def out_weight(slot):
        return [local_copy(wide.at[6 + n], w_gu.at[slot, n], w_sem.at[slot, n]) for n in range(2)]

    def staged(t):
        per = g_gd.shape[1] // spots
        return [local_copy(stage.at[0], g_gu.at[2 * t], stage_sem.at[0]),
                local_copy(stage.at[1], g_gu.at[2 * t + 1], stage_sem.at[1]),
                local_copy(stage_d, g_gd.at[t // per, pl.ds(lax.rem(t, per) * spots, spots)], stage_sem.at[2])]

    first = [local_copy(heads_hbm, heads, in_sem.at[0]), local_copy(cot_hbm, cot, in_sem.at[1]),
             local_copy(x_hbm, w_d.at[1], in_sem.at[2])] + out_weight(1)
    for copy in first + weights(0, 0):
        copy.start()
    for copy in first:
        copy.wait()
    for n in range(2):
        at = slice(n * 512, (n + 1) * 512)
        hidden[:, at] = w_d[1, :, at].astype(F32) + dot(heads[...], w_gu[1, n])
    def normalise(n, carry):
        at = pl.ds(pl.multiple_of(n * 128, 128), 128)
        h = hidden[at, :]
        y = h * scale_of(h) * gain
        nrm[at, :] = y.astype(BF)
        nrm_t[:, at] = y.T.astype(BF)
        acc[at, :] = h
        dnorm[at, :] = jnp.zeros_like(h)
        return carry
    lax.fori_loop(0, 4, normalise, 0)

    def tile(t, carry):
        slot = lax.rem(t, 2)
        for copy in weights(t, slot):
            copy.wait()
        @pl.when(t < tiles - 1)
        def _():
            for copy in weights(t + 1, 1 - slot):
                copy.start()
        @pl.when(t == tiles - 1)
        def _():
            for copy in out_weight(tiles % 2):
                copy.start()
        normed = nrm[...]
        wg, wu, wd = w_gu[slot, 0], w_gu[slot, 1], w_d[slot]
        gate = dot(normed, wg)
        up = dot(normed, wu)
        d_product = dot_tb(cot[...], wd)
        sig = jax.nn.sigmoid(gate)
        silu = gate * sig
        product = silu * up
        prod_b = product.astype(BF)
        d_gate = (d_product * up * sig * (1.0 + gate * (1.0 - sig))).astype(BF)
        d_up = (d_product * silu).astype(BF)
        acc[...] += dot(prod_b, wd)
        dnorm[...] += dot_tb(d_gate, wg) + dot_tb(d_up, wu)
        @pl.when(t > 0)
        def _():
            for copy in staged(t - 1):
                copy.wait()
            work.step(t - 1, *BACK_LAGS)
        stage[0] = as_blocks(dot(nrm_t[...], d_gate), stage.shape[1:])
        stage[1] = as_blocks(dot(nrm_t[...], d_up), stage.shape[1:])
        stage_d[...] = down_blocks(dot(product.T.astype(BF), cot[...]), stage_d.shape)
        for copy in staged(t):
            copy.start()
        return carry
    lax.fori_loop(0, tiles, tile, 0)
    for copy in staged(tiles - 1):
        copy.wait()
    work.step(tiles - 1, *BACK_LAGS)

    def finish(n, carry):
        at = pl.ds(pl.multiple_of(n * 128, 128), 128)
        h = hidden[at, :]
        du, terms = norm_back_rows(h, scale_of(h), gain, dnorm[at, :])
        d_hidden = cot[at, :].astype(F32) + du
        hidden[at, :] = d_hidden
        nrm[at, :] = d_hidden.astype(BF)
        heads_t = heads[at, :].astype(F32).T.astype(BF)
        nrm_t[:, at] = heads_t
        cot[at, :] = acc[at, :].astype(BF)
        return carry + terms
    gffn_ref[...] = lax.fori_loop(0, 4, finish, jnp.zeros(gffn_ref.shape, F32))
    last = [local_copy(cot, out_hbm, out_sem.at[0]), local_copy(hidden, dhid_hbm, out_sem.at[1])]
    for copy in last:
        copy.start()
    for copy in out_weight(tiles % 2):
        copy.wait()
    d_attn = nrm[...]
    total = jnp.zeros(hidden.shape, F32)
    for n in range(2):
        at = slice(n * 512, (n + 1) * 512)
        total = total + dot_tb(d_attn[:, at], w_gu[tiles % 2, n])
    d_tok[...] = total.astype(BF)
    for n in range(2):
        at = slice(n * 512, (n + 1) * 512)
        stage[n] = as_blocks(dot(nrm_t[...], d_attn[:, at]), stage.shape[1:])
        copy = local_copy(stage.at[n], g_go.at[n], stage_sem.at[n])
        copy.start()
    for n in range(2):
        local_copy(stage.at[n], g_go.at[n], stage_sem.at[n]).wait()
    for copy in last:
        copy.wait()


def score_phase(work, first_step, ring, d_tok, kx_hbm, vx_hbm, kf_ref, qf_ref, qa_hbm, of_hbm, do_loc, rims, back, same, every,
                kx, vx, qa, of, dq_loc, dk_loc, dv_loc, ka, va, kt, dka, dva,
                load_sem, local_sem, in_send, in_recv, back_send, back_recv, rim_send, rim_recv):
    p, c, h = place()
    rim = Rim(ring)
    rows, width = d_tok.shape
    group = 4 * rows
    mine = pl.ds(pl.multiple_of(h * rows, rows), rows)
    three = pl.ds(0, 3 * rows)
    for pair in range(2):
        cols = pair_at(0, pair)
        local_copy(d_tok.at[:, pair_at(h * 256, pair)], do_loc.at[mine, cols], local_sem.at[0, pair]).start()
        for step in range(1, 4):
            to = lax.rem(h + step, 4)
            remote(d_tok.at[:, pair_at(to * 256, pair)], do_loc.at[mine, cols], in_send.at[pair], in_recv.at[pair], (p, c, to)).start()
    same[...] = jnp.zeros_like(same)
    every[...] = jnp.zeros_like(every)

    trios = ((0, dq_loc, 0), (1, dk_loc, HALF), (2, dv_loc, HALF))
    kinds = ((0, dk_loc), (1, dv_loc))
    sides = ((rim.has_high, rim.high, HALF + group), (rim.has_low, rim.low, 0))

    def rim_copy(ref, side, kind, pair):
        there, block, first = sides[side]
        cols = pair_at(0, pair)
        return remote(ref.at[pl.ds(first, HALF), cols], rims.at[side, kind, :, cols],
                      rim_send.at[side, kind, pair], rim_recv.at[side, kind, pair], (p, block, h))

    def give(kind, pair, wanted):
        _, ref, skip = trios[kind]
        cols, at = pair_at(0, pair), pair_at(kind * width + h * 256, pair)
        for step in range(4):
            to = lax.rem(h + step, 4)
            theirs = ref.at[pl.ds(pl.multiple_of(skip + to * rows, rows), rows), cols]
            def go():
                if step == 0:
                    local_copy(theirs, back.at[:, at], local_sem.at[1 + kind, pair]).start()
                else:
                    remote(theirs, back.at[:, at], back_send.at[kind, pair], back_recv.at[kind, pair], (p, c, to)).start()
            if wanted is None:
                go()
            else:
                edge = (to == 0) | (to == 3)
                pl.when(edge if wanted else jnp.logical_not(edge))(go)

    def edges_back(pair):
        cols = pair_at(0, pair)
        for side in range(2):
            first = HALF if side == 0 else group
            @pl.when(sides[1 - side][0])
            def _():
                for kind, ref in kinds:
                    rim_copy(ref, side, kind, pair).wait_recv()
                    for m in range(4):
                        to = pl.ds(first + m * 128, 128)
                        more = rims[side, kind, pl.ds(m * 128, 128), cols].astype(F32)
                        ref[to, cols] = (ref[to, cols].astype(F32) + more).astype(BF)
        give(1, pair, True)
        give(2, pair, True)

    blocks = group // QB
    def pair_step(pair, carry):
        cols = pair_at(0, pair)
        loads = [local_copy(kx_hbm.at[:, cols], kx, load_sem.at[0]), local_copy(vx_hbm.at[:, cols], vx, load_sem.at[1]),
                 local_copy(qa_hbm.at[pl.ds(pair * 2, 2)], qa, load_sem.at[2]), local_copy(of_hbm.at[:, cols], of, load_sem.at[3])]
        for copy in loads:
            copy.start()
        dka[...] = jnp.zeros_like(dka)
        dva[...] = jnp.zeros_like(dva)
        for copy in loads:
            copy.wait()
        build_keys(0, kx, vx, kf_ref, ka, va, kt)
        local_copy(do_loc.at[mine, cols], do_loc.at[mine, cols], local_sem.at[0, pair]).wait()
        local_copy(do_loc.at[three, cols], do_loc.at[three, cols], in_recv.at[pair]).wait()
        def step(m, c):
            @pl.when(lax.rem(m, BACK_EVERY) == 0)
            def _():
                work.step(first_step + (pair * blocks + m) // BACK_EVERY, *BACK_LAGS)
            backward_block(pair, m, qf_ref, qa, do_loc, of, ka, va, kt, dka, dva, dq_loc, same, every)
            return c
        lax.fori_loop(0, blocks // 2, step, 0)
        pl.when(pair == 1)(lambda: edges_back(0))
        lax.fori_loop(blocks // 2, blocks, step, 0)
        backward_finish(pair, dka, dva, dk_loc, dv_loc)
        for side in range(2):
            @pl.when(sides[side][0])
            def _():
                for kind, ref in kinds:
                    rim_copy(ref, side, kind, pair).start()
        give(1, pair, False)
        give(2, pair, False)
        give(0, pair, None)
        return carry
    lax.fori_loop(0, 2, pair_step, 0)
    edges_back(1)
    done = first_step + 2 * blocks // BACK_EVERY
    def more(t, carry):
        work.step(t, *BACK_LAGS)
        return carry
    lax.fori_loop(done, max(done, work.steps(*BACK_LAGS)), more, 0)
    work.drain_all()

    part = back.at[:, pl.ds(0, 384)]
    for pair in range(2):
        cols = pair_at(0, pair)
        for kind in range(3):
            at = pair_at(kind * width + h * 256, pair)
            local_copy(back.at[:, at], back.at[:, at], local_sem.at[1 + kind, pair]).wait()
            local_copy(part, part, back_recv.at[kind, pair]).wait()
            local_copy(part, part, back_send.at[kind, pair]).wait()
        local_copy(do_loc.at[three, cols], do_loc.at[three, cols], in_send.at[pair]).wait()
        for side in range(2):
            @pl.when(sides[side][0])
            def _():
                for kind, ref in kinds:
                    rim_copy(ref, side, kind, pair).wait_send()


def unproject_phase(work, x_hbm, gain, wide, raw_hbm, cos_ref, sin_ref, hg_ref, dhid_hbm, back, g_qkv, gin_hbm, gattn_ref, ghead_ref,
                    before, x, nrm_t, dnorm, w, raw, stage, dhid, in_sem, w_sem, stage_sem):
    def tile_copies(t, slot):
        copies = [local_copy(wide.at[t], w.at[slot], w_sem.at[slot, 0])]
        if t < 4:
            copies.append(local_copy(raw_hbm.at[:, t * 512:(t + 1) * 512], raw.at[slot], w_sem.at[slot, 1]))
        return copies
    late = local_copy(dhid_hbm, dhid, in_sem.at[1])
    load = local_copy(x_hbm, x, in_sem.at[0])
    load.start()
    late.start()
    for copy in tile_copies(0, 0):
        copy.start()
    load.wait()
    def normalise(n, carry):
        at = pl.ds(pl.multiple_of(n * 128, 128), 128)
        u = x[at, :].astype(F32)
        nrm_t[:, at] = (u * scale_of(u) * gain).T.astype(BF)
        return carry
    lax.fori_loop(0, 4, normalise, 0)
    before()
    ghead_ref[...] = jnp.zeros_like(ghead_ref)
    for t in range(6):
        slot = t % 2
        if t < 5:
            for copy in tile_copies(t + 1, 1 - slot):
                copy.start()
        for copy in tile_copies(t, slot):
            copy.wait()
        if t < 4:
            kind = t // 2
            head_gain = hg_ref[kind:kind + 1, :]
            def unrotate(n, carry):
                at = pl.ds(pl.multiple_of(n * 128, 128), 128)
                for m in range(4):
                    part = slice(m * 128, (m + 1) * 128)
                    wide_part = slice(t * 512 + m * 128, t * 512 + (m + 1) * 128)
                    u = raw[slot, at, part].astype(F32)
                    dy = back[at, wide_part].astype(F32)
                    dy = dy * cos_ref[at, :] - swap_halves(dy) * sin_ref[at, :]
                    r = lax.rsqrt(head_mean(u * u) + EPS)
                    scaled = dy * head_gain
                    back[at, wide_part] = (r * scaled - u * (r * r * r) * head_mean(scaled * u)).astype(BF)
                    ghead_ref[kind:kind + 1, :] += jnp.sum(dy * u * r, axis=0, keepdims=True)
                return carry
            lax.fori_loop(0, 4, unrotate, 0)
        d_proj = back[:, t * 512:(t + 1) * 512]
        stage[slot] = as_blocks(dot(nrm_t[...], d_proj), stage.shape[1:])
        copy = local_copy(stage.at[slot], g_qkv.at[t], stage_sem.at[slot])
        copy.start()
        part = dot_tb(d_proj, w[slot])
        if t == 0:
            dnorm[...] = part
        else:
            dnorm[...] += part
        copy.wait()
        if t % 2:
            work.step(t // 2, *BACK_LAGS)
    late.wait()
    def finish(n, carry):
        at = pl.ds(pl.multiple_of(n * 128, 128), 128)
        u = x[at, :].astype(F32)
        du, terms = norm_back_rows(u, scale_of(u), gain, dnorm[at, :])
        dhid[at, :] = dhid[at, :] + du
        return carry + terms
    gattn_ref[...] = lax.fori_loop(0, 4, finish, jnp.zeros(gattn_ref.shape, F32))
    copy = local_copy(dhid, gin_hbm, in_sem.at[1])
    copy.start()
    copy.wait()


def train_kernel(ring, x, heads, cot, gains, wide, down, kx, vx, kf, qf, qa, of, raw, cos_ref, sin_ref, hg_ref,
                 out, gin, sums, small_out, dhid, g_gu, g_go, g_gd, g_qkv,
                 d_tok, do_loc, rims, back, same, every, gffn, gattn, ghead,
                 small, came, far, small_send, small_recv, credit,
                 local_sem, in_send, in_recv, back_send, back_recv, rim_send, rim_recv, *buffers):
    p, c, h = place()
    peers = group_peers(ring)
    greet(peers + [(p, c, 3 - h)])
    rows, width = d_tok.shape
    group, ext = 4 * rows, 4 * rows + 2 * HALF
    r, w = sums.shape[-2:]
    block = (2, ring, 2, 2, r, w)
    bufs, sems = buffers[:5], buffers[5:]
    dma = pltpu.SemaphoreType.DMA
    count = 26

    def write(i, total):
        sums[i] = total

    def write_last(i, total):
        sums[count + i] = total

    work = Scatter(ring, count, scatter_pick((g_gu, g_go, g_gd), ((16, True), (2, True), (8, False)), w), bufs, sems, sums, write)
    last = Scatter(ring, 6, scatter_pick((g_qkv,), ((6, True),), w), bufs, sems, sums, write_last)
    vm = pltpu.VMEM
    tiles = down.shape[0] // 512
    spots = g_gd.shape[0] * g_gd.shape[1] // tiles

    pl.run_scoped(
        functools.partial(feed_phase, work, heads, cot, x, gains[1], wide, down, g_gu, g_go, g_gd, out, dhid, d_tok, gffn, back),
        vm((rows, width), F32), vm((rows, width), F32), vm((rows, width), F32), vm((width, rows), BF), vm((2, 2, width, 512), BF), vm((2, 512, width), BF),
        vm((2,) + block, BF), vm((spots,) + g_gd.shape[2:], BF), dma((3,)), dma((2, 3)), dma((3,)), dma((2,)))
    def score(kx_p, vx_p, qa_p, of_p, dq_loc, dk_loc, dv_loc, ka, va, kt, dka, dva, load_sem):
        score_phase(work, tiles, ring, d_tok, kx, vx, kf, qf, qa, of, do_loc, rims, back, same, every,
                    kx_p, vx_p, qa_p, of_p, dq_loc, dk_loc, dv_loc, ka, va, kt, dka, dva,
                    load_sem, local_sem, in_send, in_recv, back_send, back_recv, rim_send, rim_recv)

    pl.run_scoped(
        score,
        vm((ext, 128), BF), vm((ext, 128), BF), vm((2, group, 128), BF), vm((group, 128), F32),
        vm((group, 256), BF), vm((ext, 256), BF), vm((ext, 256), BF),
        vm((2, ext, 128), BF), vm((2, ext, 128), BF), vm((2, 128, ext), BF), vm((2, ext, 128), F32), vm((2, ext, 128), F32),
        dma((4,)))
    for peer in peers:
        pl.semaphore_signal(credit, inc=1, device_id=peer, device_id_type=MESH)
    pl.run_scoped(
        functools.partial(unproject_phase, last, x, gains[0], wide, raw, cos_ref, sin_ref, hg_ref, dhid, back, g_qkv, gin, gattn, ghead,
                          lambda: pl.semaphore_wait(credit, len(peers))),
        vm((rows, width), BF), vm((width, rows), BF), vm((rows, width), F32), vm((2, width, 512), BF), vm((2, rows, 512), BF),
        vm((2,) + block, BF), vm((rows, width), F32), dma((2,)), dma((2, 2)), dma((2,)))

    def total_of(value):
        return jnp.sum(jnp.sum(value, axis=1, keepdims=True), axis=2, keepdims=True)
    s, e = total_of(same[...]), total_of(every[...])
    lane = lax.broadcasted_iota(jnp.int32, (1, 128), 1)
    bias = jnp.zeros((1, 128), F32)
    for m in range(4):
        bias = jnp.where(lane == h * 8 + 2 * m, s[m], jnp.where(lane == h * 8 + 2 * m + 1, e[m] - s[m], bias))
    for n in range(8):
        at = slice(n * 128, (n + 1) * 128)
        small[0, n:n + 1, :] = gattn[:, at]
        small[0, 8 + n:9 + n, :] = gffn[:, at]
    small[0, 16:18, :] = ghead[...]
    small[0, 18:19, :] = bias
    small[0, 19:24, :] = jnp.zeros((5, 128), F32)
    hops = (last.core, last.xpeer, last.ypeer)

    def hop(n):
        return remote(small.at[n], came.at[n], small_send.at[n], small_recv.at[n], hops[n])

    hop(0).start()
    def rest(t, carry):
        last.step(t, *BACK_LAGS)
        for n in range(3):
            @pl.when(t == 3 + n)
            def _():
                hop(n).wait_recv()
                small[n + 1] = small[n] + came[n]
                if n < 2:
                    hop(n + 1).start()
                else:
                    for step in range(1, ring):
                        remote(small.at[3], far.at[step - 1], small_send.at[3], small_recv.at[3], (p, lax.rem(c + step, ring), h)).start()
        return carry
    lax.fori_loop(3, last.steps(*BACK_LAGS), rest, 0)
    local_copy(far, far, small_recv.at[3]).wait()
    total = small[3]
    for step in range(1, ring):
        total = total + far[step - 1]
    small_out[...] = total
    for n in range(3):
        hop(n).wait_send()
    local_copy(far, far, small_send.at[3]).wait()
    last.drain_all()


def train(x, heads, cot, gains, wide, down, kx, vx, kf, qf, qa, of, raw, cosine, sine, head_gains, ring, item, collective_id):
    rows, width = x.shape
    group, ext = 4 * rows, 4 * rows + 2 * HALF
    r, w = item
    block = (2, ring, 2, 2, r, w)
    dma = pltpu.SemaphoreType.DMA
    vm = pltpu.VMEM
    shape = jax.ShapeDtypeStruct
    return pl.pallas_call(
        functools.partial(train_kernel, ring),
        out_shape=(
            shape((rows, width), BF), shape((rows, width), F32), shape((32, r, w), F32), shape((24, 128), F32),
            shape((rows, width), F32), shape((16,) + block, BF), shape((2,) + block, BF),
            shape((2, ring, 2, 2, 4, r, 2 * w), BF), shape((6,) + block, BF)),
        in_specs=[ANY] * 3 + [VM] + [ANY] * 4 + [VM] * 2 + [ANY] * 3 + [VM] * 3,
        out_specs=(ANY, ANY, VM, VM) + (ANY,) * 5,
        scratch_shapes=[
            vm((rows, width), BF), vm((group, 256), BF), vm((2, 2, HALF, 256), BF), vm((rows, 3 * width), BF),
            vm((4, 8, QB), F32), vm((4, 8, QB), F32), vm((1, width), F32), vm((1, width), F32), vm((2, 128), F32),
            vm((4, 24, 128), F32), vm((3, 24, 128), F32), vm((ring - 1, 24, 128), F32), dma((4,)), dma((4,)),
            pltpu.SemaphoreType.REGULAR,
            dma((4, 2)), dma((2,)), dma((2,)), dma((3, 2)), dma((3, 2)), dma((2, 2, 2)), dma((2, 2, 2)),
        ] + scatter_scratch(ring, 26, r, w),
        compiler_params=pltpu.CompilerParams(collective_id=collective_id, has_side_effects=True, vmem_limit_bytes=63 * MIB),
        name="train",
    )(x, heads, cot, gains, wide, down, kx, vx, kf, qf, qa, of, raw, cosine, sine, head_gains)


def to_blocks(weight, depth, r, w):
    parts = weight.reshape(-1, depth, weight.shape[1] // 512, r // depth, w)
    return parts.transpose(2, 0, 3, 1, 4).reshape(weight.shape[1] // 512, -1, r, w)


def from_blocks(blocks, depth):
    n, (r, w) = blocks.shape[0], blocks.shape[-2:]
    return blocks.reshape(n, -1, r // depth, depth, w).swapaxes(2, 3).reshape(n, -1, 512)


def local(
    inputs, cotangent, w_qkv, w_out, w_gate, w_up, w_down, gain_attn, gain_ffn, q_gain, k_gain, head_bias,
    segment_ids, variate_ids, time_index,
):
    ring = lax.axis_size("cp")
    head = lax.axis_index("hd")
    rows, width = inputs.shape
    depth = w_qkv.shape[0]
    r, w = item_shape(depth)

    me = (lax.axis_index("pack") * ring + lax.axis_index("cp")) * 4 + head
    down_pieces = w_down.reshape(4, r, 2, w).swapaxes(1, 2).reshape(8, r, w)
    src = jnp.concatenate([to_blocks(weight, depth, r, w)[:, 0] for weight in (w_qkv, w_out, w_gate, w_up)] + [down_pieces])
    gain_src = lax.dynamic_update_slice(jnp.zeros((2, width), BF), jnp.stack([gain_attn, gain_ffn]), (0, me * depth))
    gain_src = gain_src.reshape(16, 128)

    times = lax.dynamic_slice_in_dim(time_index, head * rows, rows, 0)
    lane = jnp.arange(128)
    frequency = jnp.exp(-math.log(theta_base) * 2.0 * (lane % 32).astype(F32) / HDIM)
    angle = times.astype(F32)[:, None] * frequency[None, :]
    cosine = jnp.cos(angle)
    sine = jnp.sin(angle) * jnp.where(lane % 64 < 32, -1.0, 1.0)[None, :]
    head_gains = jnp.stack([jnp.concatenate([q_gain, q_gain]), jnp.concatenate([k_gain, k_gain])])

    qf, kf_own = features(segment_ids, variate_ids)
    hs = head_scales(lax.dynamic_slice_in_dim(head_bias, head * 4, 4, 0))

    heads_out, of, qa, kx, vx, kf, raw, gains, wide, down = attend(
        inputs, cosine, sine, head_gains, kf_own, qf, hs, src, gain_src, 24, ring, 1)
    wide = from_blocks(wide, depth)
    gains = gains.reshape(2, 1, width)
    layer_out, grad_inputs, items, small, *_ = train(
        inputs, heads_out, cotangent, gains, wide, down.reshape(-1, width), kx, vx, kf, qf, qa, of, raw,
        cosine, sine, head_gains, ring, (r, w), 2)

    def columns(part):
        return from_blocks(part, depth).swapaxes(0, 1).reshape(depth, -1)

    pairs = items[:16].reshape(8, 2, r, w)
    down_depth = w_down.shape[0] // 4
    own_down = items[18:26].reshape(4, 2, r // down_depth, down_depth, w).transpose(0, 3, 2, 1, 4).reshape(w_down.shape)
    own_gains = lax.dynamic_slice_in_dim(small[:16].reshape(2, width), me * depth, depth, 1)
    own_heads = small[16:18, :HDIM] + small[16:18, HDIM:]
    return (
        layer_out, grad_inputs, columns(items[26:]), columns(items[16:18]), columns(pairs[:, 0]), columns(pairs[:, 1]),
        own_down, own_gains[0], own_gains[1], own_heads[0], own_heads[1], small[18, :32].reshape(HEADS, 2),
    )


def solution(mesh):
    return jax.shard_map(
        local,
        mesh=mesh,
        in_specs=(
            P(("pack", "cp", "hd"), None),
            P(("pack", "cp", "hd"), None),
            P(("pack", "cp", "hd"), None),
            P(("pack", "cp", "hd"), None),
            P(("pack", "cp", "hd"), None),
            P(("pack", "cp", "hd"), None),
            P(("pack", "cp", "hd"), None),
            P(("pack", "cp", "hd")),
            P(("pack", "cp", "hd")),
            P(),
            P(),
            P(),
            P(("pack", "cp")),
            P(("pack", "cp")),
            P(("pack", "cp")),
        ),
        out_specs=(
            P(("pack", "cp", "hd"), None),
            P(("pack", "cp", "hd"), None),
            P(("pack", "cp", "hd"), None),
            P(("pack", "cp", "hd"), None),
            P(("pack", "cp", "hd"), None),
            P(("pack", "cp", "hd"), None),
            P(("pack", "cp", "hd"), None),
            P(("pack", "cp", "hd")),
            P(("pack", "cp", "hd")),
            P(),
            P(),
            P(),
        ),
        check_vma=False,
    )
```

```python
import functools
import math

import jax
import jax.numpy as jnp
from jax import lax
from jax.experimental import pallas as pl
from jax.experimental.pallas import tpu as pltpu
from jax.sharding import PartitionSpec as P

HEADS = 16
HDIM = 64
HALF = 512
QB = 256
SPAN = QB + 2 * HALF
FAR = -1e30
EPS = 1e-6
theta_base = 10000.0
MIB = 2**20
F32, BF = jnp.float32, jnp.bfloat16
MESH = pl.DeviceIdType.MESH
VM = pl.BlockSpec(memory_space=pltpu.VMEM)
ANY = pl.BlockSpec(memory_space=pl.ANY)
ALL = slice(None)


def item_shape(rows):
    full = max(rows, 16)
    return full, rows * 512 // full


def place():
    return lax.axis_index("pack"), lax.axis_index("cp"), lax.axis_index("hd")


def greet(peers):
    barrier = pltpu.get_barrier_semaphore()
    for peer in peers:
        pl.semaphore_signal(barrier, inc=1, device_id=peer, device_id_type=MESH)
    pl.semaphore_wait(barrier, len(peers))


def group_peers(ring):
    p, c, h = place()
    peers = [(1 - p, c, h), (p, c, h + 1 - 2 * lax.rem(h, 2)), (p, c, lax.rem(h + 2, 4))]
    peers += [(p, lax.rem(c + step, ring), h) for step in range(1, ring)]
    return peers


class Scatter:
    def __init__(self, ring, count, middle, pick, buffers, sems, write):
        self.ring, self.count, self.middle, self.pick, self.write = ring, count, middle, pick, write
        self.load, self.own, self.b1, self.tail = buffers
        self.slots = self.load.shape[0]
        self.load_sem, self.send_sem, self.recv_sem = sems
        self.p, self.c, self.h = place()
        self.hy, self.hx = self.h // 2, lax.rem(self.h, 2)
        self.core = (1 - self.p, self.c, self.h)
        self.xpeer = (self.p, self.c, self.hy * 2 + 1 - self.hx)
        self.ypeer = (self.p, self.c, (1 - self.hy) * 2 + self.hx)

    def remote(self, i, stage, src, dst, device):
        return pltpu.make_async_remote_copy(
            src_ref=src, dst_ref=dst, send_sem=self.send_sem.at[stage, i],
            recv_sem=self.recv_sem.at[stage, i], device_id=device, device_id_type=MESH)

    def wait_for(self, ref, sem):
        pltpu.make_async_copy(ref, ref, sem).wait()

    def near(self, first_y):
        return self.ypeer if first_y else self.xpeer

    def spot(self, i, first_y, k):
        return (i, self.hy, k) if first_y else (i, k, self.hx)

    def copy0(self, i, src):
        return self.remote(i, 0, src, self.own.at[i], self.core)

    def copy1(self, i, first_y):
        src = self.own.at[i, :, 1 - self.hy] if first_y else self.own.at[i, :, :, 1 - self.hx]
        return self.remote(i, 1, src, self.b1.at[i], self.near(first_y))

    def half(self, i, first_y):
        return self.own.at[i, :, self.hy, 1 - self.hx] if first_y else self.own.at[i, :, 1 - self.hy, self.hx]

    def begin(self, i, first_y, mid):
        def go(mine, other):
            slot = lax.rem(i, self.slots)
            pltpu.make_async_copy(mine, self.load.at[slot], self.load_sem.at[slot]).start()
            self.copy0(i, other).start()
        self.pick(i, self.p, go)

    def stage1(self, i, first_y, mid):
        slot = lax.rem(i, self.slots)
        self.wait_for(self.load.at[slot], self.load_sem.at[slot])
        self.copy0(i, self.own.at[i]).wait_recv()
        def add(k, carry):
            self.own[i, k] = self.own[i, k] + self.load[slot, k]
            return carry
        lax.fori_loop(0, self.ring, add, 0)
        self.copy1(i, first_y).start()

    def stage2(self, i, first_y, mid):
        self.copy1(i, first_y).wait_recv()
        def add(k, carry):
            for m in range(2):
                at = (i, k, self.hy, m) if first_y else (i, k, m, self.hx)
                self.own[at] = self.own[at] + self.b1[i, k, m]
            return carry
        lax.fori_loop(0, self.ring, add, 0)
        if not mid:
            self.remote(i, 2, self.half(i, first_y), self.tail.at[i, pl.ds(0, self.ring)], self.near(not first_y)).start()
            return
        for step in range(1, self.ring):
            peer = lax.rem(self.c + step, self.ring)
            src = self.own.at[i, peer, self.hy] if first_y else self.own.at[i, peer, :, self.hx]
            self.remote(i, 2, src, self.tail.at[i, pl.ds(2 * step - 2, 2)], (self.p, peer, self.h)).start()

    def second(self, i, mid):
        return self.tail.at[i, pl.ds(0, 2 * self.ring - 2 if mid else self.ring)]

    def third(self, i, mid):
        return self.tail.at[i, pl.ds(2 * self.ring - 2, 1) if mid else pl.ds(self.ring, self.ring - 1)]

    def stage3(self, i, first_y, mid):
        self.wait_for(self.second(i, mid), self.recv_sem.at[2, i])
        if mid:
            for k in range(2):
                at = (i, self.c, self.hy, k) if first_y else (i, self.c, k, self.hx)
                total = self.own[at].astype(jnp.float32)
                for step in range(1, self.ring):
                    total = total + self.tail[i, 2 * step - 2 + k].astype(jnp.float32)
                self.own[at] = total.astype(jnp.bfloat16)
            last = (self.hy, pl.ds(1 - self.hx, 1)) if first_y else (pl.ds(1 - self.hy, 1), self.hx)
            self.remote(i, 3, self.own.at[(i, self.c) + last], self.third(i, mid), self.near(not first_y)).start()
            return
        def add(k, carry):
            at = (i, k, self.hy, self.hx)
            self.own[at] = self.own[at] + self.tail[i, k]
            return carry
        lax.fori_loop(0, self.ring, add, 0)
        for step in range(1, self.ring):
            peer = lax.rem(self.c + step, self.ring)
            self.remote(i, 3, self.own.at[i, peer, self.hy, self.hx], self.tail.at[i, self.ring + step - 1], (self.p, peer, self.h)).start()

    def finish(self, i, first_y, mid):
        self.wait_for(self.third(i, mid), self.recv_sem.at[3, i])
        total = self.own[i, self.c, self.hy, self.hx].astype(jnp.float32)
        for n in range(2 * self.ring - 2 if mid else self.ring, 2 * self.ring - 1):
            total = total + self.tail[i, n].astype(jnp.float32)
        self.write(i, total)

    def drain(self, i, first_y, mid):
        self.copy0(i, self.own.at[i]).wait_send()
        self.copy1(i, first_y).wait_send()
        self.wait_for(self.second(i, mid), self.send_sem.at[2, i])
        self.wait_for(self.third(i, mid), self.send_sem.at[3, i])

    def both(self, pair, act):
        middle = self.middle(pair)
        for first_y in (True, False):
            i = 2 * pair + (0 if first_y else 1)
            there = (pair >= 0) & (i < self.count)
            pl.when(there & middle)(functools.partial(act, i, first_y, True))
            pl.when(there & jnp.logical_not(middle))(functools.partial(act, i, first_y, False))

    def step(self, t, ahead=1, lags=(0, 1, 2, 3)):
        self.both(t, self.begin)
        self.both(t - ahead - lags[0], self.stage1)
        self.both(t - ahead - lags[1], self.stage2)
        self.both(t - ahead - lags[2], self.stage3)
        self.both(t - ahead - lags[3], self.finish)

    def steps(self, ahead=1, lags=(0, 1, 2, 3)):
        return (self.count + 1) // 2 + ahead + lags[3]

    def drain_all(self, first=0, last=None):
        def one(t, carry):
            self.both(t, self.drain)
            return carry
        lax.fori_loop(first, (self.count + 1) // 2 if last is None else last, one, 0)


def scatter_scratch(ring, count, rows, cols):
    bf = jnp.bfloat16
    return [
        pltpu.VMEM((4, ring, 2, 2, rows, cols), bf),
        pltpu.VMEM((count, ring, 2, 2, rows, cols), bf),
        pltpu.VMEM((count, ring, 2, rows, cols), bf),
        pltpu.VMEM((count, 2 * ring - 1, rows, cols), bf),
        pltpu.SemaphoreType.DMA((4,)),
        pltpu.SemaphoreType.DMA((4, count)),
        pltpu.SemaphoreType.DMA((4, count)),
    ]


def scatter_pick(grads, layout, cols):
    def pick(i, p, go):
        start = 0
        for ref, (size, outer) in zip(grads, layout):
            j = i - start
            def run(ref=ref, j=j, outer=outer):
                if outer:
                    go(ref.at[j, p], ref.at[j, 1 - p])
                else:
                    at = pl.ds(pl.multiple_of(lax.rem(j, 2) * cols, cols), cols)
                    go(ref.at[p, :, :, :, j // 2, :, at], ref.at[1 - p, :, :, :, j // 2, :, at])
            pl.when((j >= 0) & (j < size))(run)
            start += size
    return pick


class Gather:
    def __init__(self, ring, count, pick, sems):
        self.ring, self.count, self.pick = ring, count, pick
        self.local_sem, self.send_sem, self.recv_sem = sems
        self.p, self.c, self.h = place()
        self.hy, self.hx = self.h // 2, lax.rem(self.h, 2)
        self.core = (1 - self.p, self.c, self.h)
        self.xpeer = (self.p, self.c, self.hy * 2 + 1 - self.hx)
        self.ypeer = (self.p, self.c, (1 - self.hy) * 2 + self.hx)

    def remote(self, i, stage, src, dst, device):
        return pltpu.make_async_remote_copy(
            src_ref=src, dst_ref=dst, send_sem=self.send_sem.at[stage, i],
            recv_sem=self.recv_sem.at[stage, i], device_id=device, device_id_type=MESH)

    def same(self, i, stage, ref, device):
        return self.remote(i, stage, ref, ref, device)

    def begin(self, i, first_x, mid):
        def go(src, out):
            mine = out(self.p, self.c, self.hy, self.hx)
            pltpu.make_async_copy(src, mine, self.local_sem.at[i]).start()
            if mid:
                self.remote(i, 0, src, mine, self.near(first_x)).start()
                return
            for step in range(1, self.ring):
                peer = (self.p, lax.rem(self.c + step, self.ring), self.h)
                self.remote(i, 0, src, mine, peer).start()
        self.pick(i, go)

    def near(self, first_x):
        return self.xpeer if first_x else self.ypeer

    def block(self, out, first_x, mine):
        if first_x:
            return out(self.p, self.c, self.hy, self.hx if mine else 1 - self.hx)
        return out(self.p, self.c, self.hy if mine else 1 - self.hy, self.hx)

    def couple(self, out, first_x, at):
        return out(self.p, at, self.hy, ALL) if first_x else out(self.p, at, ALL, self.hx)

    def wait_for(self, ref, sem):
        pltpu.make_async_copy(ref, ref, sem).wait()

    def stage1(self, i, first_x, mid):
        def go(src, out):
            mine = out(self.p, self.c, self.hy, self.hx)
            pltpu.make_async_copy(src, mine, self.local_sem.at[i]).wait()
            if mid:
                self.same(i, 0, self.block(out, first_x, False), self.core).wait_recv()
                both = self.couple(out, first_x, self.c)
                for step in range(1, self.ring):
                    self.same(i, 1, both, (self.p, lax.rem(self.c + step, self.ring), self.h)).start()
                return
            self.wait_for(out(self.p, pl.ds(0, self.ring - 1), self.hy, self.hx), self.recv_sem.at[0, i])
            column = out(self.p, ALL, self.hy, self.hx)
            self.same(i, 1, column, self.near(first_x)).start()
            self.same(i, 3, column, self.core).start()
        self.pick(i, go)

    def first(self, out, mine, first_x):
        if first_x:
            return out(self.p, ALL, self.hy, self.hx if mine else 1 - self.hx)
        return out(self.p, ALL, self.hy if mine else 1 - self.hy, self.hx)

    def second(self, out, mine, first_x):
        if first_x:
            return out(self.p, ALL, self.hy if mine else 1 - self.hy, ALL)
        return out(self.p, ALL, ALL, self.hx if mine else 1 - self.hx)

    def stage2(self, i, first_x, mid):
        def go(src, out):
            half = self.second(out, True, first_x)
            if mid:
                self.wait_for(self.couple(out, first_x, pl.ds(0, self.ring - 1)), self.recv_sem.at[1, i])
                self.same(i, 2, half, self.near(not first_x)).start()
                self.same(i, 3, half, self.core).start()
                return
            came = self.first(out, False, first_x)
            self.same(i, 1, came, self.core).wait_recv()
            self.same(i, 2, half, self.near(not first_x)).start()
            self.same(i, 3, came, self.core).start()
        self.pick(i, go)

    def stage3(self, i, first_x, mid):
        def go(src, out):
            came = self.second(out, False, first_x)
            self.same(i, 2, came, self.core).wait_recv()
            self.same(i, 3, came, self.core).start()
        self.pick(i, go)

    def finish(self, i, first_x, mid):
        def go(src, out):
            self.wait_for(out(1 - self.p, ALL, ALL, ALL), self.recv_sem.at[3, i])
        self.pick(i, go)

    def drain(self, i, first_x, mid):
        def go(src, out):
            if mid:
                self.same(i, 0, self.block(out, first_x, True), self.core).wait_send()
                self.wait_for(self.couple(out, first_x, pl.ds(0, self.ring - 1)), self.send_sem.at[1, i])
            else:
                self.wait_for(out(self.p, pl.ds(0, self.ring - 1), self.hy, self.hx), self.send_sem.at[0, i])
                self.same(i, 1, self.first(out, True, first_x), self.core).wait_send()
            self.same(i, 2, self.second(out, True, first_x), self.core).wait_send()
            self.wait_for(out(self.p, ALL, ALL, ALL), self.send_sem.at[3, i])
        self.pick(i, go)

    def both(self, pair, act):
        middle = lax.rem(pair, 2) != 0
        for first_x in (True, False):
            i = 2 * pair + (0 if first_x else 1)
            there = (pair >= 0) & (i < self.count) & (i >= 0)
            pl.when(there & middle)(functools.partial(act, i, first_x, True))
            pl.when(there & jnp.logical_not(middle))(functools.partial(act, i, first_x, False))

    def step(self, t, ahead=2, lags=(0, 1, 2, 3)):
        self.both(t, self.begin)
        self.both(t - ahead - lags[0], self.stage1)
        self.both(t - ahead - lags[1], self.stage2)
        self.both(t - ahead - lags[2], self.stage3)
        self.both(t - ahead - lags[3], self.finish)

    def steps(self, ahead=2, lags=(0, 1, 2, 3)):
        return (self.count + 1) // 2 + ahead + lags[3]

    def drain_all(self):
        def one(t, carry):
            self.both(t, self.drain)
            return carry
        lax.fori_loop(0, (self.count + 1) // 2, one, 0)


def gather_sems(count):
    return [
        pltpu.SemaphoreType.DMA((count,)),
        pltpu.SemaphoreType.DMA((4, count)),
        pltpu.SemaphoreType.DMA((4, count)),
    ]


def gather_pick(src, wide, down, n_wide):
    cols = src.shape[-1]
    def pick(i, go):
        @pl.when(i < n_wide)
        def _():
            go(src.at[i], lambda p, c, y, x: wide.at[i, p, c, y, x])
        @pl.when(i >= n_wide)
        def _():
            j = i - n_wide
            at = pl.ds(pl.multiple_of(lax.rem(j, 2) * cols, cols), cols)
            go(src.at[i], lambda p, c, y, x: down.at[p, c, y, x, j // 2, :, at])
    return pick


def dot_tb(a, b):
    return lax.dot_general(a, b, (((1,), (1,)), ((), ())), preferred_element_type=jnp.float32)


def dot(a, b):
    return jnp.dot(a, b, preferred_element_type=jnp.float32)


def lanes(rows):
    return lax.broadcasted_iota(jnp.int32, (rows, 128), 1)


def split3(x):
    hi = x.astype(jnp.bfloat16).astype(jnp.float32)
    mid = (x - hi).astype(jnp.bfloat16).astype(jnp.float32)
    lo = x - hi - mid
    return hi, mid, lo


def at_lanes(base, first, values):
    lane = lanes(base.shape[0])
    for n, value in enumerate(values):
        base = jnp.where(lane == first + n, value, base)
    return base


def halves(x):
    return x, pltpu.roll(x, 64, 1)


def build_keys(pair, k_ref, v_ref, kf_ref, ka, va, kt=None, first=0, last=None):
    at = pl.ds(pl.multiple_of(pair * 128, 128), 128)
    rows = k_ref.shape[0]
    chunk = 512
    def one(n, carry):
        r = pl.ds(pl.multiple_of(n * chunk, chunk), chunk)
        lane = lanes(chunk)
        keys = halves(k_ref[r, at].astype(jnp.float32))
        values = halves(v_ref[r, at].astype(jnp.float32))
        feat = kf_ref[r, :].astype(jnp.float32)
        for m in range(2):
            full = jnp.where(lane < 64, keys[m], feat)
            ka[m, r, :] = full.astype(jnp.bfloat16)
            if kt is not None:
                kt[m, :, r] = full.T.astype(jnp.bfloat16)
            ones = jnp.where(lane < 67, 1.0, 0.0)
            va[m, r, :] = jnp.where(lane < 64, values[m], ones).astype(jnp.bfloat16)
        return carry
    lax.fori_loop(first, rows // chunk if last is None else last, one, 0)


def forward_block(pair, n, q_ref, qf_ref, hs_ref, ka, va, o_ref, of_ref, qa_ref):
    at = pl.ds(pl.multiple_of(pair * 128, 128), 128)
    r = pl.ds(pl.multiple_of(n * QB, QB), QB)
    lane = lanes(QB)
    queries = halves(q_ref[r, at].astype(jnp.float32) * (1.0 / math.sqrt(HDIM)))
    feat = qf_ref[r, :].astype(jnp.float32)
    row = lax.broadcasted_iota(jnp.int32, (QB, QB), 0)
    col = lax.broadcasted_iota(jnp.int32, (QB, QB), 1)
    outs = []
    for m in range(2):
        qa = jnp.where(lane < 64, queries[m], feat * hs_ref[pl.ds(pair * 2 + m, 1), :])
        qb = qa.astype(jnp.bfloat16)
        def part(first, size, mask=None):
            keys = pl.ds(pl.multiple_of(n * QB + first, QB), size)
            s = dot_tb(qb, ka[m, keys, :])
            if mask is not None:
                s = jnp.where(mask, s, FAR)
            return dot(jnp.exp(s).astype(jnp.bfloat16), va[m, keys, :])
        o = part(0, QB, col >= row) + part(QB, SPAN - 2 * QB) + part(SPAN - QB, QB, col <= row)
        total = o[:, 64:65]
        outs.append(o * (1.0 / total))
        hi, mid, lo = split3(-jnp.log(total))
        qa_ref[pair * 2 + m, r, :] = at_lanes(qa, 80, (hi, mid, lo)).astype(jnp.bfloat16)
    both = jnp.where(lane < 64, outs[0], pltpu.roll(outs[1], 64, 1))
    of_ref[r, at] = both
    o_ref[r, at] = both.astype(jnp.bfloat16)


def backward_block(pair, n, qf_ref, qa_ref, do_ref, of_ref, ka, va, kt, dka, dva, dq_ref, same, every):
    at = pl.ds(pl.multiple_of(pair * 128, 128), 128)
    r = pl.ds(pl.multiple_of(n * QB, QB), QB)
    lane = lanes(QB)
    grads = do_ref[r, at].astype(jnp.float32)
    terms = grads * of_ref[r, :]
    pieces = halves(grads)
    row = lax.broadcasted_iota(jnp.int32, (QB, QB), 0)
    col = lax.broadcasted_iota(jnp.int32, (QB, QB), 1)
    dqs = []
    qft = qf_ref[r, :].astype(jnp.float32).T[64:72, :]
    for m in range(2):
        own = (lane < 64) if m == 0 else (lane >= 64)
        delta = jnp.sum(jnp.where(own, terms, 0.0), axis=1, keepdims=True)
        da = at_lanes(jnp.where(lane < 64, pieces[m], 0.0), 64, split3(-delta)).astype(jnp.bfloat16)
        qb = qa_ref[m, r, :]
        dq = jnp.zeros((128, QB), jnp.float32)
        for first, size, edge in ((0, QB, 0), (QB, SPAN - 2 * QB, None), (SPAN - QB, QB, 1)):
            keys = pl.ds(pl.multiple_of(n * QB + first, QB), size)
            s = dot_tb(ka[m, keys, :], qb)
            if edge is not None:
                s = jnp.where((row >= col) if edge == 0 else (row <= col), s, FAR)
            p = jnp.exp(s)
            dp = dot_tb(va[m, keys, :], da)
            ds = (p * dp).astype(jnp.bfloat16)
            dva[m, keys, :] += dot(p.astype(jnp.bfloat16), da)
            dka[m, keys, :] += dot(ds, qb)
            dq = dq + dot(kt[m, :, keys], ds)
        dqs.append(dq[:64, :])
        sums = dq[64:72, :]
        pick = lax.broadcasted_iota(jnp.int32, (8, QB), 0) < 4
        h = pair * 2 + m
        same[h] += jnp.where(pick, sums * qft, 0.0)
        every[h] += jnp.where(pick, sums, 0.0)
    dq_ref[r, at] = (jnp.concatenate(dqs, axis=0).T * (1.0 / math.sqrt(HDIM))).astype(dq_ref.dtype)


def backward_finish(pair, dka, dva, dk_ref, dv_ref):
    at = pl.ds(pl.multiple_of(pair * 128, 128), 128)
    chunk = 512
    def one(n, carry):
        r = pl.ds(pl.multiple_of(n * chunk, chunk), chunk)
        lane = lanes(chunk)
        dk_ref[r, at] = jnp.where(lane < 64, dka[0, r, :], pltpu.roll(dka[1, r, :], 64, 1)).astype(dk_ref.dtype)
        dv_ref[r, at] = jnp.where(lane < 64, dva[0, r, :], pltpu.roll(dva[1, r, :], 64, 1)).astype(dv_ref.dtype)
        return carry
    lax.fori_loop(0, dk_ref.shape[0] // chunk, one, 0)


def features(seg, var):
    lane = jnp.arange(128)[None, :]
    same = (var[:, None] == (lane - 64) % 4) & (lane >= 64) & (lane < 76)
    doc = (lane >= 76) & (lane < 80)
    here = seg[:, None] == lane - 76
    keys = jnp.where(doc & ~here, FAR, jnp.where(same | ((lane >= 80) & (lane < 83)), 1.0, 0.0))
    queries = jnp.where(same | (doc & here), 1.0, 0.0)
    return queries.astype(jnp.bfloat16), keys.astype(jnp.bfloat16)


def head_scales(bias):
    hi, mid, lo = split3(bias[:, :1] - bias[:, 1:])
    lane = jnp.arange(128)[None, :]
    parts = jnp.where(lane < 68, hi, jnp.where(lane < 72, mid, lo))
    return jnp.where(lane < 64, 0.0, jnp.where(lane < 76, parts, jnp.where(lane < 80, 1.0, 0.0)))


def scale_of(x):
    return lax.rsqrt(jnp.mean(x * x, axis=-1, keepdims=True) + EPS)


def head_mean(x):
    row = lax.broadcasted_iota(jnp.int32, (128, 128), 0)
    col = lax.broadcasted_iota(jnp.int32, (128, 128), 1)
    group = jnp.where((row < 64) == (col < 64), 1.0 / HDIM, 0.0).astype(BF)
    hi = x.astype(BF)
    rest = x - hi.astype(F32)
    mid = rest.astype(BF)
    low = (rest - mid.astype(F32)).astype(BF)
    return dot(hi, group) + dot(mid, group) + dot(low, group)


def swap_halves(x):
    lane = lax.rem(lanes(x.shape[0]), 64)
    return jnp.where(lane < 32, pltpu.roll(x, 96, 1), pltpu.roll(x, 32, 1))


def norm_back_rows(u, r, gain, dy):
    scaled = dy * gain
    du = r * scaled - u * (r * r * r) * jnp.mean(scaled * u, axis=-1, keepdims=True)
    return du, jnp.sum(dy * u * r, axis=0, keepdims=True)


def as_blocks(value, shape):
    rows, cols = shape[-2:]
    if cols == value.shape[1]:
        return value.astype(BF).reshape(shape)
    depth = rows * cols // value.shape[1]
    parts = value.reshape(-1, depth, value.shape[1])
    parts = [parts[:, :, n:n + cols] for n in range(0, value.shape[1], cols)]
    return jnp.concatenate(parts, axis=1).astype(BF).reshape(shape)


def remote(src, dst, send, recv, device):
    return pltpu.make_async_remote_copy(
        src_ref=src, dst_ref=dst, send_sem=send, recv_sem=recv, device_id=device, device_id_type=MESH)


def local_copy(src, dst, sem):
    return pltpu.make_async_copy(src, dst, sem)


def wide_at(first):
    return pl.ds(pl.multiple_of(first, 256), 256)


class Rim:
    def __init__(self, ring):
        self.p, self.c, self.h = place()
        self.ring = ring
        self.has_low, self.has_high = self.c > 0, self.c < ring - 1
        self.low = lax.rem(self.c + ring - 1, ring)
        self.high = lax.rem(self.c + 1, ring)
        self.low_edge = self.has_low & (self.h == 0)
        self.high_edge = self.has_high & (self.h == 3)

    def greet(self):
        beyond = [(self.p, block, n) for block in (self.low, self.high) for n in range(4)]
        greet(group_peers(self.ring) + [(self.p, self.c, 3 - self.h)] + beyond)


def pair_at(first, pair):
    return pl.ds(pl.multiple_of(first + pair * 128, 128), 128)


LAGS = (2, (0, 1, 2, 3))
FIRST = LAGS[0] + LAGS[1][3]
EXTRA = 2
EVERY = 4


def as_matrix(value):
    rows, cols = value.shape[-2:]
    if cols == 512:
        return value.reshape(-1, 512)
    depth = rows * cols // 512
    parts = value.astype(F32).reshape(-1, rows, cols)
    parts = [parts[:, n:n + depth] for n in range(0, rows, depth)]
    return jnp.concatenate(parts, axis=2).reshape(-1, 512).astype(BF)


def attend_kernel(ring, n_wide, count, x_ref, cos_ref, sin_ref, hg_ref, kf_own, qf_ref, hs_ref, src, gain_src,
                  tok_ref, of_ref, qa_ref, kx, vx, kf_ref, raw_ref, gain_ref, wide, down,
                  rot, nrm, w_tile, gains, q_loc, o_loc, ka, va, tile_sem, local_sem, a2a_send, a2a_recv, rim_send, rim_recv,
                  kf_send, kf_recv, out_send, out_recv, *sems):
    p, c, h = place()
    rim = Rim(ring)
    greet(group_peers(ring) + [(p, c, 3 - h)])
    rows, width = tok_ref.shape
    group = 4 * rows
    mine = pl.ds(pl.multiple_of(h * rows, rows), rows)
    mine_x = pl.ds(pl.multiple_of(HALF + h * rows, rows), rows)
    places = ((0, q_loc, mine), (1, kx, mine_x), (2, vx, mine_x))
    three = pl.ds(0, 3 * rows)
    sides = ((rim.has_high, rim.high, group, 0), (rim.has_low, rim.low, HALF, HALF + group))

    small = Gather(ring, 1, lambda i, go: go(gain_src, lambda p, c, y, x: gains.at[p, c, y, x]), sems[:3])
    work = Gather(ring, count, gather_pick(src, wide, down, n_wide), sems[3:])

    def kf_copy(side):
        there, block, first, to = sides[side]
        return remote(kf_own.at[pl.ds(first - HALF * side if side else first - HALF, HALF)], kf_ref.at[pl.ds(to, HALF)],
                      kf_send.at[side], kf_recv.at[side], (p, block, h))

    def begin(t, carry):
        small.step(t, *LAGS)
        work.step(t, *LAGS)
        return carry
    lax.fori_loop(0, 2, begin, 0)
    for side in range(2):
        pl.when(sides[side][0])(lambda: kf_copy(side).start())
    kf_ref[HALF:HALF + group, :] = kf_own[...]
    lane = lax.broadcasted_iota(jnp.int32, (HALF, 128), 1)
    nothing = jnp.where((lane >= 76) & (lane < 80), FAR, 0.0).astype(BF)
    @pl.when(jnp.logical_not(rim.has_low))
    def _():
        kf_ref[0:HALF, :] = nothing
        for ref in (kx, vx):
            ref[0:HALF, :] = jnp.zeros((HALF, 256), BF)
    @pl.when(jnp.logical_not(rim.has_high))
    def _():
        kf_ref[HALF + group:2 * HALF + group, :] = nothing
        for ref in (kx, vx):
            ref[HALF + group:2 * HALF + group, :] = jnp.zeros((HALF, 256), BF)
    lax.fori_loop(2, FIRST, begin, 0)

    def share(kind, head, pair):
        ref, at = places[kind][1:]
        cols = pair_at(0, pair)
        part = rot.at[:, pair_at(kind * width + head * 256, pair)]
        there = ref.at[at, cols]
        @pl.when(head == h)
        def _():
            local_copy(part, there, local_sem.at[kind, pair]).start()
        @pl.when(head != h)
        def _():
            remote(part, there, a2a_send.at[kind, pair], a2a_recv.at[kind, pair], (p, c, head)).start()

    def tile_copy(t):
        return local_copy(wide.at[t], w_tile.at[lax.rem(t, 2)], tile_sem.at[lax.rem(t, 2)])

    for k in range(3):
        begin(FIRST + k, 0)
        for m in range(2):
            tile_copy(2 * k + m).start()
        if k == 0:
            total = gains[0, 0, 0, 0].astype(F32)
            for d in range(1, 8 * ring):
                total = total + gains[d // (4 * ring), d // 4 % ring, d // 2 % 2, d % 2].astype(F32)
            gain_ref[...] = total
            def norm(n, carry):
                at = pl.ds(pl.multiple_of(n * 128, 128), 128)
                x = x_ref[at, :].astype(F32)
                y = x * scale_of(x)
                for m in range(width // 128):
                    part = slice(m * 128, (m + 1) * 128)
                    nrm[at, part] = (y[:, part] * total[m:m + 1, :]).astype(BF)
                return carry
            lax.fori_loop(0, rows // 128, norm, 0)
        for m in range(2):
            t = 2 * k + m
            tile_copy(t).wait()
            def project(n, carry):
                at = pl.ds(pl.multiple_of(n * 128, 128), 128)
                raw = dot(nrm[at, :], as_matrix(w_tile[t % 2])).astype(BF)
                if t < 4:
                    raw_ref[at, t * 512:(t + 1) * 512] = raw
                    gain = hg_ref[t // 2:t // 2 + 1, :]
                    for m in range(4):
                        u = raw[:, m * 128:(m + 1) * 128].astype(F32)
                        y = u * lax.rsqrt(head_mean(u * u) + EPS) * gain
                        y = y * cos_ref[at, :] + swap_halves(y) * sin_ref[at, :]
                        rot[at, t * 512 + m * 128:t * 512 + (m + 1) * 128] = y.astype(BF)
                else:
                    rot[at, t * 512:(t + 1) * 512] = raw
                return carry
            lax.fori_loop(0, rows // 128, project, 0)
            for pair in range(2):
                for m2 in range(2):
                    share(t // 2, t % 2 * 2 + m2, pair)

    def rim_copy(ref, side, kind, pair):
        there, block, first, to = sides[side]
        return remote(ref.at[pl.ds(first, HALF), pair_at(0, pair)], ref.at[pl.ds(to, HALF), pair_at(0, pair)],
                      rim_send.at[side, kind, pair], rim_recv.at[side, kind, pair], (p, block, h))

    blocks = group // QB
    margin = HALF // QB
    def more(t, carry):
        work.step(t, *LAGS)
        return carry
    lax.fori_loop(FIRST + 3, FIRST + 3 + EXTRA, more, 0)
    def pair_step(pair, carry):
        cols = pair_at(0, pair)
        for kind, ref, at in places:
            local_copy(ref.at[at, cols], ref.at[at, cols], local_sem.at[kind, pair]).wait()
            local_copy(ref.at[three, cols], ref.at[three, cols], a2a_recv.at[kind, pair]).wait()
        for side in range(2):
            @pl.when(sides[side][0])
            def _():
                for kind, ref in ((0, kx), (1, vx)):
                    rim_copy(ref, side, kind, pair).start()
        build_keys(pair, kx, vx, kf_ref, ka, va, None, 1, 1 + group // HALF)
        def step(n, c):
            @pl.when(lax.rem(n, EVERY) == 0)
            def _():
                work.step(FIRST + 3 + EXTRA + (pair * blocks + n) // EVERY, *LAGS)
            forward_block(pair, lax.rem(n + margin, blocks), q_loc, qf_ref, hs_ref, ka, va, o_loc, of_ref, qa_ref)
            return c
        lax.fori_loop(0, blocks - 2 * margin, step, 0)
        for side in range(2):
            @pl.when(sides[1 - side][0])
            def _():
                for kind, ref in ((0, kx), (1, vx)):
                    rim_copy(ref, side, kind, pair).wait_recv()
                pl.when(pair == 0)(lambda: kf_copy(side).wait_recv())
        build_keys(pair, kx, vx, kf_ref, ka, va, None, 0, 1)
        build_keys(pair, kx, vx, kf_ref, ka, va, None, 1 + group // HALF, 2 + group // HALF)
        lax.fori_loop(blocks - 2 * margin, blocks, step, 0)
        to_cols = pair_at(h * 256, pair)
        local_copy(o_loc.at[mine, cols], tok_ref.at[:, to_cols], local_sem.at[3, pair]).start()
        for step_ in range(1, 4):
            to = lax.rem(h + step_, 4)
            theirs = pl.ds(pl.multiple_of(to * rows, rows), rows)
            remote(o_loc.at[theirs, cols], tok_ref.at[:, to_cols], out_send.at[pair], out_recv.at[pair], (p, c, to)).start()
        return carry
    lax.fori_loop(0, 2, pair_step, 0)

    done = FIRST + 3 + EXTRA + 2 * blocks // EVERY
    lax.fori_loop(done, max(done, work.steps(*LAGS)), more, 0)
    for pair in range(2):
        cols = pair_at(0, pair)
        local_copy(o_loc.at[mine, cols], tok_ref.at[:, pair_at(h * 256, pair)], local_sem.at[3, pair]).wait()
        part = tok_ref.at[:, pl.ds(0, 384)]
        local_copy(part, part, out_recv.at[pair]).wait()
        local_copy(part, part, out_send.at[pair]).wait()
        for kind, ref, at in places:
            local_copy(ref.at[three, cols], ref.at[three, cols], a2a_send.at[kind, pair]).wait()
        for side in range(2):
            @pl.when(sides[side][0])
            def _():
                for kind, ref in ((0, kx), (1, vx)):
                    rim_copy(ref, side, kind, pair).wait_send()
                if pair == 0:
                    kf_copy(side).wait_send()
    small.drain_all()
    work.drain_all()


def attend(x, cosine, sine, head_gains, kf, qf, hs, src, gain_src, n_wide, ring, collective_id):
    rows, width = x.shape
    group = 4 * rows
    ext = group + 2 * HALF
    count, r, w = src.shape
    dma = pltpu.SemaphoreType.DMA
    return pl.pallas_call(
        functools.partial(attend_kernel, ring, n_wide, count),
        out_shape=(
            jax.ShapeDtypeStruct((rows, width), BF),
            jax.ShapeDtypeStruct((group, 256), F32),
            jax.ShapeDtypeStruct((4, group, 128), BF),
            jax.ShapeDtypeStruct((ext, 256), BF),
            jax.ShapeDtypeStruct((ext, 256), BF),
            jax.ShapeDtypeStruct((ext, 128), BF),
            jax.ShapeDtypeStruct((rows, 2 * width), BF),
            jax.ShapeDtypeStruct((16, 128), F32),
            jax.ShapeDtypeStruct((n_wide, 2, ring, 2, 2, r, w), BF),
            jax.ShapeDtypeStruct((2, ring, 2, 2, (count - n_wide) // 2, r, 2 * w), BF),
        ),
        in_specs=[VM] * 7 + [ANY, ANY],
        out_specs=(VM,) * 8 + (ANY, ANY),
        scratch_shapes=[
            pltpu.VMEM((rows, 3 * width), BF), pltpu.VMEM((rows, width), BF), pltpu.VMEM((2, 2, ring, 2, 2, r, w), BF),
            pltpu.VMEM((2, ring, 2, 2, 16, 128), BF),
            pltpu.VMEM((group, 256), BF), pltpu.VMEM((group, 256), BF),
            pltpu.VMEM((2, ext, 128), BF), pltpu.VMEM((2, ext, 128), BF),
            dma((2,)), dma((4, 2)), dma((3, 2)), dma((3, 2)), dma((2, 2, 2)), dma((2, 2, 2)), dma((2,)), dma((2,)), dma((2,)), dma((2,)),
        ] + gather_sems(1) + gather_sems(count),
        compiler_params=pltpu.CompilerParams(collective_id=collective_id, has_side_effects=True, vmem_limit_bytes=60 * MIB),
        name="attend",
    )(x, cosine, sine, head_gains, kf, qf, hs, src, gain_src)


BACK_LAGS = (1, (0, 1, 2, 3))
BACK_EVERY = 8
LATE = 12
IN_UNPROJECT = 2


def down_blocks(value, shape):
    rows, cols = shape[-2:]
    if cols == value.shape[1]:
        return value.astype(BF).reshape(shape)
    depth = rows * cols // value.shape[1]
    parts = value.reshape(-1, depth, value.shape[1])
    parts = [parts[:, :, n:n + cols] for n in range(0, value.shape[1], cols)]
    return jnp.concatenate(parts, axis=1).astype(BF).reshape(shape)


def feed_phase(work, heads_hbm, cot_hbm, x_hbm, gain, wide, down, g_gu, g_go, g_gd, out_hbm, dhid_hbm, d_tok, gffn_ref,
               back, hidden, acc, dnorm, nrm_t, w_gu, w_d, stage, stage_d, in_sem, w_sem, stage_sem, out_sem):
    tiles = down.shape[0] // 512
    width = back.shape[1] // 3
    heads, cot, nrm = (back.at[:, n * width:(n + 1) * width] for n in range(3))
    spots = g_gd.shape[1] * g_gd.shape[0] // tiles

    def weights(t, slot):
        return [local_copy(wide.at[8 + t], w_gu.at[slot, 0], w_sem.at[slot, 0]),
                local_copy(wide.at[16 + t], w_gu.at[slot, 1], w_sem.at[slot, 1]),
                local_copy(down.at[pl.ds(pl.multiple_of(t * 512, 512), 512)], w_d.at[slot], w_sem.at[slot, 2])]

    def out_weight(slot):
        return [local_copy(wide.at[6 + n], w_gu.at[slot, n], w_sem.at[slot, n]) for n in range(2)]

    def staged(t):
        per = g_gd.shape[1] // spots
        return [local_copy(stage.at[0], g_gu.at[2 * t], stage_sem.at[0]),
                local_copy(stage.at[1], g_gu.at[2 * t + 1], stage_sem.at[1]),
                local_copy(stage_d, g_gd.at[t // per, pl.ds(lax.rem(t, per) * spots, spots)], stage_sem.at[2])]

    first = [local_copy(heads_hbm, heads, in_sem.at[0]), local_copy(cot_hbm, cot, in_sem.at[1]),
             local_copy(x_hbm, w_d.at[1], in_sem.at[2])] + out_weight(1)
    for copy in first + weights(0, 0):
        copy.start()
    for copy in first:
        copy.wait()
    for n in range(2):
        at = slice(n * 512, (n + 1) * 512)
        hidden[:, at] = w_d[1, :, at].astype(F32) + dot(heads[...], w_gu[1, n])
    def normalise(n, carry):
        at = pl.ds(pl.multiple_of(n * 128, 128), 128)
        h = hidden[at, :]
        y = h * scale_of(h) * gain
        nrm[at, :] = y.astype(BF)
        nrm_t[:, at] = y.T.astype(BF)
        acc[at, :] = h
        dnorm[at, :] = jnp.zeros_like(h)
        return carry
    lax.fori_loop(0, 4, normalise, 0)

    def tile(t, carry):
        slot = lax.rem(t, 2)
        for copy in weights(t, slot):
            copy.wait()
        @pl.when(t < tiles - 1)
        def _():
            for copy in weights(t + 1, 1 - slot):
                copy.start()
        @pl.when(t == tiles - 1)
        def _():
            for copy in out_weight(tiles % 2):
                copy.start()
        normed = nrm[...]
        wg, wu, wd = w_gu[slot, 0], w_gu[slot, 1], w_d[slot]
        gate = dot(normed, wg)
        up = dot(normed, wu)
        d_product = dot_tb(cot[...], wd)
        sig = jax.nn.sigmoid(gate)
        silu = gate * sig
        product = silu * up
        prod_b = product.astype(BF)
        d_gate = (d_product * up * sig * (1.0 + gate * (1.0 - sig))).astype(BF)
        d_up = (d_product * silu).astype(BF)
        acc[...] += dot(prod_b, wd)
        dnorm[...] += dot_tb(d_gate, wg) + dot_tb(d_up, wu)
        @pl.when(t > 0)
        def _():
            for copy in staged(t - 1):
                copy.wait()
            work.step(t - 1, *BACK_LAGS)
        stage[0] = as_blocks(dot(nrm_t[...], d_gate), stage.shape[1:])
        stage[1] = as_blocks(dot(nrm_t[...], d_up), stage.shape[1:])
        stage_d[...] = down_blocks(dot(product.T.astype(BF), cot[...]), stage_d.shape)
        for copy in staged(t):
            copy.start()
        return carry
    lax.fori_loop(0, tiles, tile, 0)
    for copy in staged(tiles - 1):
        copy.wait()
    work.step(tiles - 1, *BACK_LAGS)

    def finish(n, carry):
        at = pl.ds(pl.multiple_of(n * 128, 128), 128)
        h = hidden[at, :]
        du, terms = norm_back_rows(h, scale_of(h), gain, dnorm[at, :])
        d_hidden = cot[at, :].astype(F32) + du
        hidden[at, :] = d_hidden
        nrm[at, :] = d_hidden.astype(BF)
        heads_t = heads[at, :].astype(F32).T.astype(BF)
        nrm_t[:, at] = heads_t
        cot[at, :] = acc[at, :].astype(BF)
        return carry + terms
    gffn_ref[...] = lax.fori_loop(0, 4, finish, jnp.zeros(gffn_ref.shape, F32))
    last = [local_copy(cot, out_hbm, out_sem.at[0]), local_copy(hidden, dhid_hbm, out_sem.at[1])]
    for copy in last:
        copy.start()
    for copy in out_weight(tiles % 2):
        copy.wait()
    d_attn = nrm[...]
    total = jnp.zeros(hidden.shape, F32)
    for n in range(2):
        at = slice(n * 512, (n + 1) * 512)
        total = total + dot_tb(d_attn[:, at], w_gu[tiles % 2, n])
    d_tok[...] = total.astype(BF)
    for n in range(2):
        at = slice(n * 512, (n + 1) * 512)
        stage[n] = as_blocks(dot(nrm_t[...], d_attn[:, at]), stage.shape[1:])
        copy = local_copy(stage.at[n], g_go.at[n], stage_sem.at[n])
        copy.start()
    for n in range(2):
        local_copy(stage.at[n], g_go.at[n], stage_sem.at[n]).wait()
    for copy in last:
        copy.wait()


def score_phase(work, first_step, ring, d_tok, kx_hbm, vx_hbm, kf_ref, qf_ref, qa_hbm, of_hbm, do_loc, rims, back, same, every, between,
                kx, vx, qa, of, dq_loc, dk_loc, dv_loc, ka, va, kt, dka, dva,
                load_sem, local_sem, in_send, in_recv, back_send, back_recv, rim_send, rim_recv):
    p, c, h = place()
    rim = Rim(ring)
    rows, width = d_tok.shape
    group = 4 * rows
    mine = pl.ds(pl.multiple_of(h * rows, rows), rows)
    three = pl.ds(0, 3 * rows)
    for pair in range(2):
        cols = pair_at(0, pair)
        local_copy(d_tok.at[:, pair_at(h * 256, pair)], do_loc.at[mine, cols], local_sem.at[0, pair]).start()
        for step in range(1, 4):
            to = lax.rem(h + step, 4)
            remote(d_tok.at[:, pair_at(to * 256, pair)], do_loc.at[mine, cols], in_send.at[pair], in_recv.at[pair], (p, c, to)).start()
    same[...] = jnp.zeros_like(same)
    every[...] = jnp.zeros_like(every)

    trios = ((0, dq_loc, 0), (1, dk_loc, HALF), (2, dv_loc, HALF))
    kinds = ((0, dk_loc), (1, dv_loc))
    sides = ((rim.has_high, rim.high, HALF + group), (rim.has_low, rim.low, 0))

    def rim_copy(ref, side, kind, pair):
        there, block, first = sides[side]
        cols = pair_at(0, pair)
        return remote(ref.at[pl.ds(first, HALF), cols], rims.at[side, kind, :, cols],
                      rim_send.at[side, kind, pair], rim_recv.at[side, kind, pair], (p, block, h))

    def give(kind, pair, wanted):
        _, ref, skip = trios[kind]
        cols, at = pair_at(0, pair), pair_at(kind * width + h * 256, pair)
        for step in range(4):
            to = lax.rem(h + step, 4)
            theirs = ref.at[pl.ds(pl.multiple_of(skip + to * rows, rows), rows), cols]
            def go():
                if step == 0:
                    local_copy(theirs, back.at[:, at], local_sem.at[1 + kind, pair]).start()
                else:
                    remote(theirs, back.at[:, at], back_send.at[kind, pair], back_recv.at[kind, pair], (p, c, to)).start()
            if wanted is None:
                go()
            else:
                edge = (to == 0) | (to == 3)
                pl.when(edge if wanted else jnp.logical_not(edge))(go)

    def edges_back(pair):
        cols = pair_at(0, pair)
        for side in range(2):
            first = HALF if side == 0 else group
            @pl.when(sides[1 - side][0])
            def _():
                for kind, ref in kinds:
                    rim_copy(ref, side, kind, pair).wait_recv()
                    for m in range(4):
                        to = pl.ds(first + m * 128, 128)
                        more = rims[side, kind, pl.ds(m * 128, 128), cols].astype(F32)
                        ref[to, cols] = (ref[to, cols].astype(F32) + more).astype(BF)
        give(1, pair, True)
        give(2, pair, True)

    blocks = group // QB
    def pair_step(pair, carry):
        cols = pair_at(0, pair)
        loads = [local_copy(kx_hbm.at[:, cols], kx, load_sem.at[0]), local_copy(vx_hbm.at[:, cols], vx, load_sem.at[1]),
                 local_copy(qa_hbm.at[pl.ds(pair * 2, 2)], qa, load_sem.at[2]), local_copy(of_hbm.at[:, cols], of, load_sem.at[3])]
        for copy in loads:
            copy.start()
        dka[...] = jnp.zeros_like(dka)
        dva[...] = jnp.zeros_like(dva)
        for copy in loads:
            copy.wait()
        build_keys(0, kx, vx, kf_ref, ka, va, kt)
        local_copy(do_loc.at[mine, cols], do_loc.at[mine, cols], local_sem.at[0, pair]).wait()
        local_copy(do_loc.at[three, cols], do_loc.at[three, cols], in_recv.at[pair]).wait()
        def step(m, c):
            @pl.when(lax.rem(m, BACK_EVERY) == 0)
            def _():
                work.step(first_step + (pair * blocks + m) // BACK_EVERY, *BACK_LAGS)
            backward_block(pair, m, qf_ref, qa, do_loc, of, ka, va, kt, dka, dva, dq_loc, same, every)
            return c
        lax.fori_loop(0, blocks // 2, step, 0)
        @pl.when(pair == 1)
        def _():
            edges_back(0)
            between()
        lax.fori_loop(blocks // 2, blocks, step, 0)
        backward_finish(pair, dka, dva, dk_loc, dv_loc)
        for side in range(2):
            @pl.when(sides[side][0])
            def _():
                for kind, ref in kinds:
                    rim_copy(ref, side, kind, pair).start()
        give(1, pair, False)
        give(2, pair, False)
        give(0, pair, None)
        return carry
    lax.fori_loop(0, 2, pair_step, 0)
    edges_back(1)
    done = first_step + 2 * blocks // BACK_EVERY
    def more(t, carry):
        work.step(t, *BACK_LAGS)
        return carry
    lax.fori_loop(done, max(done, LATE), more, 0)

    part = back.at[:, pl.ds(0, 384)]
    for pair in range(2):
        cols = pair_at(0, pair)
        for kind in range(3):
            at = pair_at(kind * width + h * 256, pair)
            local_copy(back.at[:, at], back.at[:, at], local_sem.at[1 + kind, pair]).wait()
            local_copy(part, part, back_recv.at[kind, pair]).wait()
            local_copy(part, part, back_send.at[kind, pair]).wait()
        local_copy(do_loc.at[three, cols], do_loc.at[three, cols], in_send.at[pair]).wait()
        for side in range(2):
            @pl.when(sides[side][0])
            def _():
                for kind, ref in kinds:
                    rim_copy(ref, side, kind, pair).wait_send()


def unproject_phase(first, done, work, x_hbm, gain, wide, raw_hbm, cos_ref, sin_ref, hg_ref, dhid_hbm, back, g_qkv, gin_hbm, gattn_ref, ghead_ref,
                    before, x, nrm_t, dnorm, w, raw, stage, dhid, in_sem, w_sem, stage_sem):
    def tile_copies(t, slot):
        copies = [local_copy(wide.at[t], w.at[slot], w_sem.at[slot, 0])]
        if t < 4:
            copies.append(local_copy(raw_hbm.at[:, t * 512:(t + 1) * 512], raw.at[slot], w_sem.at[slot, 1]))
        return copies
    late = local_copy(dhid_hbm, dhid, in_sem.at[1])
    load = local_copy(x_hbm, x, in_sem.at[0])
    load.start()
    late.start()
    for copy in tile_copies(0, 0):
        copy.start()
    load.wait()
    def normalise(n, carry):
        at = pl.ds(pl.multiple_of(n * 128, 128), 128)
        u = x[at, :].astype(F32)
        nrm_t[:, at] = (u * scale_of(u) * gain).T.astype(BF)
        return carry
    lax.fori_loop(0, 4, normalise, 0)
    ghead_ref[...] = jnp.zeros_like(ghead_ref)
    for t in range(6):
        slot = t % 2
        if t < 5:
            for copy in tile_copies(t + 1, 1 - slot):
                copy.start()
        for copy in tile_copies(t, slot):
            copy.wait()
        if t < 4:
            kind = t // 2
            head_gain = hg_ref[kind:kind + 1, :]
            def unrotate(n, carry):
                at = pl.ds(pl.multiple_of(n * 128, 128), 128)
                for m in range(4):
                    part = slice(m * 128, (m + 1) * 128)
                    wide_part = slice(t * 512 + m * 128, t * 512 + (m + 1) * 128)
                    u = raw[slot, at, part].astype(F32)
                    dy = back[at, wide_part].astype(F32)
                    dy = dy * cos_ref[at, :] - swap_halves(dy) * sin_ref[at, :]
                    r = lax.rsqrt(head_mean(u * u) + EPS)
                    scaled = dy * head_gain
                    back[at, wide_part] = (r * scaled - u * (r * r * r) * head_mean(scaled * u)).astype(BF)
                    ghead_ref[kind:kind + 1, :] += jnp.sum(dy * u * r, axis=0, keepdims=True)
                return carry
            lax.fori_loop(0, 4, unrotate, 0)
        d_proj = back[:, t * 512:(t + 1) * 512]
        stage[slot] = as_blocks(dot(nrm_t[...], d_proj), stage.shape[1:])
        copy = local_copy(stage.at[slot], g_qkv.at[t], stage_sem.at[slot])
        copy.start()
        part = dot_tb(d_proj, w[slot])
        if t == 0:
            dnorm[...] = part
        else:
            dnorm[...] += part
        copy.wait()
        if t < 2:
            for n in range(IN_UNPROJECT // 2):
                first.step(done + t * IN_UNPROJECT // 2 + n, *BACK_LAGS)
        if t == 1:
            before()
        if t % 2:
            work.step(t // 2, *BACK_LAGS)
    late.wait()
    def finish(n, carry):
        at = pl.ds(pl.multiple_of(n * 128, 128), 128)
        u = x[at, :].astype(F32)
        du, terms = norm_back_rows(u, scale_of(u), gain, dnorm[at, :])
        dhid[at, :] = dhid[at, :] + du
        return carry + terms
    gattn_ref[...] = lax.fori_loop(0, 4, finish, jnp.zeros(gattn_ref.shape, F32))
    copy = local_copy(dhid, gin_hbm, in_sem.at[1])
    copy.start()
    copy.wait()


def train_kernel(ring, x, heads, cot, gains, wide, down, kx, vx, kf, qf, qa, of, raw, cos_ref, sin_ref, hg_ref,
                 out, gin, sums, small_out, dhid, g_gu, g_go, g_gd, g_qkv,
                 d_tok, do_loc, rims, back, same, every, gffn, gattn, ghead,
                 small, came, far, small_send, small_recv, credit,
                 local_sem, in_send, in_recv, back_send, back_recv, rim_send, rim_recv, *buffers):
    p, c, h = place()
    peers = group_peers(ring)
    greet(peers + [(p, c, 3 - h)])
    rows, width = d_tok.shape
    group, ext = 4 * rows, 4 * rows + 2 * HALF
    r, w = sums.shape[-2:]
    block = (2, ring, 2, 2, r, w)
    bufs, sems, last_sems = buffers[:4], buffers[4:7], (buffers[4],) + buffers[7:]
    dma = pltpu.SemaphoreType.DMA
    count = 26

    def write(i, total):
        sums[i] = total

    def write_last(i, total):
        sums[count + i] = total

    work = Scatter(ring, count, lambda pair: pair < 0, scatter_pick((g_gu, g_go, g_gd), ((16, True), (2, True), (8, False)), w), bufs, sems, write)
    last = Scatter(ring, 6, lambda pair: pair < 0, scatter_pick((g_qkv,), ((6, True),), w), bufs, last_sems, write_last)
    vm = pltpu.VMEM
    tiles = down.shape[0] // 512
    spots = g_gd.shape[0] * g_gd.shape[1] // tiles

    pl.run_scoped(
        functools.partial(feed_phase, work, heads, cot, x, gains[1], wide, down, g_gu, g_go, g_gd, out, dhid, d_tok, gffn, back),
        vm((rows, width), F32), vm((rows, width), F32), vm((rows, width), F32), vm((width, rows), BF), vm((2, 2, width, 512), BF), vm((2, 512, width), BF),
        vm((2,) + block, BF), vm((spots,) + g_gd.shape[2:], BF), dma((3,)), dma((2, 3)), dma((3,)), dma((2,)))
    def between():
        work.drain_all(0, 3)
        for peer in peers:
            pl.semaphore_signal(credit, inc=1, device_id=peer, device_id_type=MESH)

    def score(kx_p, vx_p, qa_p, of_p, dq_loc, dk_loc, dv_loc, ka, va, kt, dka, dva, load_sem):
        score_phase(work, tiles, ring, d_tok, kx, vx, kf, qf, qa, of, do_loc, rims, back, same, every, between,
                    kx_p, vx_p, qa_p, of_p, dq_loc, dk_loc, dv_loc, ka, va, kt, dka, dva,
                    load_sem, local_sem, in_send, in_recv, back_send, back_recv, rim_send, rim_recv)

    pl.run_scoped(
        score,
        vm((ext, 128), BF), vm((ext, 128), BF), vm((2, group, 128), BF), vm((group, 128), F32),
        vm((group, 256), BF), vm((ext, 256), BF), vm((ext, 256), BF),
        vm((2, ext, 128), BF), vm((2, ext, 128), BF), vm((2, 128, ext), BF), vm((2, ext, 128), F32), vm((2, ext, 128), F32),
        dma((4,)))
    pl.run_scoped(
        functools.partial(unproject_phase, work, max(LATE, tiles + 2 * (group // QB) // BACK_EVERY), last, x, gains[0], wide, raw, cos_ref, sin_ref, hg_ref, dhid, back, g_qkv, gin, gattn, ghead,
                          lambda: pl.semaphore_wait(credit, len(peers))),
        vm((rows, width), BF), vm((width, rows), BF), vm((rows, width), F32), vm((2, width, 512), BF), vm((2, rows, 512), BF),
        vm((2,) + block, BF), vm((rows, width), F32), dma((2,)), dma((2, 2)), dma((2,)))

    def total_of(value):
        return jnp.sum(jnp.sum(value, axis=1, keepdims=True), axis=2, keepdims=True)
    s, e = total_of(same[...]), total_of(every[...])
    lane = lax.broadcasted_iota(jnp.int32, (1, 128), 1)
    bias = jnp.zeros((1, 128), F32)
    for m in range(4):
        bias = jnp.where(lane == h * 8 + 2 * m, s[m], jnp.where(lane == h * 8 + 2 * m + 1, e[m] - s[m], bias))
    for n in range(8):
        at = slice(n * 128, (n + 1) * 128)
        small[0, n:n + 1, :] = gattn[:, at]
        small[0, 8 + n:9 + n, :] = gffn[:, at]
    small[0, 16:18, :] = ghead[...]
    small[0, 18:19, :] = bias
    small[0, 19:24, :] = jnp.zeros((5, 128), F32)
    hops = (last.core, last.xpeer, last.ypeer)

    def hop(n):
        return remote(small.at[n], came.at[n], small_send.at[n], small_recv.at[n], hops[n])

    hop(0).start()
    left = max(LATE, tiles + 2 * (group // QB) // BACK_EVERY) + IN_UNPROJECT
    def rest(t, carry):
        work.step(left + t - 3, *BACK_LAGS)
        last.step(t, *BACK_LAGS)
        for n in range(3):
            @pl.when(t == 3 + n)
            def _():
                hop(n).wait_recv()
                small[n + 1] = small[n] + came[n]
                if n < 2:
                    hop(n + 1).start()
                else:
                    for step in range(1, ring):
                        remote(small.at[3], far.at[step - 1], small_send.at[3], small_recv.at[3], (p, lax.rem(c + step, ring), h)).start()
        return carry
    lax.fori_loop(3, max(last.steps(*BACK_LAGS), work.steps(*BACK_LAGS) - left + 3), rest, 0)
    local_copy(far, far, small_recv.at[3]).wait()
    total = small[3]
    for step in range(1, ring):
        total = total + far[step - 1]
    small_out[...] = total
    for n in range(3):
        hop(n).wait_send()
    local_copy(far, far, small_send.at[3]).wait()
    work.drain_all(3)
    last.drain_all()


def train(x, heads, cot, gains, wide, down, kx, vx, kf, qf, qa, of, raw, cosine, sine, head_gains, ring, item, collective_id):
    rows, width = x.shape
    group, ext = 4 * rows, 4 * rows + 2 * HALF
    r, w = item
    block = (2, ring, 2, 2, r, w)
    dma = pltpu.SemaphoreType.DMA
    vm = pltpu.VMEM
    shape = jax.ShapeDtypeStruct
    return pl.pallas_call(
        functools.partial(train_kernel, ring),
        out_shape=(
            shape((rows, width), BF), shape((rows, width), F32), shape((32, r, w), F32), shape((24, 128), F32),
            shape((rows, width), F32), shape((16,) + block, BF), shape((2,) + block, BF),
            shape((2, ring, 2, 2, 4, r, 2 * w), BF), shape((6,) + block, BF)),
        in_specs=[ANY] * 3 + [VM] + [ANY] * 4 + [VM] * 2 + [ANY] * 3 + [VM] * 3,
        out_specs=(ANY, ANY, VM, VM) + (ANY,) * 5,
        scratch_shapes=[
            vm((rows, width), BF), vm((group, 256), BF), vm((2, 2, HALF, 256), BF), vm((rows, 3 * width), BF),
            vm((4, 8, QB), F32), vm((4, 8, QB), F32), vm((1, width), F32), vm((1, width), F32), vm((2, 128), F32),
            vm((4, 24, 128), F32), vm((3, 24, 128), F32), vm((ring - 1, 24, 128), F32), dma((4,)), dma((4,)),
            pltpu.SemaphoreType.REGULAR,
            dma((4, 2)), dma((2,)), dma((2,)), dma((3, 2)), dma((3, 2)), dma((2, 2, 2)), dma((2, 2, 2)),
        ] + scatter_scratch(ring, 26, r, w) + [dma((4, 6)), dma((4, 6))],
        compiler_params=pltpu.CompilerParams(collective_id=collective_id, has_side_effects=True, vmem_limit_bytes=63 * MIB),
        name="train",
    )(x, heads, cot, gains, wide, down, kx, vx, kf, qf, qa, of, raw, cosine, sine, head_gains)


def to_blocks(weight, depth, r, w):
    parts = weight.reshape(-1, depth, weight.shape[1] // 512, r // depth, w)
    return parts.transpose(2, 0, 3, 1, 4).reshape(weight.shape[1] // 512, -1, r, w)


def from_blocks(blocks, depth):
    n, (r, w) = blocks.shape[0], blocks.shape[-2:]
    return blocks.reshape(n, -1, r // depth, depth, w).swapaxes(2, 3).reshape(n, -1, 512)


def local(
    inputs, cotangent, w_qkv, w_out, w_gate, w_up, w_down, gain_attn, gain_ffn, q_gain, k_gain, head_bias,
    segment_ids, variate_ids, time_index,
):
    ring = lax.axis_size("cp")
    head = lax.axis_index("hd")
    rows, width = inputs.shape
    depth = w_qkv.shape[0]
    r, w = item_shape(depth)

    me = (lax.axis_index("pack") * ring + lax.axis_index("cp")) * 4 + head
    down_pieces = w_down.reshape(4, r, 2, w).swapaxes(1, 2).reshape(8, r, w)
    src = jnp.concatenate([to_blocks(weight, depth, r, w)[:, 0] for weight in (w_qkv, w_out, w_gate, w_up)] + [down_pieces])
    gain_src = lax.dynamic_update_slice(jnp.zeros((2, width), BF), jnp.stack([gain_attn, gain_ffn]), (0, me * depth))
    gain_src = gain_src.reshape(16, 128)

    times = lax.dynamic_slice_in_dim(time_index, head * rows, rows, 0)
    lane = jnp.arange(128)
    frequency = jnp.exp(-math.log(theta_base) * 2.0 * (lane % 32).astype(F32) / HDIM)
    angle = times.astype(F32)[:, None] * frequency[None, :]
    cosine = jnp.cos(angle)
    sine = jnp.sin(angle) * jnp.where(lane % 64 < 32, -1.0, 1.0)[None, :]
    head_gains = jnp.stack([jnp.concatenate([q_gain, q_gain]), jnp.concatenate([k_gain, k_gain])])

    qf, kf_own = features(segment_ids, variate_ids)
    hs = head_scales(lax.dynamic_slice_in_dim(head_bias, head * 4, 4, 0))

    heads_out, of, qa, kx, vx, kf, raw, gains, wide, down = attend(
        inputs, cosine, sine, head_gains, kf_own, qf, hs, src, gain_src, 24, ring, 1)
    wide = from_blocks(wide, depth)
    gains = gains.reshape(2, 1, width)
    layer_out, grad_inputs, items, small, *_ = train(
        inputs, heads_out, cotangent, gains, wide, down.reshape(-1, width), kx, vx, kf, qf, qa, of, raw,
        cosine, sine, head_gains, ring, (r, w), 2)

    def columns(part):
        return from_blocks(part, depth).swapaxes(0, 1).reshape(depth, -1)

    pairs = items[:16].reshape(8, 2, r, w)
    down_depth = w_down.shape[0] // 4
    own_down = items[18:26].reshape(4, 2, r // down_depth, down_depth, w).transpose(0, 3, 2, 1, 4).reshape(w_down.shape)
    own_gains = lax.dynamic_slice_in_dim(small[:16].reshape(2, width), me * depth, depth, 1)
    own_heads = small[16:18, :HDIM] + small[16:18, HDIM:]
    return (
        layer_out, grad_inputs, columns(items[26:]), columns(items[16:18]), columns(pairs[:, 0]), columns(pairs[:, 1]),
        own_down, own_gains[0], own_gains[1], own_heads[0], own_heads[1], small[18, :32].reshape(HEADS, 2),
    )


def solution(mesh):
    return jax.shard_map(
        local,
        mesh=mesh,
        in_specs=(
            P(("pack", "cp", "hd"), None),
            P(("pack", "cp", "hd"), None),
            P(("pack", "cp", "hd"), None),
            P(("pack", "cp", "hd"), None),
            P(("pack", "cp", "hd"), None),
            P(("pack", "cp", "hd"), None),
            P(("pack", "cp", "hd"), None),
            P(("pack", "cp", "hd")),
            P(("pack", "cp", "hd")),
            P(),
            P(),
            P(),
            P(("pack", "cp")),
            P(("pack", "cp")),
            P(("pack", "cp")),
        ),
        out_specs=(
            P(("pack", "cp", "hd"), None),
            P(("pack", "cp", "hd"), None),
            P(("pack", "cp", "hd"), None),
            P(("pack", "cp", "hd"), None),
            P(("pack", "cp", "hd"), None),
            P(("pack", "cp", "hd"), None),
            P(("pack", "cp", "hd"), None),
            P(("pack", "cp", "hd")),
            P(("pack", "cp", "hd")),
            P(),
            P(),
            P(),
        ),
        check_vma=False,
    )
```

```python
import functools
import math

import jax
import jax.numpy as jnp
from jax import lax
from jax.experimental import pallas as pl
from jax.experimental.pallas import tpu as pltpu
from jax.sharding import PartitionSpec as P

HEADS = 16
HDIM = 64
HALF = 512
QB = 256
SPAN = QB + 2 * HALF
FAR = -1e30
EPS = 1e-6
theta_base = 10000.0
MIB = 2**20
F32, BF = jnp.float32, jnp.bfloat16
MESH = pl.DeviceIdType.MESH
VM = pl.BlockSpec(memory_space=pltpu.VMEM)
ANY = pl.BlockSpec(memory_space=pl.ANY)
ALL = slice(None)


def item_shape(rows):
    full = max(rows, 16)
    return full, rows * 512 // full


def place():
    return lax.axis_index("pack"), lax.axis_index("cp"), lax.axis_index("hd")


def greet(peers):
    barrier = pltpu.get_barrier_semaphore()
    for peer in peers:
        pl.semaphore_signal(barrier, inc=1, device_id=peer, device_id_type=MESH)
    pl.semaphore_wait(barrier, len(peers))


def group_peers(ring):
    p, c, h = place()
    peers = [(1 - p, c, h), (p, c, h + 1 - 2 * lax.rem(h, 2)), (p, c, lax.rem(h + 2, 4))]
    peers += [(p, lax.rem(c + step, ring), h) for step in range(1, ring)]
    return peers


class Scatter:
    def __init__(self, ring, count, middle, pick, buffers, sems, write):
        self.ring, self.count, self.middle, self.pick, self.write = ring, count, middle, pick, write
        self.load, self.own, self.b1, self.tail = buffers
        self.slots = self.load.shape[0]
        self.load_sem, self.send_sem, self.recv_sem = sems
        self.p, self.c, self.h = place()
        self.hy, self.hx = self.h // 2, lax.rem(self.h, 2)
        self.core = (1 - self.p, self.c, self.h)
        self.xpeer = (self.p, self.c, self.hy * 2 + 1 - self.hx)
        self.ypeer = (self.p, self.c, (1 - self.hy) * 2 + self.hx)

    def remote(self, i, stage, src, dst, device):
        return pltpu.make_async_remote_copy(
            src_ref=src, dst_ref=dst, send_sem=self.send_sem.at[stage, i],
            recv_sem=self.recv_sem.at[stage, i], device_id=device, device_id_type=MESH)

    def wait_for(self, ref, sem):
        pltpu.make_async_copy(ref, ref, sem).wait()

    def near(self, first_y):
        return self.ypeer if first_y else self.xpeer

    def spot(self, i, first_y, k):
        return (i, self.hy, k) if first_y else (i, k, self.hx)

    def copy0(self, i, src):
        return self.remote(i, 0, src, self.own.at[i], self.core)

    def copy1(self, i, first_y):
        src = self.own.at[i, :, 1 - self.hy] if first_y else self.own.at[i, :, :, 1 - self.hx]
        return self.remote(i, 1, src, self.b1.at[i], self.near(first_y))

    def half(self, i, first_y):
        return self.own.at[i, :, self.hy, 1 - self.hx] if first_y else self.own.at[i, :, 1 - self.hy, self.hx]

    def begin(self, i, first_y, mid):
        def go(mine, other):
            slot = lax.rem(i, self.slots)
            pltpu.make_async_copy(mine, self.load.at[slot], self.load_sem.at[slot]).start()
            self.copy0(i, other).start()
        self.pick(i, self.p, go)

    def stage1(self, i, first_y, mid):
        slot = lax.rem(i, self.slots)
        self.wait_for(self.load.at[slot], self.load_sem.at[slot])
        self.copy0(i, self.own.at[i]).wait_recv()
        def add(k, carry):
            self.own[i, k] = self.own[i, k] + self.load[slot, k]
            return carry
        lax.fori_loop(0, self.ring, add, 0)
        self.copy1(i, first_y).start()

    def stage2(self, i, first_y, mid):
        self.copy1(i, first_y).wait_recv()
        def add(k, carry):
            for m in range(2):
                at = (i, k, self.hy, m) if first_y else (i, k, m, self.hx)
                self.own[at] = self.own[at] + self.b1[i, k, m]
            return carry
        lax.fori_loop(0, self.ring, add, 0)
        if not mid:
            self.remote(i, 2, self.half(i, first_y), self.tail.at[i, pl.ds(0, self.ring)], self.near(not first_y)).start()
            return
        for step in range(1, self.ring):
            peer = lax.rem(self.c + step, self.ring)
            src = self.own.at[i, peer, self.hy] if first_y else self.own.at[i, peer, :, self.hx]
            self.remote(i, 2, src, self.tail.at[i, pl.ds(2 * step - 2, 2)], (self.p, peer, self.h)).start()

    def second(self, i, mid):
        return self.tail.at[i, pl.ds(0, 2 * self.ring - 2 if mid else self.ring)]

    def third(self, i, mid):
        return self.tail.at[i, pl.ds(2 * self.ring - 2, 1) if mid else pl.ds(self.ring, self.ring - 1)]

    def stage3(self, i, first_y, mid):
        self.wait_for(self.second(i, mid), self.recv_sem.at[2, i])
        if mid:
            for k in range(2):
                at = (i, self.c, self.hy, k) if first_y else (i, self.c, k, self.hx)
                total = self.own[at].astype(jnp.float32)
                for step in range(1, self.ring):
                    total = total + self.tail[i, 2 * step - 2 + k].astype(jnp.float32)
                self.own[at] = total.astype(jnp.bfloat16)
            last = (self.hy, pl.ds(1 - self.hx, 1)) if first_y else (pl.ds(1 - self.hy, 1), self.hx)
            self.remote(i, 3, self.own.at[(i, self.c) + last], self.third(i, mid), self.near(not first_y)).start()
            return
        def add(k, carry):
            at = (i, k, self.hy, self.hx)
            self.own[at] = self.own[at] + self.tail[i, k]
            return carry
        lax.fori_loop(0, self.ring, add, 0)
        for step in range(1, self.ring):
            peer = lax.rem(self.c + step, self.ring)
            self.remote(i, 3, self.own.at[i, peer, self.hy, self.hx], self.tail.at[i, self.ring + step - 1], (self.p, peer, self.h)).start()

    def finish(self, i, first_y, mid):
        self.wait_for(self.third(i, mid), self.recv_sem.at[3, i])
        total = self.own[i, self.c, self.hy, self.hx].astype(jnp.float32)
        for n in range(2 * self.ring - 2 if mid else self.ring, 2 * self.ring - 1):
            total = total + self.tail[i, n].astype(jnp.float32)
        self.write(i, total)

    def drain(self, i, first_y, mid):
        self.copy0(i, self.own.at[i]).wait_send()
        self.copy1(i, first_y).wait_send()
        self.wait_for(self.second(i, mid), self.send_sem.at[2, i])
        self.wait_for(self.third(i, mid), self.send_sem.at[3, i])

    def both(self, pair, act):
        middle = self.middle(pair)
        for first_y in (True, False):
            i = 2 * pair + (0 if first_y else 1)
            there = (pair >= 0) & (i < self.count)
            pl.when(there & middle)(functools.partial(act, i, first_y, True))
            pl.when(there & jnp.logical_not(middle))(functools.partial(act, i, first_y, False))

    def step(self, t, ahead=1, lags=(0, 1, 2, 3)):
        self.both(t, self.begin)
        self.both(t - ahead - lags[0], self.stage1)
        self.both(t - ahead - lags[1], self.stage2)
        self.both(t - ahead - lags[2], self.stage3)
        self.both(t - ahead - lags[3], self.finish)

    def steps(self, ahead=1, lags=(0, 1, 2, 3)):
        return (self.count + 1) // 2 + ahead + lags[3]

    def drain_all(self, first=0, last=None):
        def one(t, carry):
            self.both(t, self.drain)
            return carry
        lax.fori_loop(first, (self.count + 1) // 2 if last is None else last, one, 0)


def scatter_scratch(ring, count, rows, cols):
    bf = jnp.bfloat16
    return [
        pltpu.VMEM((4, ring, 2, 2, rows, cols), bf),
        pltpu.VMEM((count, ring, 2, 2, rows, cols), bf),
        pltpu.VMEM((count, ring, 2, rows, cols), bf),
        pltpu.VMEM((count, 2 * ring - 1, rows, cols), bf),
        pltpu.SemaphoreType.DMA((4,)),
        pltpu.SemaphoreType.DMA((4, count)),
        pltpu.SemaphoreType.DMA((4, count)),
    ]


def scatter_pick(grads, layout, cols):
    def pick(i, p, go):
        start = 0
        for ref, (size, outer) in zip(grads, layout):
            j = i - start
            def run(ref=ref, j=j, outer=outer):
                if outer:
                    go(ref.at[j, p], ref.at[j, 1 - p])
                else:
                    at = pl.ds(pl.multiple_of(lax.rem(j, 2) * cols, cols), cols)
                    go(ref.at[p, :, :, :, j // 2, :, at], ref.at[1 - p, :, :, :, j // 2, :, at])
            pl.when((j >= 0) & (j < size))(run)
            start += size
    return pick


class Gather:
    def __init__(self, ring, count, pick, sems):
        self.ring, self.count, self.pick = ring, count, pick
        self.local_sem, self.send_sem, self.recv_sem = sems
        self.p, self.c, self.h = place()
        self.hy, self.hx = self.h // 2, lax.rem(self.h, 2)
        self.core = (1 - self.p, self.c, self.h)
        self.xpeer = (self.p, self.c, self.hy * 2 + 1 - self.hx)
        self.ypeer = (self.p, self.c, (1 - self.hy) * 2 + self.hx)

    def remote(self, i, stage, src, dst, device):
        return pltpu.make_async_remote_copy(
            src_ref=src, dst_ref=dst, send_sem=self.send_sem.at[stage, i],
            recv_sem=self.recv_sem.at[stage, i], device_id=device, device_id_type=MESH)

    def same(self, i, stage, ref, device):
        return self.remote(i, stage, ref, ref, device)

    def begin(self, i, first_x, mid):
        def go(src, out):
            mine = out(self.p, self.c, self.hy, self.hx)
            pltpu.make_async_copy(src, mine, self.local_sem.at[i]).start()
            if mid:
                self.remote(i, 0, src, mine, self.near(first_x)).start()
                return
            for step in range(1, self.ring):
                peer = (self.p, lax.rem(self.c + step, self.ring), self.h)
                self.remote(i, 0, src, mine, peer).start()
        self.pick(i, go, True)

    def near(self, first_x):
        return self.xpeer if first_x else self.ypeer

    def block(self, out, first_x, mine):
        if first_x:
            return out(self.p, self.c, self.hy, self.hx if mine else 1 - self.hx)
        return out(self.p, self.c, self.hy if mine else 1 - self.hy, self.hx)

    def couple(self, out, first_x, at):
        return out(self.p, at, self.hy, ALL) if first_x else out(self.p, at, ALL, self.hx)

    def wait_for(self, ref, sem):
        pltpu.make_async_copy(ref, ref, sem).wait()

    def stage1(self, i, first_x, mid):
        def go(src, out):
            mine = out(self.p, self.c, self.hy, self.hx)
            self.wait_for(mine, self.local_sem.at[i])
            if mid:
                self.same(i, 0, self.block(out, first_x, False), self.core).wait_recv()
                both = self.couple(out, first_x, self.c)
                for step in range(1, self.ring):
                    self.same(i, 1, both, (self.p, lax.rem(self.c + step, self.ring), self.h)).start()
                return
            self.wait_for(out(self.p, pl.ds(0, self.ring - 1), self.hy, self.hx), self.recv_sem.at[0, i])
            column = out(self.p, ALL, self.hy, self.hx)
            self.same(i, 1, column, self.near(first_x)).start()
            self.same(i, 3, column, self.core).start()
        self.pick(i, go)

    def first(self, out, mine, first_x):
        if first_x:
            return out(self.p, ALL, self.hy, self.hx if mine else 1 - self.hx)
        return out(self.p, ALL, self.hy if mine else 1 - self.hy, self.hx)

    def second(self, out, mine, first_x):
        if first_x:
            return out(self.p, ALL, self.hy if mine else 1 - self.hy, ALL)
        return out(self.p, ALL, ALL, self.hx if mine else 1 - self.hx)

    def stage2(self, i, first_x, mid):
        def go(src, out):
            half = self.second(out, True, first_x)
            if mid:
                self.wait_for(self.couple(out, first_x, pl.ds(0, self.ring - 1)), self.recv_sem.at[1, i])
                self.same(i, 2, half, self.near(not first_x)).start()
                self.same(i, 3, half, self.core).start()
                return
            came = self.first(out, False, first_x)
            self.same(i, 1, came, self.core).wait_recv()
            self.same(i, 2, half, self.near(not first_x)).start()
            self.same(i, 3, came, self.core).start()
        self.pick(i, go)

    def stage3(self, i, first_x, mid):
        def go(src, out):
            came = self.second(out, False, first_x)
            self.same(i, 2, came, self.core).wait_recv()
            self.same(i, 3, came, self.core).start()
        self.pick(i, go)

    def finish(self, i, first_x, mid):
        def go(src, out):
            self.wait_for(out(1 - self.p, ALL, ALL, ALL), self.recv_sem.at[3, i])
        self.pick(i, go)

    def drain(self, i, first_x, mid):
        def go(src, out):
            if mid:
                self.same(i, 0, self.block(out, first_x, True), self.core).wait_send()
                self.wait_for(self.couple(out, first_x, pl.ds(0, self.ring - 1)), self.send_sem.at[1, i])
            else:
                self.wait_for(out(self.p, pl.ds(0, self.ring - 1), self.hy, self.hx), self.send_sem.at[0, i])
                self.same(i, 1, self.first(out, True, first_x), self.core).wait_send()
            self.same(i, 2, self.second(out, True, first_x), self.core).wait_send()
            self.wait_for(out(self.p, ALL, ALL, ALL), self.send_sem.at[3, i])
        self.pick(i, go)

    def both(self, pair, act):
        middle = lax.rem(pair, 2) != 0
        for first_x in (True, False):
            i = 2 * pair + (0 if first_x else 1)
            there = (pair >= 0) & (i < self.count) & (i >= 0)
            pl.when(there & middle)(functools.partial(act, i, first_x, True))
            pl.when(there & jnp.logical_not(middle))(functools.partial(act, i, first_x, False))

    def step(self, t, ahead=2, lags=(0, 1, 2, 3)):
        self.both(t, self.begin)
        self.both(t - ahead - lags[0], self.stage1)
        self.both(t - ahead - lags[1], self.stage2)
        self.both(t - ahead - lags[2], self.stage3)
        self.both(t - ahead - lags[3], self.finish)

    def steps(self, ahead=2, lags=(0, 1, 2, 3)):
        return (self.count + 1) // 2 + ahead + lags[3]

    def drain_all(self):
        def one(t, carry):
            self.both(t, self.drain)
            return carry
        lax.fori_loop(0, (self.count + 1) // 2, one, 0)


def gather_sems(count):
    return [
        pltpu.SemaphoreType.DMA((count,)),
        pltpu.SemaphoreType.DMA((4, count)),
        pltpu.SemaphoreType.DMA((4, count)),
    ]


def gather_pick(srcs, wide, down, n_wide, cols):
    def pick(i, go, source=False):
        def in_wide(src):
            go(src, lambda p, c, y, x: wide.at[i, p, c, y, x])
        def in_down(src):
            j = i - n_wide
            at = pl.ds(pl.multiple_of(lax.rem(j, 2) * cols, cols), cols)
            go(src, lambda p, c, y, x: down.at[p, c, y, x, j // 2, :, at])
        if len(srcs) == 1 or not source:
            pl.when(i < n_wide)(lambda: in_wide(srcs[0].at[i] if source else None))
            pl.when(i >= n_wide)(lambda: in_down(srcs[0].at[i] if source else None))
            return
        start = 0
        for ref in srcs[:-1]:
            n = ref.shape[1] // cols
            @pl.when((i >= start) & (i < start + n))
            def _():
                in_wide(ref.at[:, pl.ds(pl.multiple_of((i - start) * cols, cols), cols)])
            start += n
        @pl.when(i >= n_wide)
        def _():
            j = i - n_wide
            rows = srcs[-1].shape[0] // 4
            at = pl.ds(pl.multiple_of(j // 2 * rows, rows), rows)
            in_down(srcs[-1].at[at, pl.ds(pl.multiple_of(lax.rem(j, 2) * cols, cols), cols)])
    return pick


def dot_tb(a, b):
    return lax.dot_general(a, b, (((1,), (1,)), ((), ())), preferred_element_type=jnp.float32)


def dot(a, b):
    return jnp.dot(a, b, preferred_element_type=jnp.float32)


def lanes(rows):
    return lax.broadcasted_iota(jnp.int32, (rows, 128), 1)


def split3(x):
    hi = x.astype(jnp.bfloat16).astype(jnp.float32)
    mid = (x - hi).astype(jnp.bfloat16).astype(jnp.float32)
    lo = x - hi - mid
    return hi, mid, lo


def at_lanes(base, first, values):
    lane = lanes(base.shape[0])
    for n, value in enumerate(values):
        base = jnp.where(lane == first + n, value, base)
    return base


def halves(x):
    return x, pltpu.roll(x, 64, 1)


def build_keys(pair, k_ref, v_ref, kf_ref, ka, va, kt=None, first=0, last=None):
    at = pl.ds(pl.multiple_of(pair * 128, 128), 128)
    rows = k_ref.shape[0]
    chunk = 512
    def one(n, carry):
        r = pl.ds(pl.multiple_of(n * chunk, chunk), chunk)
        lane = lanes(chunk)
        keys = halves(k_ref[r, at].astype(jnp.float32))
        values = halves(v_ref[r, at].astype(jnp.float32))
        feat = kf_ref[r, :].astype(jnp.float32)
        for m in range(2):
            full = jnp.where(lane < 64, keys[m], feat)
            ka[m, r, :] = full.astype(jnp.bfloat16)
            if kt is not None:
                kt[m, :, r] = full.T.astype(jnp.bfloat16)
            ones = jnp.where(lane < 67, 1.0, 0.0)
            va[m, r, :] = jnp.where(lane < 64, values[m], ones).astype(jnp.bfloat16)
        return carry
    lax.fori_loop(first, rows // chunk if last is None else last, one, 0)


def forward_block(pair, n, q_ref, qf_ref, hs_ref, ka, va, o_ref, of_ref, qa_ref):
    at = pl.ds(pl.multiple_of(pair * 128, 128), 128)
    r = pl.ds(pl.multiple_of(n * QB, QB), QB)
    lane = lanes(QB)
    queries = halves(q_ref[r, at].astype(jnp.float32) * (1.0 / math.sqrt(HDIM)))
    feat = qf_ref[r, :].astype(jnp.float32)
    row = lax.broadcasted_iota(jnp.int32, (QB, QB), 0)
    col = lax.broadcasted_iota(jnp.int32, (QB, QB), 1)
    outs = []
    for m in range(2):
        qa = jnp.where(lane < 64, queries[m], feat * hs_ref[pl.ds(pair * 2 + m, 1), :])
        qb = qa.astype(jnp.bfloat16)
        def part(first, size, mask=None):
            keys = pl.ds(pl.multiple_of(n * QB + first, QB), size)
            s = dot_tb(qb, ka[m, keys, :])
            if mask is not None:
                s = jnp.where(mask, s, FAR)
            return dot(jnp.exp(s).astype(jnp.bfloat16), va[m, keys, :])
        o = part(0, QB, col >= row) + part(QB, SPAN - 2 * QB) + part(SPAN - QB, QB, col <= row)
        total = o[:, 64:65]
        outs.append(o * (1.0 / total))
        hi, mid, lo = split3(-jnp.log(total))
        qa_ref[pair * 2 + m, r, :] = at_lanes(qa, 80, (hi, mid, lo)).astype(jnp.bfloat16)
    both = jnp.where(lane < 64, outs[0], pltpu.roll(outs[1], 64, 1))
    of_ref[r, at] = both
    o_ref[r, at] = both.astype(jnp.bfloat16)


def backward_block(pair, n, qf_ref, qa_ref, do_ref, of_ref, ka, va, kt, dka, dva, dq_ref, same, every):
    at = pl.ds(pl.multiple_of(pair * 128, 128), 128)
    r = pl.ds(pl.multiple_of(n * QB, QB), QB)
    lane = lanes(QB)
    grads = do_ref[r, at].astype(jnp.float32)
    terms = grads * of_ref[r, :]
    pieces = halves(grads)
    row = lax.broadcasted_iota(jnp.int32, (QB, QB), 0)
    col = lax.broadcasted_iota(jnp.int32, (QB, QB), 1)
    dqs = []
    qft = qf_ref[r, :].astype(jnp.float32).T[64:72, :]
    for m in range(2):
        own = (lane < 64) if m == 0 else (lane >= 64)
        delta = jnp.sum(jnp.where(own, terms, 0.0), axis=1, keepdims=True)
        da = at_lanes(jnp.where(lane < 64, pieces[m], 0.0), 64, split3(-delta)).astype(jnp.bfloat16)
        qb = qa_ref[m, r, :]
        dq = jnp.zeros((128, QB), jnp.float32)
        for first, size, edge in ((0, QB, 0), (QB, SPAN - 2 * QB, None), (SPAN - QB, QB, 1)):
            keys = pl.ds(pl.multiple_of(n * QB + first, QB), size)
            s = dot_tb(ka[m, keys, :], qb)
            if edge is not None:
                s = jnp.where((row >= col) if edge == 0 else (row <= col), s, FAR)
            p = jnp.exp(s)
            dp = dot_tb(va[m, keys, :], da)
            ds = (p * dp).astype(jnp.bfloat16)
            dva[m, keys, :] += dot(p.astype(jnp.bfloat16), da)
            dka[m, keys, :] += dot(ds, qb)
            dq = dq + dot(kt[m, :, keys], ds)
        dqs.append(dq[:64, :])
        sums = dq[64:72, :]
        pick = lax.broadcasted_iota(jnp.int32, (8, QB), 0) < 4
        h = pair * 2 + m
        same[h] += jnp.where(pick, sums * qft, 0.0)
        every[h] += jnp.where(pick, sums, 0.0)
    dq_ref[r, at] = (jnp.concatenate(dqs, axis=0).T * (1.0 / math.sqrt(HDIM))).astype(dq_ref.dtype)


def backward_finish(pair, dka, dva, dk_ref, dv_ref):
    at = pl.ds(pl.multiple_of(pair * 128, 128), 128)
    chunk = 512
    def one(n, carry):
        r = pl.ds(pl.multiple_of(n * chunk, chunk), chunk)
        lane = lanes(chunk)
        dk_ref[r, at] = jnp.where(lane < 64, dka[0, r, :], pltpu.roll(dka[1, r, :], 64, 1)).astype(dk_ref.dtype)
        dv_ref[r, at] = jnp.where(lane < 64, dva[0, r, :], pltpu.roll(dva[1, r, :], 64, 1)).astype(dv_ref.dtype)
        return carry
    lax.fori_loop(0, dk_ref.shape[0] // chunk, one, 0)


def features(seg, var):
    lane = jnp.arange(128)[None, :]
    same = (var[:, None] == (lane - 64) % 4) & (lane >= 64) & (lane < 76)
    doc = (lane >= 76) & (lane < 80)
    here = seg[:, None] == lane - 76
    keys = jnp.where(doc & ~here, FAR, jnp.where(same | ((lane >= 80) & (lane < 83)), 1.0, 0.0))
    queries = jnp.where(same | (doc & here), 1.0, 0.0)
    return queries.astype(jnp.bfloat16), keys.astype(jnp.bfloat16)


def head_scales(bias):
    hi, mid, lo = split3(bias[:, :1] - bias[:, 1:])
    lane = jnp.arange(128)[None, :]
    parts = jnp.where(lane < 68, hi, jnp.where(lane < 72, mid, lo))
    return jnp.where(lane < 64, 0.0, jnp.where(lane < 76, parts, jnp.where(lane < 80, 1.0, 0.0)))


def scale_of(x):
    return lax.rsqrt(jnp.mean(x * x, axis=-1, keepdims=True) + EPS)


def head_mean(x):
    row = lax.broadcasted_iota(jnp.int32, (128, 128), 0)
    col = lax.broadcasted_iota(jnp.int32, (128, 128), 1)
    group = jnp.where((row < 64) == (col < 64), 1.0 / HDIM, 0.0).astype(BF)
    hi = x.astype(BF)
    rest = x - hi.astype(F32)
    mid = rest.astype(BF)
    low = (rest - mid.astype(F32)).astype(BF)
    return dot(hi, group) + dot(mid, group) + dot(low, group)


def swap_halves(x):
    lane = lax.rem(lanes(x.shape[0]), 64)
    return jnp.where(lane < 32, pltpu.roll(x, 96, 1), pltpu.roll(x, 32, 1))


def norm_back_rows(u, r, gain, dy):
    scaled = dy * gain
    du = r * scaled - u * (r * r * r) * jnp.mean(scaled * u, axis=-1, keepdims=True)
    return du, jnp.sum(dy * u * r, axis=0, keepdims=True)


def as_blocks(value, shape):
    rows, cols = shape[-2:]
    if cols == value.shape[1]:
        return value.astype(BF).reshape(shape)
    depth = rows * cols // value.shape[1]
    parts = value.reshape(-1, depth, value.shape[1])
    parts = [parts[:, :, n:n + cols] for n in range(0, value.shape[1], cols)]
    return jnp.concatenate(parts, axis=1).astype(BF).reshape(shape)


def remote(src, dst, send, recv, device):
    return pltpu.make_async_remote_copy(
        src_ref=src, dst_ref=dst, send_sem=send, recv_sem=recv, device_id=device, device_id_type=MESH)


def local_copy(src, dst, sem):
    return pltpu.make_async_copy(src, dst, sem)


def wide_at(first):
    return pl.ds(pl.multiple_of(first, 256), 256)


class Rim:
    def __init__(self, ring):
        self.p, self.c, self.h = place()
        self.ring = ring
        self.has_low, self.has_high = self.c > 0, self.c < ring - 1
        self.low = lax.rem(self.c + ring - 1, ring)
        self.high = lax.rem(self.c + 1, ring)
        self.low_edge = self.has_low & (self.h == 0)
        self.high_edge = self.has_high & (self.h == 3)

    def greet(self):
        beyond = [(self.p, block, n) for block in (self.low, self.high) for n in range(4)]
        greet(group_peers(self.ring) + [(self.p, self.c, 3 - self.h)] + beyond)


def pair_at(first, pair):
    return pl.ds(pl.multiple_of(first + pair * 128, 128), 128)


LAGS = (2, (0, 1, 2, 3))
FIRST = LAGS[0] + LAGS[1][3]
EXTRA = 2
EVERY = 4


def as_matrix(value):
    rows, cols = value.shape[-2:]
    if cols == 512:
        return value.reshape(-1, 512)
    depth = rows * cols // 512
    parts = value.astype(F32).reshape(-1, rows, cols)
    parts = [parts[:, n:n + depth] for n in range(0, rows, depth)]
    return jnp.concatenate(parts, axis=2).reshape(-1, 512).astype(BF)


def attend_kernel(ring, n_wide, count, n_src, x_ref, cos_ref, sin_ref, hg_ref, kf_own, qf_ref, hs_ref, gain_src, *refs):
    (tok_ref, of_ref, qa_ref, kx, vx, kf_ref, raw_ref, gain_ref, wide, down,
                  rot, nrm, w_tile, gains, q_loc, o_loc, ka, va, tile_sem, local_sem, a2a_send, a2a_recv, rim_send, rim_recv,
                  kf_send, kf_recv, out_send, out_recv, *sems) = refs[n_src:]
    p, c, h = place()
    rim = Rim(ring)
    greet(group_peers(ring) + [(p, c, 3 - h)])
    rows, width = tok_ref.shape
    group = 4 * rows
    mine = pl.ds(pl.multiple_of(h * rows, rows), rows)
    mine_x = pl.ds(pl.multiple_of(HALF + h * rows, rows), rows)
    places = ((0, q_loc, mine), (1, kx, mine_x), (2, vx, mine_x))
    three = pl.ds(0, 3 * rows)
    sides = ((rim.has_high, rim.high, group, 0), (rim.has_low, rim.low, HALF, HALF + group))

    small = Gather(ring, 1, lambda i, go, source=False: go(gain_src, lambda p, c, y, x: gains.at[p, c, y, x]), sems[:3])
    work = Gather(ring, count, gather_pick(refs[:n_src], wide, down, n_wide, wide.shape[-1]), sems[3:])

    def kf_copy(side):
        there, block, first, to = sides[side]
        return remote(kf_own.at[pl.ds(first - HALF * side if side else first - HALF, HALF)], kf_ref.at[pl.ds(to, HALF)],
                      kf_send.at[side], kf_recv.at[side], (p, block, h))

    def begin(t, carry):
        small.step(t, *LAGS)
        work.step(t, *LAGS)
        return carry
    lax.fori_loop(0, 2, begin, 0)
    for side in range(2):
        pl.when(sides[side][0])(lambda: kf_copy(side).start())
    kf_ref[HALF:HALF + group, :] = kf_own[...]
    lane = lax.broadcasted_iota(jnp.int32, (HALF, 128), 1)
    nothing = jnp.where((lane >= 76) & (lane < 80), FAR, 0.0).astype(BF)
    @pl.when(jnp.logical_not(rim.has_low))
    def _():
        kf_ref[0:HALF, :] = nothing
        for ref in (kx, vx):
            ref[0:HALF, :] = jnp.zeros((HALF, 256), BF)
    @pl.when(jnp.logical_not(rim.has_high))
    def _():
        kf_ref[HALF + group:2 * HALF + group, :] = nothing
        for ref in (kx, vx):
            ref[HALF + group:2 * HALF + group, :] = jnp.zeros((HALF, 256), BF)
    lax.fori_loop(2, FIRST, begin, 0)

    def share(kind, head, pair):
        ref, at = places[kind][1:]
        cols = pair_at(0, pair)
        part = rot.at[:, pair_at(kind * width + head * 256, pair)]
        there = ref.at[at, cols]
        @pl.when(head == h)
        def _():
            local_copy(part, there, local_sem.at[kind, pair]).start()
        @pl.when(head != h)
        def _():
            remote(part, there, a2a_send.at[kind, pair], a2a_recv.at[kind, pair], (p, c, head)).start()

    def tile_copy(t):
        return local_copy(wide.at[t], w_tile.at[lax.rem(t, 2)], tile_sem.at[lax.rem(t, 2)])

    for k in range(3):
        begin(FIRST + k, 0)
        for m in range(2):
            tile_copy(2 * k + m).start()
        if k == 0:
            total = gains[0, 0, 0, 0].astype(F32)
            for d in range(1, 8 * ring):
                total = total + gains[d // (4 * ring), d // 4 % ring, d // 2 % 2, d % 2].astype(F32)
            gain_ref[...] = total
            def norm(n, carry):
                at = pl.ds(pl.multiple_of(n * 128, 128), 128)
                x = x_ref[at, :].astype(F32)
                y = x * scale_of(x)
                for m in range(width // 128):
                    part = slice(m * 128, (m + 1) * 128)
                    nrm[at, part] = (y[:, part] * total[m:m + 1, :]).astype(BF)
                return carry
            lax.fori_loop(0, rows // 128, norm, 0)
        for m in range(2):
            t = 2 * k + m
            tile_copy(t).wait()
            def project(n, carry):
                at = pl.ds(pl.multiple_of(n * 128, 128), 128)
                raw = dot(nrm[at, :], as_matrix(w_tile[t % 2])).astype(BF)
                if t < 4:
                    raw_ref[at, t * 512:(t + 1) * 512] = raw
                    gain = hg_ref[t // 2:t // 2 + 1, :]
                    for m in range(4):
                        u = raw[:, m * 128:(m + 1) * 128].astype(F32)
                        y = u * lax.rsqrt(head_mean(u * u) + EPS) * gain
                        y = y * cos_ref[at, :] + swap_halves(y) * sin_ref[at, :]
                        rot[at, t * 512 + m * 128:t * 512 + (m + 1) * 128] = y.astype(BF)
                else:
                    rot[at, t * 512:(t + 1) * 512] = raw
                return carry
            lax.fori_loop(0, rows // 128, project, 0)
            for pair in range(2):
                for m2 in range(2):
                    share(t // 2, t % 2 * 2 + m2, pair)

    def rim_copy(ref, side, kind, pair):
        there, block, first, to = sides[side]
        return remote(ref.at[pl.ds(first, HALF), pair_at(0, pair)], ref.at[pl.ds(to, HALF), pair_at(0, pair)],
                      rim_send.at[side, kind, pair], rim_recv.at[side, kind, pair], (p, block, h))

    blocks = group // QB
    margin = HALF // QB
    def more(t, carry):
        work.step(t, *LAGS)
        return carry
    lax.fori_loop(FIRST + 3, FIRST + 3 + EXTRA, more, 0)
    def pair_step(pair, carry):
        cols = pair_at(0, pair)
        for kind, ref, at in places:
            local_copy(ref.at[at, cols], ref.at[at, cols], local_sem.at[kind, pair]).wait()
            local_copy(ref.at[three, cols], ref.at[three, cols], a2a_recv.at[kind, pair]).wait()
        for side in range(2):
            @pl.when(sides[side][0])
            def _():
                for kind, ref in ((0, kx), (1, vx)):
                    rim_copy(ref, side, kind, pair).start()
        build_keys(pair, kx, vx, kf_ref, ka, va, None, 1, 1 + group // HALF)
        def step(n, c):
            @pl.when(lax.rem(n, EVERY) == 0)
            def _():
                work.step(FIRST + 3 + EXTRA + (pair * blocks + n) // EVERY, *LAGS)
            forward_block(pair, lax.rem(n + margin, blocks), q_loc, qf_ref, hs_ref, ka, va, o_loc, of_ref, qa_ref)
            return c
        lax.fori_loop(0, blocks - 2 * margin, step, 0)
        for side in range(2):
            @pl.when(sides[1 - side][0])
            def _():
                for kind, ref in ((0, kx), (1, vx)):
                    rim_copy(ref, side, kind, pair).wait_recv()
                pl.when(pair == 0)(lambda: kf_copy(side).wait_recv())
        build_keys(pair, kx, vx, kf_ref, ka, va, None, 0, 1)
        build_keys(pair, kx, vx, kf_ref, ka, va, None, 1 + group // HALF, 2 + group // HALF)
        lax.fori_loop(blocks - 2 * margin, blocks, step, 0)
        to_cols = pair_at(h * 256, pair)
        local_copy(o_loc.at[mine, cols], tok_ref.at[:, to_cols], local_sem.at[3, pair]).start()
        for step_ in range(1, 4):
            to = lax.rem(h + step_, 4)
            theirs = pl.ds(pl.multiple_of(to * rows, rows), rows)
            remote(o_loc.at[theirs, cols], tok_ref.at[:, to_cols], out_send.at[pair], out_recv.at[pair], (p, c, to)).start()
        return carry
    lax.fori_loop(0, 2, pair_step, 0)

    done = FIRST + 3 + EXTRA + 2 * blocks // EVERY
    lax.fori_loop(done, max(done, work.steps(*LAGS)), more, 0)
    for pair in range(2):
        cols = pair_at(0, pair)
        local_copy(o_loc.at[mine, cols], tok_ref.at[:, pair_at(h * 256, pair)], local_sem.at[3, pair]).wait()
        part = tok_ref.at[:, pl.ds(0, 384)]
        local_copy(part, part, out_recv.at[pair]).wait()
        local_copy(part, part, out_send.at[pair]).wait()
        for kind, ref, at in places:
            local_copy(ref.at[three, cols], ref.at[three, cols], a2a_send.at[kind, pair]).wait()
        for side in range(2):
            @pl.when(sides[side][0])
            def _():
                for kind, ref in ((0, kx), (1, vx)):
                    rim_copy(ref, side, kind, pair).wait_send()
                if pair == 0:
                    kf_copy(side).wait_send()
    small.drain_all()
    work.drain_all()


def attend(x, cosine, sine, head_gains, kf, qf, hs, srcs, gain_src, item, n_wide, count, ring, collective_id):
    rows, width = x.shape
    group = 4 * rows
    ext = group + 2 * HALF
    r, w = item
    dma = pltpu.SemaphoreType.DMA
    return pl.pallas_call(
        functools.partial(attend_kernel, ring, n_wide, count, len(srcs)),
        out_shape=(
            jax.ShapeDtypeStruct((rows, width), BF),
            jax.ShapeDtypeStruct((group, 256), F32),
            jax.ShapeDtypeStruct((4, group, 128), BF),
            jax.ShapeDtypeStruct((ext, 256), BF),
            jax.ShapeDtypeStruct((ext, 256), BF),
            jax.ShapeDtypeStruct((ext, 128), BF),
            jax.ShapeDtypeStruct((rows, 2 * width), BF),
            jax.ShapeDtypeStruct((16, 128), F32),
            jax.ShapeDtypeStruct((n_wide, 2, ring, 2, 2, r, w), BF),
            jax.ShapeDtypeStruct((2, ring, 2, 2, (count - n_wide) // 2, r, 2 * w), BF),
        ),
        in_specs=[VM] * 7 + [ANY] * (1 + len(srcs)),
        out_specs=(VM,) * 8 + (ANY, ANY),
        scratch_shapes=[
            pltpu.VMEM((rows, 3 * width), BF), pltpu.VMEM((rows, width), BF), pltpu.VMEM((2, 2, ring, 2, 2, r, w), BF),
            pltpu.VMEM((2, ring, 2, 2, 16, 128), BF),
            pltpu.VMEM((group, 256), BF), pltpu.VMEM((group, 256), BF),
            pltpu.VMEM((2, ext, 128), BF), pltpu.VMEM((2, ext, 128), BF),
            dma((2,)), dma((4, 2)), dma((3, 2)), dma((3, 2)), dma((2, 2, 2)), dma((2, 2, 2)), dma((2,)), dma((2,)), dma((2,)), dma((2,)),
        ] + gather_sems(1) + gather_sems(count),
        compiler_params=pltpu.CompilerParams(collective_id=collective_id, has_side_effects=True, vmem_limit_bytes=60 * MIB),
        name="attend",
    )(x, cosine, sine, head_gains, kf, qf, hs, gain_src, *srcs)


BACK_LAGS = (1, (0, 1, 2, 3))
BACK_EVERY = 8
LATE = 12
IN_UNPROJECT = 2


def down_blocks(value, shape):
    rows, cols = shape[-2:]
    if cols == value.shape[1]:
        return value.astype(BF).reshape(shape)
    depth = rows * cols // value.shape[1]
    parts = value.reshape(-1, depth, value.shape[1])
    parts = [parts[:, :, n:n + cols] for n in range(0, value.shape[1], cols)]
    return jnp.concatenate(parts, axis=1).astype(BF).reshape(shape)


def feed_phase(work, heads_hbm, cot_hbm, x_hbm, gain, wide, down, g_gu, g_go, g_gd, out_hbm, dhid_hbm, d_tok, gffn_ref,
               back, hidden, acc, dnorm, nrm_t, w_gu, w_d, stage, stage_d, in_sem, w_sem, stage_sem, out_sem):
    tiles = down.shape[0] // 512
    width = back.shape[1] // 3
    heads, cot, nrm = (back.at[:, n * width:(n + 1) * width] for n in range(3))
    spots = g_gd.shape[1] * g_gd.shape[0] // tiles

    def weights(t, slot):
        return [local_copy(wide.at[8 + t], w_gu.at[slot, 0], w_sem.at[slot, 0]),
                local_copy(wide.at[16 + t], w_gu.at[slot, 1], w_sem.at[slot, 1]),
                local_copy(down.at[pl.ds(pl.multiple_of(t * 512, 512), 512)], w_d.at[slot], w_sem.at[slot, 2])]

    def out_weight(slot):
        return [local_copy(wide.at[6 + n], w_gu.at[slot, n], w_sem.at[slot, n]) for n in range(2)]

    def staged(t):
        per = g_gd.shape[1] // spots
        return [local_copy(stage.at[0], g_gu.at[2 * t], stage_sem.at[0]),
                local_copy(stage.at[1], g_gu.at[2 * t + 1], stage_sem.at[1]),
                local_copy(stage_d, g_gd.at[t // per, pl.ds(lax.rem(t, per) * spots, spots)], stage_sem.at[2])]

    first = [local_copy(heads_hbm, heads, in_sem.at[0]), local_copy(cot_hbm, cot, in_sem.at[1]),
             local_copy(x_hbm, w_d.at[1], in_sem.at[2])] + out_weight(1)
    for copy in first + weights(0, 0):
        copy.start()
    for copy in first:
        copy.wait()
    for n in range(2):
        at = slice(n * 512, (n + 1) * 512)
        hidden[:, at] = w_d[1, :, at].astype(F32) + dot(heads[...], w_gu[1, n])
    def normalise(n, carry):
        at = pl.ds(pl.multiple_of(n * 128, 128), 128)
        h = hidden[at, :]
        y = h * scale_of(h) * gain
        nrm[at, :] = y.astype(BF)
        nrm_t[:, at] = y.T.astype(BF)
        acc[at, :] = h
        dnorm[at, :] = jnp.zeros_like(h)
        return carry
    lax.fori_loop(0, 4, normalise, 0)

    def tile(t, carry):
        slot = lax.rem(t, 2)
        for copy in weights(t, slot):
            copy.wait()
        @pl.when(t < tiles - 1)
        def _():
            for copy in weights(t + 1, 1 - slot):
                copy.start()
        @pl.when(t == tiles - 1)
        def _():
            for copy in out_weight(tiles % 2):
                copy.start()
        normed = nrm[...]
        wg, wu, wd = w_gu[slot, 0], w_gu[slot, 1], w_d[slot]
        gate = dot(normed, wg)
        up = dot(normed, wu)
        d_product = dot_tb(cot[...], wd)
        @pl.when(t > 0)
        def _():
            for copy in staged(t - 1):
                copy.wait()
            work.step(t - 1, *BACK_LAGS)
        sig = jax.nn.sigmoid(gate)
        silu = gate * sig
        product = silu * up
        prod_b = product.astype(BF)
        d_gate = (d_product * up * sig * (1.0 + gate * (1.0 - sig))).astype(BF)
        d_up = (d_product * silu).astype(BF)
        acc[...] += dot(prod_b, wd)
        dnorm[...] += dot_tb(d_gate, wg) + dot_tb(d_up, wu)
        stage[0] = as_blocks(dot(nrm_t[...], d_gate), stage.shape[1:])
        stage[1] = as_blocks(dot(nrm_t[...], d_up), stage.shape[1:])
        stage_d[...] = down_blocks(dot(product.T.astype(BF), cot[...]), stage_d.shape)
        for copy in staged(t):
            copy.start()
        return carry
    lax.fori_loop(0, tiles, tile, 0)
    for copy in staged(tiles - 1):
        copy.wait()
    work.step(tiles - 1, *BACK_LAGS)

    def finish(n, carry):
        at = pl.ds(pl.multiple_of(n * 128, 128), 128)
        h = hidden[at, :]
        du, terms = norm_back_rows(h, scale_of(h), gain, dnorm[at, :])
        d_hidden = cot[at, :].astype(F32) + du
        hidden[at, :] = d_hidden
        nrm[at, :] = d_hidden.astype(BF)
        heads_t = heads[at, :].astype(F32).T.astype(BF)
        nrm_t[:, at] = heads_t
        cot[at, :] = acc[at, :].astype(BF)
        return carry + terms
    gffn_ref[...] = lax.fori_loop(0, 4, finish, jnp.zeros(gffn_ref.shape, F32))
    work.step(tiles, *BACK_LAGS)
    last = [local_copy(cot, out_hbm, out_sem.at[0]), local_copy(hidden, dhid_hbm, out_sem.at[1])]
    for copy in last:
        copy.start()
    for copy in out_weight(tiles % 2):
        copy.wait()
    d_attn = nrm[...]
    total = jnp.zeros(hidden.shape, F32)
    for n in range(2):
        at = slice(n * 512, (n + 1) * 512)
        total = total + dot_tb(d_attn[:, at], w_gu[tiles % 2, n])
    d_tok[...] = total.astype(BF)
    for n in range(2):
        at = slice(n * 512, (n + 1) * 512)
        stage[n] = as_blocks(dot(nrm_t[...], d_attn[:, at]), stage.shape[1:])
        copy = local_copy(stage.at[n], g_go.at[n], stage_sem.at[n])
        copy.start()
    for n in range(2):
        local_copy(stage.at[n], g_go.at[n], stage_sem.at[n]).wait()
    for copy in last:
        copy.wait()


def score_phase(work, first_step, ring, d_tok, kx_hbm, vx_hbm, kf_ref, qf_ref, qa_hbm, of_hbm, do_loc, rims, back, same, every, between,
                kx, vx, qa, of, dq_loc, dk_loc, dv_loc, ka, va, kt, dka, dva,
                load_sem, local_sem, in_send, in_recv, back_send, back_recv, rim_send, rim_recv):
    p, c, h = place()
    rim = Rim(ring)
    rows, width = d_tok.shape
    group = 4 * rows
    mine = pl.ds(pl.multiple_of(h * rows, rows), rows)
    three = pl.ds(0, 3 * rows)
    for pair in range(2):
        cols = pair_at(0, pair)
        local_copy(d_tok.at[:, pair_at(h * 256, pair)], do_loc.at[mine, cols], local_sem.at[0, pair]).start()
        for step in range(1, 4):
            to = lax.rem(h + step, 4)
            remote(d_tok.at[:, pair_at(to * 256, pair)], do_loc.at[mine, cols], in_send.at[pair], in_recv.at[pair], (p, c, to)).start()
    same[...] = jnp.zeros_like(same)
    every[...] = jnp.zeros_like(every)

    trios = ((0, dq_loc, 0), (1, dk_loc, HALF), (2, dv_loc, HALF))
    kinds = ((0, dk_loc), (1, dv_loc))
    sides = ((rim.has_high, rim.high, HALF + group), (rim.has_low, rim.low, 0))

    def rim_copy(ref, side, kind, pair):
        there, block, first = sides[side]
        cols = pair_at(0, pair)
        return remote(ref.at[pl.ds(first, HALF), cols], rims.at[side, kind, :, cols],
                      rim_send.at[side, kind, pair], rim_recv.at[side, kind, pair], (p, block, h))

    def give(kind, pair, wanted):
        _, ref, skip = trios[kind]
        cols, at = pair_at(0, pair), pair_at(kind * width + h * 256, pair)
        for step in range(4):
            to = lax.rem(h + step, 4)
            theirs = ref.at[pl.ds(pl.multiple_of(skip + to * rows, rows), rows), cols]
            def go():
                if step == 0:
                    local_copy(theirs, back.at[:, at], local_sem.at[1 + kind, pair]).start()
                else:
                    remote(theirs, back.at[:, at], back_send.at[kind, pair], back_recv.at[kind, pair], (p, c, to)).start()
            if wanted is None:
                go()
            else:
                edge = (to == 0) | (to == 3)
                pl.when(edge if wanted else jnp.logical_not(edge))(go)

    def edges_back(pair):
        cols = pair_at(0, pair)
        for side in range(2):
            first = HALF if side == 0 else group
            @pl.when(sides[1 - side][0])
            def _():
                for kind, ref in kinds:
                    rim_copy(ref, side, kind, pair).wait_recv()
                    for m in range(4):
                        to = pl.ds(first + m * 128, 128)
                        more = rims[side, kind, pl.ds(m * 128, 128), cols].astype(F32)
                        ref[to, cols] = (ref[to, cols].astype(F32) + more).astype(BF)
        give(1, pair, True)
        give(2, pair, True)

    blocks = group // QB
    def pair_step(pair, carry):
        cols = pair_at(0, pair)
        loads = [local_copy(kx_hbm.at[:, cols], kx, load_sem.at[0]), local_copy(vx_hbm.at[:, cols], vx, load_sem.at[1]),
                 local_copy(qa_hbm.at[pl.ds(pair * 2, 2)], qa, load_sem.at[2]), local_copy(of_hbm.at[:, cols], of, load_sem.at[3])]
        for copy in loads:
            copy.start()
        dka[...] = jnp.zeros_like(dka)
        dva[...] = jnp.zeros_like(dva)
        for copy in loads:
            copy.wait()
        build_keys(0, kx, vx, kf_ref, ka, va, kt)
        local_copy(do_loc.at[mine, cols], do_loc.at[mine, cols], local_sem.at[0, pair]).wait()
        local_copy(do_loc.at[three, cols], do_loc.at[three, cols], in_recv.at[pair]).wait()
        def step(m, c):
            @pl.when(lax.rem(m, BACK_EVERY) == 0)
            def _():
                work.step(first_step + (pair * blocks + m) // BACK_EVERY, *BACK_LAGS)
            backward_block(pair, m, qf_ref, qa, do_loc, of, ka, va, kt, dka, dva, dq_loc, same, every)
            return c
        lax.fori_loop(0, blocks // 2, step, 0)
        @pl.when(pair == 1)
        def _():
            edges_back(0)
            between()
        lax.fori_loop(blocks // 2, blocks, step, 0)
        backward_finish(pair, dka, dva, dk_loc, dv_loc)
        for side in range(2):
            @pl.when(sides[side][0])
            def _():
                for kind, ref in kinds:
                    rim_copy(ref, side, kind, pair).start()
        give(1, pair, False)
        give(2, pair, False)
        give(0, pair, None)
        return carry
    lax.fori_loop(0, 2, pair_step, 0)
    edges_back(1)
    done = first_step + 2 * blocks // BACK_EVERY
    def more(t, carry):
        work.step(t, *BACK_LAGS)
        return carry
    lax.fori_loop(done, max(done, LATE), more, 0)

    part = back.at[:, pl.ds(0, 384)]
    for pair in range(2):
        cols = pair_at(0, pair)
        for kind in range(3):
            at = pair_at(kind * width + h * 256, pair)
            local_copy(back.at[:, at], back.at[:, at], local_sem.at[1 + kind, pair]).wait()
            local_copy(part, part, back_recv.at[kind, pair]).wait()
            local_copy(part, part, back_send.at[kind, pair]).wait()
        local_copy(do_loc.at[three, cols], do_loc.at[three, cols], in_send.at[pair]).wait()
        for side in range(2):
            @pl.when(sides[side][0])
            def _():
                for kind, ref in kinds:
                    rim_copy(ref, side, kind, pair).wait_send()


def unproject_phase(first, done, work, x_hbm, gain, wide, raw_hbm, cos_ref, sin_ref, hg_ref, dhid_hbm, back, g_qkv, gin_hbm, gattn_ref, ghead_ref,
                    before, x, nrm_t, dnorm, w, raw, stage, dhid, in_sem, w_sem, stage_sem):
    def tile_copies(t, slot):
        copies = [local_copy(wide.at[t], w.at[slot], w_sem.at[slot, 0])]
        if t < 4:
            copies.append(local_copy(raw_hbm.at[:, t * 512:(t + 1) * 512], raw.at[slot], w_sem.at[slot, 1]))
        return copies
    late = local_copy(dhid_hbm, dhid, in_sem.at[1])
    load = local_copy(x_hbm, x, in_sem.at[0])
    load.start()
    late.start()
    for copy in tile_copies(0, 0):
        copy.start()
    load.wait()
    def normalise(n, carry):
        at = pl.ds(pl.multiple_of(n * 128, 128), 128)
        u = x[at, :].astype(F32)
        nrm_t[:, at] = (u * scale_of(u) * gain).T.astype(BF)
        return carry
    lax.fori_loop(0, 4, normalise, 0)
    ghead_ref[...] = jnp.zeros_like(ghead_ref)
    for t in range(6):
        slot = t % 2
        if t < 5:
            for copy in tile_copies(t + 1, 1 - slot):
                copy.start()
        for copy in tile_copies(t, slot):
            copy.wait()
        if t < 4:
            kind = t // 2
            head_gain = hg_ref[kind:kind + 1, :]
            def unrotate(n, carry):
                at = pl.ds(pl.multiple_of(n * 128, 128), 128)
                for m in range(4):
                    part = slice(m * 128, (m + 1) * 128)
                    wide_part = slice(t * 512 + m * 128, t * 512 + (m + 1) * 128)
                    u = raw[slot, at, part].astype(F32)
                    dy = back[at, wide_part].astype(F32)
                    dy = dy * cos_ref[at, :] - swap_halves(dy) * sin_ref[at, :]
                    r = lax.rsqrt(head_mean(u * u) + EPS)
                    scaled = dy * head_gain
                    back[at, wide_part] = (r * scaled - u * (r * r * r) * head_mean(scaled * u)).astype(BF)
                    ghead_ref[kind:kind + 1, :] += jnp.sum(dy * u * r, axis=0, keepdims=True)
                return carry
            lax.fori_loop(0, 4, unrotate, 0)
        d_proj = back[:, t * 512:(t + 1) * 512]
        stage[slot] = as_blocks(dot(nrm_t[...], d_proj), stage.shape[1:])
        copy = local_copy(stage.at[slot], g_qkv.at[t], stage_sem.at[slot])
        copy.start()
        part = dot_tb(d_proj, w[slot])
        if t == 0:
            dnorm[...] = part
        else:
            dnorm[...] += part
        copy.wait()
        if t < 2:
            for n in range(IN_UNPROJECT // 2):
                first.step(done + t * IN_UNPROJECT // 2 + n, *BACK_LAGS)
        if t == 1:
            before()
        if t % 2:
            work.step(t // 2, *BACK_LAGS)
    late.wait()
    def finish(n, carry):
        at = pl.ds(pl.multiple_of(n * 128, 128), 128)
        u = x[at, :].astype(F32)
        du, terms = norm_back_rows(u, scale_of(u), gain, dnorm[at, :])
        dhid[at, :] = dhid[at, :] + du
        return carry + terms
    gattn_ref[...] = lax.fori_loop(0, 4, finish, jnp.zeros(gattn_ref.shape, F32))
    copy = local_copy(dhid, gin_hbm, in_sem.at[1])
    copy.start()
    copy.wait()


def train_kernel(ring, x, heads, cot, gains, wide, down, kx, vx, kf, qf, qa, of, raw, cos_ref, sin_ref, hg_ref,
                 out, gin, sums, small_out, dhid, g_gu, g_go, g_gd, g_qkv,
                 d_tok, do_loc, rims, back, same, every, gffn, gattn, ghead,
                 small, came, far, small_send, small_recv, credit,
                 local_sem, in_send, in_recv, back_send, back_recv, rim_send, rim_recv, *buffers):
    p, c, h = place()
    peers = group_peers(ring)
    greet(peers + [(p, c, 3 - h)])
    rows, width = d_tok.shape
    group, ext = 4 * rows, 4 * rows + 2 * HALF
    r, w = sums.shape[-2:]
    block = (2, ring, 2, 2, r, w)
    bufs, sems, last_sems = buffers[:4], buffers[4:7], (buffers[4],) + buffers[7:]
    dma = pltpu.SemaphoreType.DMA
    count = 26

    def write(i, total):
        sums[i] = total

    def write_last(i, total):
        sums[count + i] = total

    work = Scatter(ring, count, lambda pair: pair < 0, scatter_pick((g_gu, g_gd, g_go), ((16, True), (8, False), (2, True)), w), bufs, sems, write)
    last = Scatter(ring, 6, lambda pair: pair < 0, scatter_pick((g_qkv,), ((6, True),), w), bufs, last_sems, write_last)
    vm = pltpu.VMEM
    tiles = down.shape[0] // 512
    spots = g_gd.shape[0] * g_gd.shape[1] // tiles

    pl.run_scoped(
        functools.partial(feed_phase, work, heads, cot, x, gains[1], wide, down, g_gu, g_go, g_gd, out, dhid, d_tok, gffn, back),
        vm((rows, width), F32), vm((rows, width), F32), vm((rows, width), F32), vm((width, rows), BF), vm((2, 2, width, 512), BF), vm((2, 512, width), BF),
        vm((2,) + block, BF), vm((spots,) + g_gd.shape[2:], BF), dma((3,)), dma((2, 3)), dma((3,)), dma((2,)))
    def between():
        work.drain_all(0, 3)
        for peer in peers:
            pl.semaphore_signal(credit, inc=1, device_id=peer, device_id_type=MESH)

    def score(kx_p, vx_p, qa_p, of_p, dq_loc, dk_loc, dv_loc, ka, va, kt, dka, dva, load_sem):
        score_phase(work, tiles + 1, ring, d_tok, kx, vx, kf, qf, qa, of, do_loc, rims, back, same, every, between,
                    kx_p, vx_p, qa_p, of_p, dq_loc, dk_loc, dv_loc, ka, va, kt, dka, dva,
                    load_sem, local_sem, in_send, in_recv, back_send, back_recv, rim_send, rim_recv)

    pl.run_scoped(
        score,
        vm((ext, 128), BF), vm((ext, 128), BF), vm((2, group, 128), BF), vm((group, 128), F32),
        vm((group, 256), BF), vm((ext, 256), BF), vm((ext, 256), BF),
        vm((2, ext, 128), BF), vm((2, ext, 128), BF), vm((2, 128, ext), BF), vm((2, ext, 128), F32), vm((2, ext, 128), F32),
        dma((4,)))
    pl.run_scoped(
        functools.partial(unproject_phase, work, max(LATE, tiles + 1 + 2 * (group // QB) // BACK_EVERY), last, x, gains[0], wide, raw, cos_ref, sin_ref, hg_ref, dhid, back, g_qkv, gin, gattn, ghead,
                          lambda: pl.semaphore_wait(credit, len(peers))),
        vm((rows, width), BF), vm((width, rows), BF), vm((rows, width), F32), vm((2, width, 512), BF), vm((2, rows, 512), BF),
        vm((2,) + block, BF), vm((rows, width), F32), dma((2,)), dma((2, 2)), dma((2,)))

    def total_of(value):
        return jnp.sum(jnp.sum(value, axis=1, keepdims=True), axis=2, keepdims=True)
    s, e = total_of(same[...]), total_of(every[...])
    lane = lax.broadcasted_iota(jnp.int32, (1, 128), 1)
    bias = jnp.zeros((1, 128), F32)
    for m in range(4):
        bias = jnp.where(lane == h * 8 + 2 * m, s[m], jnp.where(lane == h * 8 + 2 * m + 1, e[m] - s[m], bias))
    for n in range(8):
        at = slice(n * 128, (n + 1) * 128)
        small[0, n:n + 1, :] = gattn[:, at]
        small[0, 8 + n:9 + n, :] = gffn[:, at]
    small[0, 16:18, :] = ghead[...]
    small[0, 18:19, :] = bias
    small[0, 19:24, :] = jnp.zeros((5, 128), F32)
    hops = (last.core, last.xpeer, last.ypeer)

    def hop(n):
        return remote(small.at[n], came.at[n], small_send.at[n], small_recv.at[n], hops[n])

    hop(0).start()
    left = max(LATE, tiles + 1 + 2 * (group // QB) // BACK_EVERY) + IN_UNPROJECT
    def rest(t, carry):
        work.step(left + t - 3, *BACK_LAGS)
        last.step(t, *BACK_LAGS)
        for n in range(3):
            @pl.when(t == 3 + n)
            def _():
                hop(n).wait_recv()
                small[n + 1] = small[n] + came[n]
                if n < 2:
                    hop(n + 1).start()
                else:
                    for step in range(1, ring):
                        remote(small.at[3], far.at[step - 1], small_send.at[3], small_recv.at[3], (p, lax.rem(c + step, ring), h)).start()
        return carry
    lax.fori_loop(3, max(last.steps(*BACK_LAGS), work.steps(*BACK_LAGS) - left + 3), rest, 0)
    local_copy(far, far, small_recv.at[3]).wait()
    total = small[3]
    for step in range(1, ring):
        total = total + far[step - 1]
    small_out[...] = total
    for n in range(3):
        hop(n).wait_send()
    local_copy(far, far, small_send.at[3]).wait()
    work.drain_all(3)
    last.drain_all()


def train(x, heads, cot, gains, wide, down, kx, vx, kf, qf, qa, of, raw, cosine, sine, head_gains, ring, item, collective_id):
    rows, width = x.shape
    group, ext = 4 * rows, 4 * rows + 2 * HALF
    r, w = item
    block = (2, ring, 2, 2, r, w)
    dma = pltpu.SemaphoreType.DMA
    vm = pltpu.VMEM
    shape = jax.ShapeDtypeStruct
    return pl.pallas_call(
        functools.partial(train_kernel, ring),
        out_shape=(
            shape((rows, width), BF), shape((rows, width), F32), shape((32, r, w), F32), shape((24, 128), F32),
            shape((rows, width), F32), shape((16,) + block, BF), shape((2,) + block, BF),
            shape((2, ring, 2, 2, 4, r, 2 * w), BF), shape((6,) + block, BF)),
        in_specs=[ANY] * 3 + [VM] + [ANY] * 4 + [VM] * 2 + [ANY] * 3 + [VM] * 3,
        out_specs=(ANY, ANY, VM, VM) + (ANY,) * 5,
        scratch_shapes=[
            vm((rows, width), BF), vm((group, 256), BF), vm((2, 2, HALF, 256), BF), vm((rows, 3 * width), BF),
            vm((4, 8, QB), F32), vm((4, 8, QB), F32), vm((1, width), F32), vm((1, width), F32), vm((2, 128), F32),
            vm((4, 24, 128), F32), vm((3, 24, 128), F32), vm((ring - 1, 24, 128), F32), dma((4,)), dma((4,)),
            pltpu.SemaphoreType.REGULAR,
            dma((4, 2)), dma((2,)), dma((2,)), dma((3, 2)), dma((3, 2)), dma((2, 2, 2)), dma((2, 2, 2)),
        ] + scatter_scratch(ring, 26, r, w) + [dma((4, 6)), dma((4, 6))],
        compiler_params=pltpu.CompilerParams(collective_id=collective_id, has_side_effects=True, vmem_limit_bytes=63 * MIB),
        name="train",
    )(x, heads, cot, gains, wide, down, kx, vx, kf, qf, qa, of, raw, cosine, sine, head_gains)


def to_blocks(weight, depth, r, w):
    parts = weight.reshape(-1, depth, weight.shape[1] // 512, r // depth, w)
    return parts.transpose(2, 0, 3, 1, 4).reshape(weight.shape[1] // 512, -1, r, w)


def from_blocks(blocks, depth):
    n, (r, w) = blocks.shape[0], blocks.shape[-2:]
    return blocks.reshape(n, -1, r // depth, depth, w).swapaxes(2, 3).reshape(n, -1, 512)


def local(
    inputs, cotangent, w_qkv, w_out, w_gate, w_up, w_down, gain_attn, gain_ffn, q_gain, k_gain, head_bias,
    segment_ids, variate_ids, time_index,
):
    ring = lax.axis_size("cp")
    head = lax.axis_index("hd")
    rows, width = inputs.shape
    depth = w_qkv.shape[0]
    r, w = item_shape(depth)

    me = (lax.axis_index("pack") * ring + lax.axis_index("cp")) * 4 + head
    srcs = (w_qkv, w_out, w_gate, w_up, w_down)
    if r != depth:
        down_pieces = w_down.reshape(4, r, 2, w).swapaxes(1, 2).reshape(8, r, w)
        srcs = (jnp.concatenate([to_blocks(weight, depth, r, w)[:, 0] for weight in srcs[:4]] + [down_pieces]),)
    gain_src = lax.dynamic_update_slice(jnp.zeros((2, width), BF), jnp.stack([gain_attn, gain_ffn]), (0, me * depth))
    gain_src = gain_src.reshape(16, 128)

    times = lax.dynamic_slice_in_dim(time_index, head * rows, rows, 0)
    lane = jnp.arange(128)
    frequency = jnp.exp(-math.log(theta_base) * 2.0 * (lane % 32).astype(F32) / HDIM)
    angle = times.astype(F32)[:, None] * frequency[None, :]
    cosine = jnp.cos(angle)
    sine = jnp.sin(angle) * jnp.where(lane % 64 < 32, -1.0, 1.0)[None, :]
    head_gains = jnp.stack([jnp.concatenate([q_gain, q_gain]), jnp.concatenate([k_gain, k_gain])])

    qf, kf_own = features(segment_ids, variate_ids)
    hs = head_scales(lax.dynamic_slice_in_dim(head_bias, head * 4, 4, 0))

    heads_out, of, qa, kx, vx, kf, raw, gains, wide, down = attend(
        inputs, cosine, sine, head_gains, kf_own, qf, hs, srcs, gain_src, (r, w), 24, 32, ring, 1)
    wide = from_blocks(wide, depth)
    gains = gains.reshape(2, 1, width)
    layer_out, grad_inputs, items, small, *_ = train(
        inputs, heads_out, cotangent, gains, wide, down.reshape(-1, width), kx, vx, kf, qf, qa, of, raw,
        cosine, sine, head_gains, ring, (r, w), 2)

    def columns(part):
        return from_blocks(part, depth).swapaxes(0, 1).reshape(depth, -1)

    pairs = items[:16].reshape(8, 2, r, w)
    down_depth = w_down.shape[0] // 4
    own_down = items[16:24].reshape(4, 2, r // down_depth, down_depth, w).transpose(0, 3, 2, 1, 4).reshape(w_down.shape)
    own_gains = lax.dynamic_slice_in_dim(small[:16].reshape(2, width), me * depth, depth, 1)
    own_heads = small[16:18, :HDIM] + small[16:18, HDIM:]
    return (
        layer_out, grad_inputs, columns(items[26:]), columns(items[24:26]), columns(pairs[:, 0]), columns(pairs[:, 1]),
        own_down, own_gains[0], own_gains[1], own_heads[0], own_heads[1], small[18, :32].reshape(HEADS, 2),
    )


def solution(mesh):
    return jax.shard_map(
        local,
        mesh=mesh,
        in_specs=(
            P(("pack", "cp", "hd"), None),
            P(("pack", "cp", "hd"), None),
            P(("pack", "cp", "hd"), None),
            P(("pack", "cp", "hd"), None),
            P(("pack", "cp", "hd"), None),
            P(("pack", "cp", "hd"), None),
            P(("pack", "cp", "hd"), None),
            P(("pack", "cp", "hd")),
            P(("pack", "cp", "hd")),
            P(),
            P(),
            P(),
            P(("pack", "cp")),
            P(("pack", "cp")),
            P(("pack", "cp")),
        ),
        out_specs=(
            P(("pack", "cp", "hd"), None),
            P(("pack", "cp", "hd"), None),
            P(("pack", "cp", "hd"), None),
            P(("pack", "cp", "hd"), None),
            P(("pack", "cp", "hd"), None),
            P(("pack", "cp", "hd"), None),
            P(("pack", "cp", "hd"), None),
            P(("pack", "cp", "hd")),
            P(("pack", "cp", "hd")),
            P(),
            P(),
            P(),
        ),
        check_vma=False,
    )
```
